32 devices in a mesh: owner: 4 (over y, core), tensor: 8 (over z, x).
Axes of the slice: x: 2, y: 2, z: 4, core: 2. Of those that a mesh axis runs over, the one named last changes fastest.
Arguments:
- hidden: bfloat16 [128, 2048], P('owner', 'tensor'), may hold values from -6 to 6
- attention_gain: bfloat16 [2048], replicated, may hold values from 0.5 to 1.5
- query_weight: bfloat16 [9216, 2048], P('tensor'), may hold values from -1 to 1
- out_weight: bfloat16 [2048, 8192], P('tensor'), may hold values from -1.796875 to 1.796875
- root_cache: bfloat16 [32768, 576], P('tensor'), may hold values from -4 to 4
- group_cache: bfloat16 [48, 1024, 576], P('owner', 'tensor'), may hold values from -4 to 4
- group_length: int32 [48], P('owner'), may hold values from 128 to 1024, as said below
- suffix_cache: bfloat16 [128, 512, 576], P('owner', 'tensor'), may hold values from -4 to 4
- suffix_length: int32 [128], P('owner'), may hold values from 1 to 512, as said below
- group_of: int32 [128], P('owner'), may hold values from 0 to 47, as said below
- mixture_gain: bfloat16 [2048], replicated, may hold values from 0.5 to 1.5
- routes: int32 [128, 6], P('owner'), may hold values from 0 to 31, all different within a row; in each aligned block of 32 rows (0 to 31, 32 to 63, ...) at most 12 rows name the same one
- route_weight: float32 [128, 6], P('owner'), may hold values from 0.1 to 1
- expert_gate: bfloat16 [32, 1408, 2048], P(('owner', 'tensor')), may hold values from -0.125 to 0.125
- expert_up: bfloat16 [32, 1408, 2048], P(('owner', 'tensor')), may hold values from -0.125 to 0.125
- expert_down: bfloat16 [32, 1408, 2048], P(('owner', 'tensor')), may hold values from -0.15625 to 0.15625
- shared_gate: bfloat16 [2816, 2048], P('tensor'), may hold values from -0.125 to 0.125
- shared_up: bfloat16 [2816, 2048], P('tensor'), may hold values from -0.125 to 0.125
- shared_down: bfloat16 [2816, 2048], P('tensor'), may hold values from -0.109375 to 0.109375
Outputs:
- layer_out: bfloat16 [128, 2048], P('owner', 'tensor')
The draws below stay inside these ranges and needn't reach their ends.
Inputs may be any that keep to these rules, and one draw needn't show every extreme that they name: `group_of`: the groups of owner o are o * 12 to (o + 1) * 12 - 1. Among the requests of one owner (rows o * 32 to (o + 1) * 32 - 1), at most 16 have their group on any one owner, and some owner gets exactly 16 of them. `group_length`: some group prompt uses all 1024 positions. `suffix_length`: some request uses all 512 suffix positions. `routes`: each row names 6 different experts; among the rows of one owner no expert is named more than 12 times, and that is reached.
All inputs are finite; a program needn't handle non-finite values.
Results may differ from the reference program's by a relative error of at most 0.012.
The reference program's roundings to bfloat16 on the way count: a program that leaves them out, or rounds other values in their place, can miss the bound.
Values may be sent and summed in bfloat16 or wider, within the bound.
No kernel may reach another device: no remote copies, remote signals or barrier semaphores. Data moves between devices by JAX's collectives and lax.ppermute only.
A program may use at most 128 MiB of HBM per device.

```python
import math
import jax
import jax.numpy as jnp
import numpy as np
from jax import lax

D = 2048
H = 16
LAT = 512
ROPE = 64
KVW = 576
FF = 1408
SHARED_FF = 2816
TOPK = 6
EXPERTS = 32
FSPLIT = 1
ROOT = 32768
GROUP_OWN = 12
GROUPS = 48
GMAX = 1024
SMAX = 512
REQ_OWN = 32
REQUESTS = 128
CAP = 16
ECAP = 12
RSEG = 4096
GSEG = 128
SSEG = 64
N_OWNER = 4
N_TENSOR = 8


def cache_rows(key, salt_value, array_shape, spread):
    inner_key = jax.random.fold_in(key, salt_value)
    base_rows = jnp.clip(jax.random.normal(inner_key, array_shape, jnp.float32) * spread, -4.0, 4.0)
    return base_rows


def root_rows(key):
    inner_key = jax.random.fold_in(key, 11)
    row_scale = jnp.exp(jax.random.uniform(jax.random.fold_in(key, 14), (ROOT, 1), jnp.float32, -1.15, 1.15))
    mean_sign = jax.random.rademacher(jax.random.fold_in(key, 15), (LAT,), jnp.float32)
    mean_pick = jax.random.uniform(jax.random.fold_in(key, 16), (LAT,), jnp.float32) < 0.25
    mean_vector = jnp.concatenate([jnp.where(mean_pick, 0.3 * mean_sign, 0.0), jnp.zeros((ROPE,), jnp.float32)])
    base_rows = jax.random.normal(inner_key, (ROOT, KVW), jnp.float32) * 0.5
    rows = jnp.clip(mean_vector[None, :] + row_scale * base_rows, -4.0, 4.0)
    return rows


def draw_root_cache(key, part):
    return root_rows(key).astype(jnp.bfloat16)


def draw_group_cache(key, part):
    return cache_rows(key, 12, (GROUPS, GMAX, KVW), 1.6).astype(jnp.bfloat16)


def draw_suffix_cache(key, part):
    return cache_rows(key, 13, (REQUESTS, SMAX, KVW), 1.4).astype(jnp.bfloat16)


def draw_query_weight(key, part):
    array_shape = (H * KVW, D)
    inner_key = jax.random.fold_in(key, 21)
    base_rows = jnp.clip(jax.random.normal(inner_key, array_shape, jnp.float32), -4.0, 4.0) / math.sqrt(D)
    return base_rows.astype(jnp.bfloat16)


def draw_group_of(key, part):

    def one_block(block_key):
        block_keys = jax.random.split(block_key, 4)
        hot_owner = jax.random.randint(block_keys[0], (), 0, N_OWNER)
        slots = jnp.arange(N_OWNER * CAP)
        priority = jax.random.permutation(block_keys[1], N_OWNER * CAP)
        ranked = jnp.where(slots // CAP == hot_owner, priority - N_OWNER * CAP, priority)
        taken_slots = jnp.argsort(ranked, stable=True)[:REQ_OWN]
        owner_index = taken_slots // CAP
        member = jax.random.randint(block_keys[2], (REQ_OWN,), 0, GROUP_OWN)
        shuffle = jax.random.permutation(block_keys[3], REQ_OWN)
        return (owner_index * GROUP_OWN + member)[shuffle]
    block_keys = jax.random.split(jax.random.fold_in(key, 31), N_OWNER)
    return jax.vmap(one_block)(block_keys).reshape(-1).astype(jnp.int32)


def draw_group_length(key, part):
    lengths = jax.random.randint(jax.random.fold_in(key, 41), (GROUPS,), GMAX // 8, GMAX + 1)
    longest = jax.random.randint(jax.random.fold_in(key, 42), (), 0, GROUPS)
    return jnp.where(jnp.arange(GROUPS) == longest, GMAX, lengths).astype(jnp.int32)


def draw_suffix_length(key, part):
    lengths = jax.random.randint(jax.random.fold_in(key, 51), (REQUESTS,), 1, SMAX + 1)
    longest = jax.random.randint(jax.random.fold_in(key, 52), (), 0, REQUESTS)
    return jnp.where(jnp.arange(REQUESTS) == longest, SMAX, lengths).astype(jnp.int32)


def steps_of(own_key, extent, cuts, least, high):
    loudness = 1.0
    for position, shards_of in cuts:
        heights = jax.random.uniform(jax.random.fold_in(jax.random.fold_in(own_key, 6), position), (shards_of,), jnp.float32, least / len(cuts), high / len(cuts))
        loudness = loudness * jnp.repeat(jnp.exp(heights), extent[position] // shards_of).reshape((-1,) + (1,) * (len(extent) - 1 - position))
    return loudness


def routed_block(key, own, number, rows, count, top, limit, lean):
    order = jax.random.permutation(key, count)
    heavy_load, common = load_shares(count, rows * top, limit, lean, True), load_shares(count, rows * top, limit, lean, False)
    places = jnp.arange(count)

    def named(sizes, rotation):
        used = int((sizes > 0).sum())
        fixed = max(1, used // 4)
        shifted = fixed + (places - fixed + rotation * (used - fixed)) % max(1, count - fixed)
        return jnp.zeros((count,), jnp.int32).at[order[jnp.where(places < fixed, places, shifted)]].set(jnp.asarray(sizes, jnp.int32))

    sizes = jnp.where(number % 4 == 0, named(heavy_load, number // 4), named(common, number - number // 4 - 1))
    mixed = jax.random.permutation(jax.random.fold_in(own, 3), count)
    source_of, receiver = mixed[0:count // 2 * 2:2], mixed[1:count // 2 * 2:2]
    slack = jnp.minimum(sizes[source_of] - 1, limit - sizes[receiver]) // 2
    slack = jnp.where((source_of == order[0]) | (receiver == order[0]) | (sizes[receiver] == 0), 0, jnp.maximum(slack, 0))
    shifted = jax.random.randint(jax.random.fold_in(own, 4), (count // 2,), 0, 1 << 20) % (slack + 1)
    sizes = sizes.at[source_of].add(-shifted).at[receiver].add(shifted)
    labels = jnp.searchsorted(jnp.cumsum(sizes), jnp.arange(rows * top), side="right").astype(jnp.int32)
    table = labels.reshape(top, rows).T
    table = table[jax.random.permutation(jax.random.fold_in(own, 1), rows)]
    rotation = jax.random.randint(jax.random.fold_in(own, 2), (rows, 1), 0, top)
    return jnp.take_along_axis(table, (jnp.arange(top)[None, :] + rotation) % top, axis=1)


def load_shares(count, total, limit, skew, full):
    weights = [(1 << 20) // math.isqrt(rank ** skew) + 1 for rank in range(1, count + 1)]
    largest = limit if full else min(limit, max(-(-total // count), total * weights[0] // sum(weights)))
    least = 1 if total - largest >= count - 1 else 0
    counts, rest = [largest] + [least] * (count - 1), total - largest - least * (count - 1)
    while rest > 0:
        movable = [i for i in range(1, count) if counts[i] < largest] or [i for i in range(1, count) if counts[i] < limit]
        whole, budget = sum([weights[i] for i in movable]), rest
        for i in movable:
            addition = min(limit - counts[i], max(1, budget * weights[i] // whole), rest)
            counts[i] = counts[i] + addition
            rest = rest - addition
    return np.array(counts)


def gaussian(own_key, dims, deviation, reach, cuts=(), dtype=jnp.bfloat16):
    factor_of = steps_of(own_key, dims, cuts, -0.22, 0.18) if cuts else 1.0
    drawn = jax.random.normal(own_key, dims, jnp.float32) * deviation * factor_of
    return jnp.minimum(jnp.maximum(drawn, -reach), reach).astype(dtype)


def setup_inputs(seed: int = 0) -> dict:
    seeds = jax.random.split(jax.random.key(seed), 20)
    hidden = gaussian(seeds[0], (REQUESTS, D), 1.0, 6.0, ((0, 4), (1, 8)))
    attention_gain = jnp.clip(1.0 + 0.1 * jax.random.normal(seeds[1], (D,), jnp.float32), 0.5, 1.5).astype(jnp.bfloat16)
    query_weight = draw_query_weight(jax.random.fold_in(seeds[19], 71), 0)
    out_weight = gaussian(seeds[3], (D, H * LAT), 0.3, 1.796875, ((0, 8),))
    root_cache = draw_root_cache(jax.random.fold_in(seeds[19], 71), 0)
    group_cache = draw_group_cache(jax.random.fold_in(seeds[19], 71), 0)
    group_length = draw_group_length(jax.random.fold_in(seeds[19], 71), 0)
    suffix_cache = draw_suffix_cache(jax.random.fold_in(seeds[19], 71), 0)
    suffix_length = draw_suffix_length(jax.random.fold_in(seeds[19], 71), 0)
    group_of = draw_group_of(jax.random.fold_in(seeds[19], 71), 0)
    mixture_gain = jnp.clip(1.0 + 0.1 * jax.random.normal(seeds[10], (D,), jnp.float32), 0.5, 1.5).astype(jnp.bfloat16)
    routes_keys = jax.random.split(jax.random.fold_in(seeds[11], 1), REQUESTS // REQ_OWN)
    routes_turns = jax.random.permutation(jax.random.fold_in(seeds[11], 3), REQUESTS // REQ_OWN)
    routes = jax.vmap(lambda own, number: routed_block(jax.random.fold_in(seeds[11], 2), own, number, REQ_OWN, EXPERTS, TOPK, ECAP, 2))(routes_keys, routes_turns).reshape((REQUESTS, TOPK))
    route_weight = jnp.clip(jnp.exp(math.log(1.0) - 2.3025851 * jax.random.uniform(seeds[12], (REQUESTS, TOPK), jnp.float32) ** steps_of(seeds[12], (REQUESTS, TOPK), ((0, 4),), -0.2, 0.2)), 0.1, 1.0)
    expert_gate = gaussian(seeds[13], (EXPERTS * FSPLIT, FF // FSPLIT, D), D ** -0.5, 0.125, ((0, 32),))
    expert_up = gaussian(seeds[14], (EXPERTS * FSPLIT, FF // FSPLIT, D), D ** -0.5, 0.125, ((0, 32),))
    expert_down = gaussian(seeds[15], (EXPERTS * FSPLIT, FF // FSPLIT, D), FF ** -0.5, 0.15625, ((0, 32),))
    shared_gate = gaussian(seeds[16], (SHARED_FF, D), D ** -0.5, 0.125, ((0, 8),))
    shared_up = gaussian(seeds[17], (SHARED_FF, D), D ** -0.5, 0.125, ((0, 8),))
    shared_down = gaussian(seeds[18], (SHARED_FF, D), SHARED_FF ** -0.5, 0.109375, ((0, 8),))
    return dict(hidden=hidden, attention_gain=attention_gain, query_weight=query_weight, out_weight=out_weight, root_cache=root_cache, group_cache=group_cache, group_length=group_length, suffix_cache=suffix_cache, suffix_length=suffix_length, group_of=group_of, mixture_gain=mixture_gain, routes=routes, route_weight=route_weight, expert_gate=expert_gate, expert_up=expert_up, expert_down=expert_down, shared_gate=shared_gate, shared_up=shared_up, shared_down=shared_down)


score_scale = 192.0 ** (-0.5)
lowest = -1e+30
epsilon = 1e-06

def rms_rows(values, gain_vector):
    values = values.astype(jnp.float32)
    scaled = values * lax.rsqrt(lax.optimization_barrier(jnp.mean(values * values, axis=-1, keepdims=True)) + epsilon)
    return scaled * gain_vector.astype(jnp.float32)

def settle(rounded):
    return lax.optimization_barrier(rounded).astype(jnp.float32)

def block_softmax(scores, usable, values, formula):
    masked = jnp.where(usable, scores, lowest)
    peak_score = lax.optimization_barrier(jnp.max(masked, axis=-1, keepdims=True))
    weights = jnp.where(usable, jnp.exp(masked - peak_score), 0.0)
    total_mass = lax.optimization_barrier(jnp.sum(weights, axis=-1))
    numerator = jnp.einsum(formula, settle(weights.astype(jnp.bfloat16)), values)
    present = total_mass > 0.0
    safe_total = jnp.where(present, total_mass, 1.0)
    block_out = numerator / safe_total[..., None]
    log_mass = jnp.where(present, peak_score[..., 0] + jnp.log(safe_total), lowest)
    return (block_out, log_mass)

def reference(hidden, attention_gain, query_weight, out_weight, root_cache, group_cache, group_length, suffix_cache, suffix_length, group_of, mixture_gain, routes, route_weight, expert_gate, expert_up, expert_down, shared_gate, shared_up, shared_down):
    normed = rms_rows(hidden, attention_gain).astype(jnp.bfloat16)
    queries = jnp.dot(normed, query_weight.T, preferred_element_type=jnp.float32).astype(jnp.bfloat16)
    queries = queries.reshape(N_OWNER, REQ_OWN, H, KVW)
    root_blocks = root_cache.astype(jnp.float32).reshape(N_TENSOR, RSEG, KVW)
    suffix_all = suffix_cache.reshape(N_OWNER, REQ_OWN, SMAX, KVW)
    suffix_counts = suffix_length.reshape(N_OWNER, REQ_OWN)
    parents = group_of.reshape(N_OWNER, REQ_OWN)
    suffix_positions = jnp.arange(SMAX).reshape(N_TENSOR, SSEG)
    group_positions = jnp.arange(GMAX).reshape(N_TENSOR, GSEG)

    def attend(pieces):
        query_rows, suffix_rows, suffix_count, parent = pieces
        query_rows = query_rows.astype(jnp.float32)
        root_scores = jnp.einsum('rhc,bpc->rhbp', query_rows, root_blocks) * score_scale
        root_out, root_mass = block_softmax(root_scores, jnp.ones(root_scores.shape, bool), root_blocks[..., :LAT], 'rhbp,bpl->rhbl')
        suffix_rows = suffix_rows.astype(jnp.float32).reshape(REQ_OWN, N_TENSOR, SSEG, KVW)
        suffix_scores = jnp.einsum('rhc,rbpc->rhbp', query_rows, suffix_rows) * score_scale
        suffix_usable = (suffix_positions[None, :, :] < suffix_count[:, None, None])[:, None, :, :]
        suffix_out, suffix_mass = block_softmax(suffix_scores, suffix_usable, suffix_rows[..., :LAT], 'rhbp,rbpl->rhbl')
        group_rows = group_cache[parent].astype(jnp.float32).reshape(REQ_OWN, N_TENSOR, GSEG, KVW)
        group_scores = jnp.einsum('rhc,rbpc->rhbp', query_rows, group_rows) * score_scale
        group_usable = (group_positions[None, :, :] < group_length[parent][:, None, None])[:, None, :, :]
        group_out, group_mass = block_softmax(group_scores, group_usable, group_rows[..., :LAT], 'rhbp,rbpl->rhbl')
        group_out = settle(group_out.astype(jnp.bfloat16))
        all_mass = jnp.concatenate([root_mass, suffix_mass, group_mass], axis=2)
        all_out = jnp.concatenate([root_out, suffix_out, group_out], axis=2)
        peak_mass = lax.optimization_barrier(jnp.max(all_mass, axis=2, keepdims=True))
        scales = jnp.exp(all_mass - peak_mass)
        joined = lax.optimization_barrier(jnp.sum(scales[..., None] * all_out, axis=2)) / lax.optimization_barrier(jnp.sum(scales, axis=2))[..., None]
        return joined.astype(jnp.bfloat16).reshape(REQ_OWN, H * LAT)
    attention = lax.map(attend, (queries, suffix_all, suffix_counts, parents)).reshape(REQUESTS, H * LAT)
    mid = (hidden.astype(jnp.float32) + jnp.dot(attention, out_weight.T, preferred_element_type=jnp.float32)).astype(jnp.bfloat16)
    mixture_in = rms_rows(mid, mixture_gain).astype(jnp.bfloat16)
    matches = routes[:, :, None] == jnp.arange(EXPERTS).astype(jnp.int32)[None, None, :]
    share = lax.optimization_barrier(jnp.sum(matches.astype(jnp.float32) * route_weight[:, :, None], axis=1))
    hit_table = jnp.any(matches, axis=1).astype(jnp.int32)
    gate_all = expert_gate.reshape(EXPERTS, FF, D)
    up_all = expert_up.reshape(EXPERTS, FF, D)
    down_all = expert_down.reshape(EXPERTS, FSPLIT, FF // FSPLIT, D)

    def expert_step(routed_total, pieces):
        gate_rows, up_rows, down_rows, column, hit_rows = pieces
        picked = jnp.argsort(1 - hit_rows, stable=True)[:N_OWNER * ECAP].astype(jnp.int32)
        inputs = mixture_in[picked]
        gate_part = jnp.dot(inputs, gate_rows.T, preferred_element_type=jnp.float32)
        up_part = jnp.dot(inputs, up_rows.T, preferred_element_type=jnp.float32)
        activation = settle((jax.nn.silu(gate_part) * up_part).astype(jnp.bfloat16))
        blocks = jnp.einsum('rbf,bfd->rbd', activation.reshape(N_OWNER * ECAP, FSPLIT, FF // FSPLIT), down_rows.astype(jnp.float32))
        parts = lax.optimization_barrier(jnp.sum(settle(blocks.astype(jnp.bfloat16)), axis=1))
        return (routed_total.at[picked].add(column[picked][:, None] * parts), None)
    routed, _ = lax.scan(expert_step, jnp.zeros((REQUESTS, D), jnp.float32), (gate_all, up_all, down_all, share.T, hit_table.T))
    shared_gate_part = jnp.dot(mixture_in, shared_gate.T, preferred_element_type=jnp.float32)
    shared_up_part = jnp.dot(mixture_in, shared_up.T, preferred_element_type=jnp.float32)
    shared_act = (jax.nn.silu(shared_gate_part) * shared_up_part).astype(jnp.bfloat16)
    shared = jnp.dot(shared_act, shared_down, preferred_element_type=jnp.float32)
    return (mid.astype(jnp.float32) + routed + shared).astype(jnp.bfloat16)
```

```python
import functools

import jax
import jax.numpy as jnp
from jax import lax
from jax.experimental import pallas as pl
from jax.experimental.pallas import tpu as pltpu
from jax.sharding import PartitionSpec as P

H = 16
LAT = 512
KVW = 576
EXP_OWN = 8
GROUP_OWN = 12
PIECES = 8
PAIR = 2 * KVW
LANES = 128
MIB = 1 << 20

score_scale = 192.0 ** (-0.5)
log2e = 1.4426950408889634
ln2 = 0.6931471805599453
lowest = -1e30
epsilon = 1e-06

NT = (((1,), (1,)), ((), ()))


def dot_nt(a, b):
    return lax.dot_general(a, b, NT, preferred_element_type=jnp.float32)


def dot_nn(a, b):
    return jnp.dot(a, b, preferred_element_type=jnp.float32)


def call(body, out_shape, vmem_mib, flops, nbytes, **options):
    return pl.pallas_call(
        body,
        out_shape=out_shape,
        compiler_params=pltpu.CompilerParams(vmem_limit_bytes=vmem_mib * MIB),
        cost_estimate=pl.CostEstimate(
            flops=int(flops), bytes_accessed=int(nbytes), transcendentals=0
        ),
        **options,
    )


def whole(shape):
    return pl.BlockSpec(shape, lambda *_: (0,) * len(shape))


def split_three(column):
    first = column.astype(jnp.bfloat16).astype(jnp.float32)
    second = (column - first).astype(jnp.bfloat16).astype(jnp.float32)
    third = (column - first - second).astype(jnp.bfloat16).astype(jnp.float32)
    return first, second, third


def normalised(read_piece, gain, width):
    rows = jnp.concatenate([read_piece(k) for k in range(PIECES)], axis=-1).astype(jnp.float32)
    square = jnp.sum(rows * rows, axis=-1, keepdims=True) * (1.0 / width)
    return (rows * lax.rsqrt(square + epsilon) * gain).astype(jnp.bfloat16)


def project_body(rows_ref, gain_ref, weight_ref, out_ref, normed_ref):
    @pl.when(pl.program_id(0) == 0)
    def _():
        normed_ref[...] = normalised(
            lambda k: rows_ref[k], gain_ref[...], normed_ref.shape[1]
        )

    out_ref[...] = dot_nt(normed_ref[...], weight_ref[...]).astype(jnp.bfloat16)


def project(rows, gain, weight):
    pieces, requests, part = rows.shape
    columns, width = weight.shape
    steps = 3 if columns % (3 * LANES) == 0 else 1
    return call(
        project_body,
        jax.ShapeDtypeStruct((requests, columns), jnp.bfloat16),
        24,
        2 * requests * columns * width,
        2 * columns * width,
        grid=(steps,),
        in_specs=[
            whole(rows.shape),
            whole(gain.shape),
            pl.BlockSpec((columns // steps, width), lambda i: (i, 0)),
        ],
        out_specs=pl.BlockSpec((requests, columns // steps), lambda i: (0, i)),
        scratch_shapes=[pltpu.VMEM((requests, width), jnp.bfloat16)],
    )(rows, gain, weight)


def pick_body(pick_ref, extra_ref, rows_ref, out_ref):
    owners, slots, _ = out_ref.shape
    for k in range(PIECES):
        picked = dot_nn(pick_ref[...], rows_ref[k]).astype(jnp.bfloat16)
        for o in range(owners):
            out_ref[o, :, k * PAIR : (k + 1) * PAIR] = picked[o * slots : (o + 1) * slots]
    for o in range(owners):
        out_ref[o, :, PIECES * PAIR :] = extra_ref[o]


def pick_queries(pick, extra, rows, owners, slots):
    return call(
        pick_body,
        jax.ShapeDtypeStruct((owners, slots, H * KVW + LANES), jnp.bfloat16),
        16,
        2 * owners * slots * rows.shape[1] * H * KVW,
        4 * owners * slots * H * KVW,
    )(pick, extra, rows)


def root_body(root_steps, rows_ref, root_ref, suffix_ref, holder_ref, out_ref, mass_ref, q_ref, m_ref, l_ref, acc_ref):
    step = pl.program_id(0)
    requests = rows_ref.shape[1]

    @pl.when(step == 0)
    def _():
        for k in range(PIECES):
            for j in range(2):
                at = (2 * k + j) * requests
                q_ref[at : at + requests, :] = rows_ref[k, :, j * KVW : (j + 1) * KVW]
        m_ref[...] = jnp.full(m_ref.shape, lowest, jnp.float32)
        l_ref[...] = jnp.zeros(l_ref.shape, jnp.float32)
        acc_ref[...] = jnp.zeros(acc_ref.shape, jnp.float32)

    def take(scores, block_ref):
        peak = jnp.maximum(m_ref[...], jnp.max(scores, axis=-1, keepdims=True))
        weights = jnp.exp2(scores - peak)
        shrink = jnp.exp2(m_ref[...] - peak)
        l_ref[...] = l_ref[...] * shrink + jnp.sum(weights, axis=-1, keepdims=True)
        acc_ref[...] = acc_ref[...] * shrink + dot_nn(
            weights.astype(jnp.bfloat16), block_ref[:, :LAT]
        )
        m_ref[...] = peak

    @pl.when(step < root_steps)
    def _():
        take(dot_nt(q_ref[...], root_ref[...]) * (score_scale * log2e), root_ref)

    @pl.when(step >= root_steps)
    def _():
        scores = dot_nt(q_ref[...], suffix_ref[...]) * (score_scale * log2e)
        request = lax.broadcasted_iota(jnp.int32, (q_ref.shape[0], 1), 0) % requests
        take(jnp.where(holder_ref[...] == request, scores, lowest), suffix_ref)

    @pl.when(step == pl.num_programs(0) - 1)
    def _():
        total = l_ref[...]
        out_ref[...] = acc_ref[...] / total
        mass_ref[...] = jnp.broadcast_to(m_ref[...] * ln2 + jnp.log(total), mass_ref.shape)


def root_attention(rows, root, suffix, holder):
    requests = rows.shape[1]
    count = H * requests
    block = 512
    root_steps, suffix_steps = root.shape[0] // block, suffix.shape[0] // block
    return call(
        functools.partial(root_body, root_steps),
        (
            jax.ShapeDtypeStruct((count, LAT), jnp.float32),
            jax.ShapeDtypeStruct((count, LANES), jnp.float32),
        ),
        32,
        2 * count * (root.shape[0] + suffix.shape[0]) * (KVW + LAT),
        2 * KVW * (root.shape[0] + suffix.shape[0]),
        grid=(root_steps + suffix_steps,),
        in_specs=[
            whole(rows.shape),
            pl.BlockSpec((block, KVW), lambda i: (jnp.minimum(i, root_steps - 1), 0)),
            pl.BlockSpec((block, KVW), lambda i: (jnp.maximum(i - root_steps, 0), 0)),
            pl.BlockSpec((1, block), lambda i: (0, jnp.maximum(i - root_steps, 0))),
        ],
        out_specs=(whole((count, LAT)), whole((count, LANES))),
        scratch_shapes=[
            pltpu.VMEM((count, KVW), jnp.bfloat16),
            pltpu.VMEM((count, 1), jnp.float32),
            pltpu.VMEM((count, 1), jnp.float32),
            pltpu.VMEM((count, LAT), jnp.float32),
        ],
    )(rows, root, suffix, holder)


def group_body(rows_ref, cache_ref, holder_ref, out_ref, q_ref):
    slots = rows_ref.shape[1]
    for h in range(H):
        q_ref[h * slots : (h + 1) * slots, :] = rows_ref[0, :, h * KVW : (h + 1) * KVW]
    asked = rows_ref[0, :, H * KVW :][:, :1].astype(jnp.float32)
    asked = jnp.concatenate([asked] * H, axis=0)
    usable = holder_ref[...] == asked
    scores = dot_nt(q_ref[...], cache_ref[...]) * (score_scale * log2e)
    scores = jnp.where(usable, scores, lowest)
    peak = jnp.max(scores, axis=-1, keepdims=True)
    weights = jnp.where(usable, jnp.exp2(scores - peak), 0.0)
    total = jnp.sum(weights, axis=-1, keepdims=True)
    present = total > 0.0
    safe = jnp.where(present, total, 1.0)
    block_out = dot_nn(weights.astype(jnp.bfloat16), cache_ref[:, :LAT]) / safe
    mass = jnp.where(present, peak * ln2 + jnp.log(safe), lowest)
    lane = lax.broadcasted_iota(jnp.int32, (slots, LANES), 1)
    extra = jnp.zeros((slots, LANES), jnp.float32)
    for h in range(H):
        at = slice(h * slots, (h + 1) * slots)
        out_ref[0, :, h * LAT : (h + 1) * LAT] = block_out[at].astype(jnp.bfloat16)
        for k, part in enumerate(split_three(mass[at])):
            extra = jnp.where(lane == k * H + h, part, extra)
    out_ref[0, :, H * LAT :] = extra.astype(jnp.bfloat16)


def group_attention(rows, cache, holder):
    owners, slots, width = rows.shape
    positions = cache.shape[0]
    return call(
        group_body,
        jax.ShapeDtypeStruct((owners, slots, H * LAT + LANES), jnp.bfloat16),
        32,
        2 * owners * slots * H * positions * (KVW + LAT),
        2 * KVW * positions,
        grid=(owners,),
        in_specs=[
            pl.BlockSpec((1, slots, width), lambda i: (i, 0, 0)),
            whole(cache.shape),
            whole(holder.shape),
        ],
        out_specs=pl.BlockSpec((1, slots, H * LAT + LANES), lambda i: (i, 0, 0)),
        scratch_shapes=[pltpu.VMEM((H * slots, KVW), jnp.bfloat16)],
    )(rows, cache, holder)


def local_body(unpick_ref, back_ref, first_ref, mass_ref, out_ref):
    requests = unpick_ref.shape[0]
    unpick = unpick_ref[...]
    extra = dot_nn(unpick, back_ref[:, H * LAT :])
    lane = lax.broadcasted_iota(jnp.int32, (requests, LANES), 1)
    for h in range(H):
        at = slice(h * requests, (h + 1) * requests)
        group_out = dot_nn(unpick, back_ref[:, h * LAT : (h + 1) * LAT])
        group_mass = (
            extra[:, h : h + 1] + extra[:, H + h : H + h + 1] + extra[:, 2 * H + h : 2 * H + h + 1]
        )
        first_mass = mass_ref[at, :1]
        peak = jnp.maximum(first_mass, group_mass)
        first_weight = jnp.exp(first_mass - peak)
        group_weight = jnp.exp(group_mass - peak)
        total = first_weight + group_weight
        out = (first_weight * first_ref[at, :] + group_weight * group_out) / total
        out_ref[at, :LAT] = out.astype(jnp.bfloat16)
        tail = jnp.zeros((requests, LANES), jnp.float32)
        for k, part in enumerate(split_three(peak + jnp.log(total))):
            tail = jnp.where(lane == k, part, tail)
        out_ref[at, LAT:] = tail.astype(jnp.bfloat16)


def local_join(unpick, back, first, mass):
    count = first.shape[0]
    return call(
        local_body,
        jax.ShapeDtypeStruct((count, LAT + LANES), jnp.bfloat16),
        24,
        2 * unpick.shape[0] * back.shape[0] * back.shape[1],
        4 * count * LAT,
    )(unpick, back, first, mass)


def join_body(parts_ref, out_ref):
    sources, copies = parts_ref.shape[0], out_ref.shape[0]
    tails = [parts_ref[s, :, LAT:].astype(jnp.float32) for s in range(sources)]
    masses = [t[:, 0:1] + t[:, 1:2] + t[:, 2:3] for t in tails]
    peak = functools.reduce(jnp.maximum, masses)
    scales = [jnp.exp(mass - peak) for mass in masses]
    total = functools.reduce(jnp.add, scales)
    out = functools.reduce(
        jnp.add,
        [scales[s] * parts_ref[s, :, :LAT].astype(jnp.float32) for s in range(sources)],
    )
    out = (out / total).astype(jnp.bfloat16)
    for c in range(copies):
        out_ref[c] = out


def join(parts):
    sources, rows, _ = parts.shape
    return call(
        join_body,
        jax.ShapeDtypeStruct((sources, rows, LAT), jnp.bfloat16),
        16,
        2 * sources * rows * LAT,
        4 * sources * rows * LAT,
    )(parts)


def output_body(rows_ref, weight_ref, hidden_ref, out_ref, acc_ref):
    step = pl.program_id(0)
    requests = hidden_ref.shape[0]
    heads = weight_ref.shape[1] // LAT

    @pl.when(step == 0)
    def _():
        acc_ref[...] = hidden_ref[...].astype(jnp.float32)

    acc = acc_ref[...]
    for h in range(heads):
        acc = acc + dot_nt(
            rows_ref[h * requests : (h + 1) * requests, :],
            weight_ref[:, h * LAT : (h + 1) * LAT],
        )
    acc_ref[...] = acc

    @pl.when(step == pl.num_programs(0) - 1)
    def _():
        out_ref[...] = acc.astype(jnp.bfloat16)


def output_projection(rows, weight, hidden):
    features, width = weight.shape
    requests = hidden.shape[0]
    steps = 4
    heads = H // steps
    return call(
        output_body,
        jax.ShapeDtypeStruct(hidden.shape, jnp.bfloat16),
        24,
        2 * requests * features * width,
        2 * features * width,
        grid=(steps,),
        in_specs=[
            pl.BlockSpec((heads * requests, LAT), lambda i: (i, 0)),
            pl.BlockSpec((features, heads * LAT), lambda i: (0, i)),
            whole(hidden.shape),
        ],
        out_specs=whole(hidden.shape),
        scratch_shapes=[pltpu.VMEM(hidden.shape, jnp.float32)],
    )(rows, weight, hidden)


def gated(rows, gate, up):
    gate_part = dot_nt(rows, gate)
    up_part = dot_nt(rows, up)
    return (gate_part / (1.0 + jnp.exp(-gate_part)) * up_part).astype(jnp.bfloat16)


def expert_body(pick_ref, rows_ref, gain_ref, gate_ref, up_ref, down_ref, out_ref, slot_ref, acc_ref):
    step = pl.program_id(0)
    owners, _, requests, part = rows_ref.shape
    width = gain_ref.shape[1]

    @pl.when(step == 0)
    def _():
        rows = jnp.concatenate(
            [
                normalised(lambda k, o=o: rows_ref[o, k], gain_ref[...], width)
                for o in range(owners)
            ],
            axis=0,
        )
        slot_ref[...] = dot_nn(pick_ref[...], rows).astype(jnp.bfloat16)
        acc_ref[...] = jnp.zeros(acc_ref.shape, jnp.float32)

    acc_ref[...] += dot_nn(gated(slot_ref[...], gate_ref[0], up_ref[0]), down_ref[0])

    @pl.when(step == pl.num_programs(0) - 1)
    def _():
        slots = out_ref.shape[2]
        for o in range(owners):
            for k in range(PIECES):
                out_ref[o, k] = acc_ref[
                    o * slots : (o + 1) * slots, k * part : (k + 1) * part
                ].astype(jnp.bfloat16)


def expert(pick, rows, gain, gate, up, down, slots):
    owners, _, requests, part = rows.shape
    _, units, width = gate.shape
    steps = 4 if units % 64 == 0 and units > 704 else 1
    weights = pl.BlockSpec((1, units // steps, width), lambda i: (0, i, 0))
    return call(
        expert_body,
        jax.ShapeDtypeStruct((owners, PIECES, slots, part), jnp.bfloat16),
        40,
        6 * pick.shape[0] * units * width,
        6 * units * width,
        grid=(steps,),
        in_specs=[whole(pick.shape), whole(rows.shape), whole(gain.shape), weights, weights, weights],
        out_specs=whole((owners, PIECES, slots, part)),
        scratch_shapes=[
            pltpu.VMEM((owners * slots, width), jnp.bfloat16),
            pltpu.VMEM((owners * slots, width), jnp.float32),
        ],
    )(pick, rows, gain, gate, up, down)


def shared_body(rows_ref, gain_ref, gate_ref, up_ref, down_ref, out_ref):
    part = rows_ref.shape[2]
    rows = normalised(lambda k: rows_ref[k], gain_ref[...], gain_ref.shape[1])
    out = dot_nn(gated(rows, gate_ref[...], up_ref[...]), down_ref[...])
    for k in range(PIECES):
        out_ref[k] = out[:, k * part : (k + 1) * part].astype(jnp.bfloat16)


def shared_expert(rows, gain, gate, up, down):
    return call(
        shared_body,
        jax.ShapeDtypeStruct(rows.shape, jnp.bfloat16),
        32,
        6 * rows.shape[1] * gate.shape[0] * gate.shape[1],
        6 * gate.shape[0] * gate.shape[1],
    )(rows, gain, gate, up, down)


def final_body(parts_ref, weight_ref, shared_ref, mid_ref, out_ref):
    weight = weight_ref[...]
    high = weight.astype(jnp.bfloat16)
    rest = weight - high.astype(jnp.float32)
    low = rest.astype(jnp.bfloat16)
    lower = (rest - low.astype(jnp.float32)).astype(jnp.bfloat16)
    parts = parts_ref[...]
    total = dot_nn(high, parts) + (dot_nn(low, parts) + dot_nn(lower, parts))
    for k in range(shared_ref.shape[0]):
        total = total + shared_ref[k].astype(jnp.float32)
    out_ref[...] = (mid_ref[...].astype(jnp.float32) + total).astype(jnp.bfloat16)


def final_sum(parts, weight, shared, mid):
    return call(
        final_body,
        jax.ShapeDtypeStruct(mid.shape, jnp.bfloat16),
        24,
        2 * weight.shape[0] * parts.shape[0] * parts.shape[1],
        2 * parts.shape[0] * parts.shape[1],
    )(parts, weight, shared, mid)


def spread(x, axis, count):
    return lax.all_to_all(jnp.broadcast_to(x[None], (count,) + x.shape), axis, 0, 0, tiled=True)


def gather_pieces(x):
    devices = x.shape[-3]
    each = devices // PIECES
    if each == 1:
        return x
    lead, (rows, columns) = x.shape[:-3], x.shape[-2:]
    x = x.reshape(lead + (PIECES, each, rows, columns))
    return jnp.swapaxes(x, -3, -2).reshape(lead + (PIECES, rows, each * columns))


def scatter_pieces(x, devices):
    each = devices // PIECES
    if each == 1:
        return x
    lead, (rows, columns) = x.shape[:-3], x.shape[-2:]
    x = x.reshape(lead + (PIECES, rows, each, columns // each))
    return jnp.swapaxes(x, -3, -2).reshape(lead + (devices, rows, columns // each))


def ranks(hits):
    count = hits.shape[0]
    ahead = jnp.arange(count)[:, None] > jnp.arange(count)[None, :]
    return jnp.sum(jnp.where(ahead[:, :, None], hits.astype(jnp.int32)[None], 0), axis=1)


def local(
    hidden,
    attention_gain,
    query_weight,
    out_weight,
    root_cache,
    group_cache,
    group_length,
    suffix_cache,
    suffix_length,
    group_of,
    mixture_gain,
    routes,
    route_weight,
    expert_gate,
    expert_up,
    expert_down,
    shared_gate,
    shared_up,
    shared_down,
):
    owners, tensors = lax.axis_size("owner"), lax.axis_size("tensor")
    owner_index, tensor_index = lax.axis_index("owner"), lax.axis_index("tensor")
    requests = hidden.shape[0]
    fanout = routes.shape[1]
    split = tensors // EXP_OWN
    slots = -(-2 * requests // (owners * 16)) * 16
    expert_slots = -(-2 * requests * fanout // (EXP_OWN * owners * 16)) * 16

    destination = group_of // GROUP_OWN
    owner_range = jnp.arange(owners)
    to_owner = destination[:, None] == owner_range[None, :]
    slot_rank = ranks(to_owner)
    placed = to_owner[:, :, None] & (slot_rank[:, :, None] == jnp.arange(slots))
    unpick = placed.reshape(requests, owners * slots).astype(jnp.bfloat16)
    pick = unpick.T
    asked = jnp.sum(
        jnp.where(placed, (group_of % GROUP_OWN + 1)[:, None, None], 0), axis=0
    ).astype(jnp.bfloat16)
    named = routes.astype(jnp.bfloat16).reshape(slots, requests * fanout // slots)
    extra = jnp.concatenate(
        [
            asked[:, :, None],
            jnp.broadcast_to(named[None], (owners,) + named.shape),
            jnp.zeros((owners, slots, LANES - 1 - named.shape[1]), jnp.bfloat16),
        ],
        axis=2,
    )
    suffix_span, group_span = suffix_cache.shape[1], group_cache.shape[1]
    suffix_usable = (
        tensor_index * suffix_span + jnp.arange(suffix_span)[None, :] < suffix_length[:, None]
    )
    suffix_holder = jnp.where(suffix_usable, jnp.arange(requests)[:, None], -1).reshape(1, -1)
    group_usable = (
        tensor_index * group_span + jnp.arange(group_span)[None, :] < group_length[:, None]
    )
    group_holder = (
        jnp.where(group_usable, jnp.arange(1, GROUP_OWN + 1)[:, None], -1)
        .reshape(1, -1)
        .astype(jnp.float32)
    )
    experts = jnp.arange(owners * EXP_OWN)
    hits = routes[:, :, None] == experts[None, None, :]
    share = jnp.sum(jnp.where(hits, route_weight[:, :, None], 0.0), axis=1)
    hit = jnp.any(hits, axis=1)
    taken = hit[:, :, None] & (ranks(hit)[:, :, None] == jnp.arange(expert_slots))
    back_weight = jnp.where(taken, share[:, :, None], 0.0)
    back_weight = jnp.repeat(back_weight, split, axis=1).reshape(requests, -1)

    rows = gather_pieces(spread(hidden, "tensor", tensors))
    projected = project(rows, attention_gain.astype(jnp.float32)[None], query_weight)
    queries = gather_pieces(spread(projected, "tensor", tensors))
    sent = pick_queries(pick, extra, queries, owners, slots)
    arrived = lax.all_to_all(sent, "owner", 0, 0, tiled=True)
    first, mass = root_attention(
        queries, root_cache, suffix_cache.reshape(-1, KVW), suffix_holder
    )
    answered = group_attention(arrived, group_cache.reshape(-1, KVW), group_holder)
    back = lax.all_to_all(answered, "owner", 0, 0, tiled=True)
    parts = local_join(unpick, back.reshape(owners * slots, -1), first, mass)
    parts = lax.all_to_all(
        parts.reshape(tensors, -1, LAT + LANES), "tensor", 0, 0, tiled=True
    )
    attention = lax.all_to_all(join(parts), "tensor", 0, 0, tiled=True)
    mid = output_projection(attention.reshape(-1, LAT), out_weight, hidden)

    everything = spread(mid, ("owner", "tensor"), owners * tensors)
    everything = gather_pieces(everything.reshape((owners, tensors) + mid.shape))
    gain = mixture_gain.astype(jnp.float32)[None]
    all_routes = (
        arrived[:, :, H * KVW + 1 : H * KVW + 1 + named.shape[1]]
        .reshape(owners, requests, fanout)
        .astype(jnp.int32)
    )
    mine = owner_index * EXP_OWN + tensor_index // split
    called = jnp.any(all_routes == mine, axis=2)
    call_rank = ranks(called.T).T
    expert_pick = called[:, None, :] & (
        call_rank[:, None, :] == jnp.arange(expert_slots)[None, :, None]
    )
    expert_pick = jnp.where(
        (owner_range[:, None] == owner_range[None, :])[:, None, :, None],
        expert_pick[:, :, None, :],
        False,
    )
    expert_pick = expert_pick.reshape(owners * expert_slots, owners * requests).astype(jnp.bfloat16)
    results = expert(
        expert_pick, everything, gain, expert_gate, expert_up, expert_down, expert_slots
    )
    results = scatter_pieces(results, tensors).reshape(
        (owners * tensors, expert_slots, mid.shape[1])
    )
    returned = lax.all_to_all(results, ("owner", "tensor"), 0, 0, tiled=True)
    own_rows = lax.dynamic_index_in_dim(everything, owner_index, 0, keepdims=False)
    shared = shared_expert(own_rows, gain, shared_gate, shared_up, shared_down)
    shared = lax.all_to_all(scatter_pieces(shared, tensors), "tensor", 0, 0, tiled=True)
    return final_sum(returned.reshape(-1, mid.shape[1]), back_weight, shared, mid)


def solution(mesh):
    return jax.shard_map(
        local,
        mesh=mesh,
        in_specs=(
            P("owner", "tensor"),
            P(),
            P("tensor", None),
            P("tensor", None),
            P("tensor", None),
            P("owner", "tensor", None),
            P("owner"),
            P("owner", "tensor", None),
            P("owner"),
            P("owner"),
            P(),
            P("owner", None),
            P("owner", None),
            P(("owner", "tensor"), None, None),
            P(("owner", "tensor"), None, None),
            P(("owner", "tensor"), None, None),
            P("tensor", None),
            P("tensor", None),
            P("tensor", None),
        ),
        out_specs=P("owner", "tensor"),
        check_vma=False,
    )
```

```python
import functools

import jax
import jax.numpy as jnp
from jax import lax
from jax.experimental import pallas as pl
from jax.experimental.pallas import tpu as pltpu
from jax.sharding import Mesh
from jax.sharding import PartitionSpec as P

H = 16
LAT = 512
KVW = 576
EXP_OWN = 8
GROUP_OWN = 12
PIECES = 8
PAIR = 2 * KVW
LANES = 128
OWNER = ("pair", "core")
MASS_ROWS = 8
MIB = 1 << 20

score_scale = 192.0 ** (-0.5)
log2e = 1.4426950408889634
ln2 = 0.6931471805599453
lowest = -1e30
epsilon = 1e-06

NT = (((1,), (1,)), ((), ()))


def dot_nt(a, b):
    return lax.dot_general(a, b, NT, preferred_element_type=jnp.float32)


def dot_nn(a, b):
    return jnp.dot(a, b, preferred_element_type=jnp.float32)


def call(body, out_shape, vmem_mib, flops, nbytes, **options):
    return pl.pallas_call(
        body,
        out_shape=out_shape,
        compiler_params=pltpu.CompilerParams(vmem_limit_bytes=vmem_mib * MIB),
        cost_estimate=pl.CostEstimate(
            flops=int(flops), bytes_accessed=int(nbytes), transcendentals=0
        ),
        **options,
    )


VMEM = pl.BlockSpec(memory_space=pltpu.VMEM)
HBM = pl.BlockSpec(memory_space=pltpu.HBM)


def in_hbm(x):
    return pltpu.with_memory_space_constraint(x, pltpu.HBM)


def whole(shape):
    return pl.BlockSpec(shape, lambda *_: (0,) * len(shape))


def split_three(column):
    first = column.astype(jnp.bfloat16).astype(jnp.float32)
    second = (column - first).astype(jnp.bfloat16).astype(jnp.float32)
    third = (column - first - second).astype(jnp.bfloat16).astype(jnp.float32)
    return first, second, third


def normalised(read_piece, gain, width):
    rows = jnp.concatenate([read_piece(k) for k in range(PIECES)], axis=-1).astype(jnp.float32)
    square = jnp.sum(rows * rows, axis=-1, keepdims=True) * (1.0 / width)
    return (rows * lax.rsqrt(square + epsilon) * gain.astype(jnp.float32)).astype(jnp.bfloat16)


def project_body(rows_ref, gain_ref, weight_hbm, out_ref, weight_ref, sems):
    steps, each, width = weight_ref.shape
    copies = [
        pltpu.make_async_copy(
            weight_hbm.at[pl.ds(c * each, each)], weight_ref.at[c], sems.at[c]
        )
        for c in range(steps)
    ]
    for copy in copies:
        copy.start()
    normed = normalised(lambda k: rows_ref[k], gain_ref[...], width)
    for step in range(steps):
        copies[step].wait()
        out = dot_nt(normed, weight_ref[step]).astype(jnp.bfloat16)
        for k in range(out_ref.shape[0]):
            out_ref[k, :, step * each : (step + 1) * each] = out


def project(rows, gain, weight, copies):
    pieces, requests, part = rows.shape
    columns, width = weight.shape
    steps = 3 if columns % (3 * LANES) == 0 else 1
    return call(
        project_body,
        jax.ShapeDtypeStruct((copies, requests, columns), jnp.bfloat16),
        16,
        2 * requests * columns * width,
        2 * columns * width,
        in_specs=[VMEM, VMEM, HBM],
        out_specs=VMEM,
        scratch_shapes=[
            pltpu.VMEM((steps, columns // steps, width), jnp.bfloat16),
            pltpu.SemaphoreType.DMA((steps,)),
        ],
    )(rows, gain, in_hbm(weight))


def pick_body(pick_ref, extra_ref, rows_ref, out_ref):
    owners, slots, _ = out_ref.shape
    for k in range(PIECES):
        picked = dot_nn(pick_ref[...], rows_ref[k]).astype(jnp.bfloat16)
        for o in range(owners):
            out_ref[o, :, k * PAIR : (k + 1) * PAIR] = picked[o * slots : (o + 1) * slots]
    for o in range(owners):
        out_ref[o, :, PIECES * PAIR :] = extra_ref[o]


def pick_queries(pick, extra, rows, owners, slots):
    return call(
        pick_body,
        jax.ShapeDtypeStruct((owners, slots, H * KVW + LANES), jnp.bfloat16),
        16,
        2 * owners * slots * rows.shape[1] * H * KVW,
        4 * owners * slots * H * KVW,
    )(pick, extra, rows)


def running_softmax(scores, value_dot, at, m_ref, l_ref, acc_ref):
    before = m_ref[at, :]
    peak = jnp.maximum(before, jnp.max(scores, axis=-1, keepdims=True))
    weights = jnp.exp2(scores - peak)
    shrink = jnp.exp2(before - peak)
    l_ref[at, :] = l_ref[at, :] * shrink + jnp.sum(weights, axis=-1, keepdims=True)
    acc_ref[at, :] = acc_ref[at, :] * shrink + value_dot(weights.astype(jnp.bfloat16))
    m_ref[at, :] = peak


def finish(out_ref, m_ref, l_ref, acc_ref):
    total = l_ref[...]
    out_ref[:, :LAT] = acc_ref[...] / total
    out_ref[:, LAT:] = jnp.broadcast_to(
        m_ref[...] * ln2 + jnp.log(total), (total.shape[0], LANES)
    )


def by_head(rows_ref, q_ref):
    requests = rows_ref.shape[1]
    for k in range(PIECES):
        for j in range(2):
            at = (2 * k + j) * requests
            q_ref[at : at + requests, :] = rows_ref[k, :, j * KVW : (j + 1) * KVW]


def halves_of(count):
    return [slice(0, count // 2), slice(count // 2, count)]


def attention_scratch(count):
    return [
        pltpu.VMEM((count, KVW), jnp.bfloat16),
        pltpu.VMEM((count, 1), jnp.float32),
        pltpu.VMEM((count, 1), jnp.float32),
        pltpu.VMEM((count, LAT), jnp.float32),
    ]


def root_body(rows_ref, cache_ref, out_ref, q_ref, m_ref, l_ref, acc_ref):
    step = pl.program_id(0)

    @pl.when(step == 0)
    def _():
        by_head(rows_ref, q_ref)
        m_ref[...] = jnp.full(m_ref.shape, lowest, jnp.float32)
        l_ref[...] = jnp.zeros(l_ref.shape, jnp.float32)
        acc_ref[...] = jnp.zeros(acc_ref.shape, jnp.float32)

    halves = halves_of(q_ref.shape[0])
    scores = [dot_nn(q_ref[at, :], cache_ref[...]) * (score_scale * log2e) for at in halves]
    for at, block in zip(halves, scores):
        running_softmax(
            block, lambda w: dot_nt(w, cache_ref[:LAT, :]), at, m_ref, l_ref, acc_ref
        )

    @pl.when(step == pl.num_programs(0) - 1)
    def _():
        finish(out_ref, m_ref, l_ref, acc_ref)


def root_attention(rows, cache):
    count = H * rows.shape[1]
    positions = cache.shape[1]
    block = min(1024, positions)
    return call(
        root_body,
        pltpu.HBM((count, LAT + LANES), jnp.float32),
        32,
        2 * count * positions * (KVW + LAT),
        2 * KVW * positions,
        grid=(positions // block,),
        in_specs=[whole(rows.shape), pl.BlockSpec((KVW, block), lambda i: (0, i))],
        out_specs=whole((count, LAT + LANES)),
        scratch_shapes=attention_scratch(count),
    )(rows, in_hbm(cache))


def suffix_body(rows_ref, cache_ref, holder_ref, first_ref, out_ref, q_ref):
    requests = rows_ref.shape[1]
    each = q_ref.shape[1] // H
    group = pl.program_id(0)
    for k in range(PIECES):
        for j in range(2):
            h = 2 * k + j
            q_ref[0, h * each : (h + 1) * each, :] = rows_ref[
                k, pl.ds(pl.multiple_of(group * each, each), each), j * KVW : (j + 1) * KVW
            ]
    scores = dot_nt(q_ref[0], cache_ref[...]) * (score_scale * log2e)
    request = lax.broadcasted_iota(jnp.int32, (H * each, 1), 0) % each + group * each
    usable = holder_ref[...] == request
    scores = jnp.where(usable, scores, lowest)
    first = jnp.concatenate(
        [
            first_ref[pl.ds(pl.multiple_of(h * requests + group * each, each), each), :]
            for h in range(H)
        ],
        axis=0,
    )
    mass = first[:, LAT : LAT + 1] * log2e
    peak = jnp.maximum(mass, jnp.max(scores, axis=-1, keepdims=True))
    weights = jnp.exp2(scores - peak)
    shrink = jnp.exp2(mass - peak)
    total = shrink + jnp.sum(weights, axis=-1, keepdims=True)
    out = first[:, :LAT] * shrink + dot_nn(weights.astype(jnp.bfloat16), cache_ref[:, :LAT])
    out = out / total
    mass = jnp.broadcast_to(peak * ln2 + jnp.log(total), (H * each, LANES))
    for h in range(H):
        at = pl.ds(pl.multiple_of(h * requests + group * each, each), each)
        out_ref[at, :LAT] = out[h * each : (h + 1) * each]
        out_ref[at, LAT:] = mass[h * each : (h + 1) * each]


def suffix_attention(rows, cache, holder, first):
    requests = rows.shape[1]
    count = H * requests
    positions = cache.shape[0]
    groups = 2
    block = positions // groups
    return call(
        suffix_body,
        pltpu.HBM((count, LAT + LANES), jnp.float32),
        32,
        2 * count * block * (KVW + LAT),
        2 * KVW * positions,
        grid=(groups,),
        in_specs=[
            whole(rows.shape),
            pl.BlockSpec((block, KVW), lambda i: (i, 0)),
            pl.BlockSpec((1, block), lambda i: (0, i)),
            whole((count, LAT + LANES)),
        ],
        out_specs=whole((count, LAT + LANES)),
        scratch_shapes=[pltpu.VMEM((1, count // groups, KVW), jnp.bfloat16)],
    )(rows, in_hbm(cache), holder, in_hbm(first))


def group_body(rows_ref, cache_hbm, holder_ref, out_hbm, q_ref, keys_ref, out_ref, sems, out_sems):
    owners, slots, _ = rows_ref.shape
    groups, _, span = cache_hbm.shape
    copies = [
        pltpu.make_async_copy(
            cache_hbm.at[g], keys_ref.at[:, pl.ds(g * span, span)], sems.at[g]
        )
        for g in range(groups)
    ]
    for copy in copies:
        copy.start()
    for o in range(owners):
        for h in range(H):
            q_ref[o, h * slots : (h + 1) * slots, :] = rows_ref[o, :, h * KVW : (h + 1) * KVW]
    for copy in copies:
        copy.wait()
    lane = lax.broadcasted_iota(jnp.int32, (slots, LANES), 1)
    scores = [dot_nn(q_ref[o], keys_ref[...]) for o in range(owners)]
    sent = []
    for o in range(owners):
        asked = rows_ref[o, :, H * KVW :][:, :1].astype(jnp.float32)
        asked = jnp.concatenate([asked] * H, axis=0)
        usable = holder_ref[...] == asked
        block = jnp.where(usable, scores[o] * (score_scale * log2e), lowest)
        peak = jnp.max(block, axis=-1, keepdims=True)
        weights = jnp.where(usable, jnp.exp2(block - peak), 0.0)
        total = jnp.sum(weights, axis=-1, keepdims=True)
        present = total > 0.0
        safe = jnp.where(present, total, 1.0)
        block_out = dot_nt(weights.astype(jnp.bfloat16), keys_ref[:LAT, :]) / safe
        mass = jnp.where(present, peak * ln2 + jnp.log(safe), lowest)
        extra = jnp.zeros((slots, LANES), jnp.float32)
        for h in range(H):
            at = slice(h * slots, (h + 1) * slots)
            out_ref[o, :, h * LAT : (h + 1) * LAT] = block_out[at].astype(jnp.bfloat16)
            for k, part in enumerate(split_three(mass[at])):
                extra = jnp.where(lane == k * H + h, part, extra)
        out_ref[o, :, H * LAT :] = extra.astype(jnp.bfloat16)
        copy = pltpu.make_async_copy(out_ref.at[o], out_hbm.at[o], out_sems.at[o])
        copy.start()
        sent.append(copy)
    for copy in sent:
        copy.wait()


def group_attention(rows, cache, holder):
    owners, slots, _ = rows.shape
    groups, _, span = cache.shape
    width = H * LAT + LANES
    return call(
        group_body,
        pltpu.HBM((owners, slots, width), jnp.bfloat16),
        40,
        2 * owners * slots * H * groups * span * (KVW + LAT),
        2 * KVW * groups * span,
        in_specs=[VMEM, HBM, VMEM],
        out_specs=HBM,
        scratch_shapes=[
            pltpu.VMEM((owners, H * slots, KVW), jnp.bfloat16),
            pltpu.VMEM((KVW, groups * span), jnp.bfloat16),
            pltpu.VMEM((owners, slots, width), jnp.bfloat16),
            pltpu.SemaphoreType.DMA((groups,)),
            pltpu.SemaphoreType.DMA((owners,)),
        ],
    )(rows, in_hbm(cache), holder)


def local_body(unpick_ref, back_ref, first_hbm, out_ref, first_ref, out_mass_ref, sem):
    copy = pltpu.make_async_copy(first_hbm, first_ref, sem)
    copy.start()
    requests = unpick_ref.shape[0]
    unpick = unpick_ref[...]
    extra = dot_nn(unpick, back_ref[:, H * LAT :])
    shares, length = out_ref.shape[0], out_ref.shape[1] - MASS_ROWS
    copy.wait()
    for h in range(H):
        at = slice(h * requests, (h + 1) * requests)
        group_out = dot_nn(unpick, back_ref[:, h * LAT : (h + 1) * LAT])
        group_mass = (
            extra[:, h : h + 1] + extra[:, H + h : H + h + 1] + extra[:, 2 * H + h : 2 * H + h + 1]
        )
        first_mass = first_ref[at, LAT : LAT + 1]
        peak = jnp.maximum(first_mass, group_mass)
        first_weight = jnp.exp(first_mass - peak)
        group_weight = jnp.exp(group_mass - peak)
        total = first_weight + group_weight
        out = (first_weight * first_ref[at, :LAT] + group_weight * group_out) / total
        out = out.astype(jnp.bfloat16)
        each = min(length, requests)
        for k in range(requests // each):
            share, row = divmod(h * requests + k * each, length)
            out_ref[share, row : row + each, :] = out[k * each : (k + 1) * each]
        out_mass_ref[at, :] = peak + jnp.log(total)
    diagonal = lax.broadcasted_iota(jnp.int32, (length, LAT), 0) == lax.broadcasted_iota(
        jnp.int32, (length, LAT), 1
    )
    row = lax.broadcasted_iota(jnp.int32, (MASS_ROWS, LAT), 0)
    for share in range(shares):
        masses = jnp.where(diagonal, out_mass_ref[share * length : (share + 1) * length, :], 0.0)
        masses = jnp.sum(masses, axis=0, keepdims=True)
        tail = jnp.zeros((MASS_ROWS, LAT), jnp.float32)
        for k, part in enumerate(split_three(masses)):
            tail = jnp.where(row == k, part, tail)
        out_ref[share, length:, :] = tail.astype(jnp.bfloat16)


def local_join(unpick, back, first, shares):
    count = first.shape[0]
    return call(
        local_body,
        jax.ShapeDtypeStruct((shares, count // shares + MASS_ROWS, LAT), jnp.bfloat16),
        10,
        2 * unpick.shape[0] * back.shape[0] * back.shape[1],
        4 * count * LAT,
        in_specs=[VMEM, VMEM, HBM],
        out_specs=VMEM,
        scratch_shapes=[
            pltpu.VMEM(first.shape, jnp.float32),
            pltpu.VMEM((count, 1), jnp.float32),
            pltpu.SemaphoreType.DMA,
        ],
    )(unpick, back, in_hbm(first))


def join_body(parts_ref, out_ref):
    sources, copies, length = parts_ref.shape[0], out_ref.shape[0], out_ref.shape[1]
    diagonal = lax.broadcasted_iota(jnp.int32, (length, LAT), 0) == lax.broadcasted_iota(
        jnp.int32, (length, LAT), 1
    )
    masses = []
    for s in range(sources):
        tail = parts_ref[s, length:, :].astype(jnp.float32)
        mass = tail[0:1] + tail[1:2] + tail[2:3]
        masses.append(jnp.sum(jnp.where(diagonal, mass, 0.0), axis=1, keepdims=True))
    peak = functools.reduce(jnp.maximum, masses)
    scales = [jnp.exp(mass - peak) for mass in masses]
    total = functools.reduce(jnp.add, scales)
    out = functools.reduce(
        jnp.add,
        [scales[s] * parts_ref[s, :length, :].astype(jnp.float32) for s in range(sources)],
    )
    out = (out / total).astype(jnp.bfloat16)
    for c in range(copies):
        out_ref[c] = out


def join(parts):
    sources, rows, _ = parts.shape
    rows -= MASS_ROWS
    return call(
        join_body,
        jax.ShapeDtypeStruct((sources, rows, LAT), jnp.bfloat16),
        6,
        3e10,
        4 * sources * rows * LAT,
    )(parts)


def output_body(rows_ref, weight_ref, hidden_ref, out_ref, copies_ref):
    requests = hidden_ref.shape[0]
    total = hidden_ref[...].astype(jnp.float32)
    for h in range(H):
        total = total + dot_nt(
            rows_ref[h * requests : (h + 1) * requests, :],
            weight_ref[:, h * LAT : (h + 1) * LAT],
        )
    out = total.astype(jnp.bfloat16)
    out_ref[...] = out
    for c in range(copies_ref.shape[0]):
        copies_ref[c] = out


def output_projection(rows, weight, hidden, copies):
    features, width = weight.shape
    requests = hidden.shape[0]
    return call(
        output_body,
        (
            jax.ShapeDtypeStruct(hidden.shape, jnp.bfloat16),
            jax.ShapeDtypeStruct((copies,) + hidden.shape, jnp.bfloat16),
        ),
        8,
        2 * requests * features * width,
        2 * features * width,
        in_specs=[VMEM] * 3,
        out_specs=(VMEM, VMEM),
    )(rows, weight, hidden)


def gated(rows, gate, up):
    gate_part = dot_nt(rows, gate)
    up_part = dot_nt(rows, up)
    return (gate_part / (1.0 + jnp.exp(-gate_part)) * up_part).astype(jnp.bfloat16)


def expert_body(pick_ref, rows_ref, gain_ref, shared_gate_ref, shared_up_ref, shared_down_ref, gate_ref, up_ref, down_ref, out_ref):
    owners, _, requests, part = rows_ref.shape
    width = gain_ref.shape[1]
    share = requests // owners
    slots = out_ref.shape[2] - share
    rows = jnp.concatenate(
        [
            normalised(lambda k, o=o: rows_ref[o, k], gain_ref[...], width)
            for o in range(owners)
        ],
        axis=0,
    )
    rows = dot_nn(pick_ref[...], rows).astype(jnp.bfloat16)
    named, rest = rows[: owners * slots], rows[owners * slots :]
    shared = dot_nn(gated(rest, shared_gate_ref[...], shared_up_ref[...]), shared_down_ref[...])
    units = gate_ref.shape[1]
    steps = 4 if units % 64 == 0 and units > 704 else 1
    each = units // steps
    total = jnp.zeros((owners * slots, width), jnp.float32)
    for c in range(steps):
        at = slice(c * each, (c + 1) * each)
        total = total + dot_nn(
            gated(named, gate_ref[0, at, :], up_ref[0, at, :]), down_ref[0, at, :]
        )
    for o in range(owners):
        both = jnp.concatenate(
            [total[o * slots : (o + 1) * slots], shared[o * share : (o + 1) * share]], axis=0
        ).astype(jnp.bfloat16)
        for k in range(PIECES):
            out_ref[o, k] = both[:, k * part : (k + 1) * part]


def expert(pick, rows, gain, slots, shared, weights):
    owners, _, requests, part = rows.shape
    _, units, width = weights[0].shape
    return call(
        expert_body,
        jax.ShapeDtypeStruct(
            (owners, PIECES, slots + requests // owners, part), jnp.bfloat16
        ),
        12,
        6 * pick.shape[0] * units * width,
        6 * units * width,
        in_specs=[VMEM] * 9,
        out_specs=VMEM,
    )(pick, rows, gain, *shared, *weights)


def final_body(parts_ref, weight_ref, mid_ref, out_ref):
    weight = weight_ref[...]
    high = weight.astype(jnp.bfloat16)
    rest = weight - high.astype(jnp.float32)
    low = rest.astype(jnp.bfloat16)
    lower = (rest - low.astype(jnp.float32)).astype(jnp.bfloat16)
    parts = parts_ref[...]
    total = dot_nn(high, parts) + (dot_nn(low, parts) + dot_nn(lower, parts))
    out_ref[...] = (mid_ref[...].astype(jnp.float32) + total).astype(jnp.bfloat16)


def final_sum(parts, weight, mid):
    return call(
        final_body,
        jax.ShapeDtypeStruct(mid.shape, jnp.bfloat16),
        16,
        2 * weight.shape[0] * parts.shape[0] * parts.shape[1],
        2 * parts.shape[0] * parts.shape[1],
    )(parts, weight, mid)


def exchange(x, axis):
    return lax.all_to_all(x, axis, 0, 0, tiled=True)


def gather_pieces(x):
    devices = x.shape[-3]
    each = devices // PIECES
    if each == 1:
        return x
    lead, (rows, columns) = x.shape[:-3], x.shape[-2:]
    x = x.reshape(lead + (PIECES, each, rows, columns))
    return jnp.swapaxes(x, -3, -2).reshape(lead + (PIECES, rows, each * columns))


def scatter_pieces(x, devices):
    each = devices // PIECES
    if each == 1:
        return x
    lead, (rows, columns) = x.shape[:-3], x.shape[-2:]
    x = x.reshape(lead + (PIECES, rows, each, columns // each))
    return jnp.swapaxes(x, -3, -2).reshape(lead + (devices, rows, columns // each))


def ranks(hits):
    count = hits.shape[0]
    ahead = jnp.arange(count)[:, None] > jnp.arange(count)[None, :]
    return jnp.sum(jnp.where(ahead[:, :, None], hits.astype(jnp.int32)[None], 0), axis=1)


def local(
    hidden,
    attention_gain,
    query_weight,
    out_weight,
    root_cache,
    group_cache,
    group_length,
    suffix_cache,
    suffix_length,
    group_of,
    mixture_gain,
    routes,
    route_weight,
    expert_gate,
    expert_up,
    expert_down,
    shared_gate,
    shared_up,
    shared_down,
):
    owners, tensors = lax.axis_size(OWNER), lax.axis_size("tensor")
    owner_index, tensor_index = lax.axis_index(OWNER), lax.axis_index("tensor")
    requests = hidden.shape[0]
    fanout = routes.shape[1]
    pairs = owners // 2
    split = tensors // EXP_OWN
    slots = -(-2 * requests // (owners * 16)) * 16
    expert_slots = -(-2 * requests * fanout // (EXP_OWN * owners * 16)) * 16

    if group_cache.shape[1] % LANES:
        group_columns = group_cache.reshape(-1, KVW).T[None]
    else:
        group_columns = jnp.swapaxes(group_cache, 1, 2)
    rows = exchange(jnp.broadcast_to(hidden[None], (tensors,) + hidden.shape), "tensor")

    projected = project(
        gather_pieces(rows), attention_gain[None], query_weight, tensors
    )
    projected, group_of, group_length, suffix_length, routes, route_weight = (
        lax.optimization_barrier(
            (projected, group_of, group_length, suffix_length, routes, route_weight)
        )
    )
    destination = group_of // GROUP_OWN
    owner_range = jnp.arange(owners)
    to_owner = destination[:, None] == owner_range[None, :]
    slot_rank = ranks(to_owner)
    placed = to_owner[:, :, None] & (slot_rank[:, :, None] == jnp.arange(slots))
    unpick = placed.reshape(requests, owners * slots).astype(jnp.bfloat16)
    pick = unpick.T
    asked = jnp.sum(
        jnp.where(placed, (group_of % GROUP_OWN + 1)[:, None, None], 0), axis=0
    ).astype(jnp.bfloat16)
    named = routes.astype(jnp.bfloat16).reshape(slots, requests * fanout // slots)
    extra = jnp.where(
        jnp.arange(LANES) == 0,
        asked[:, :, None],
        jnp.pad(named, ((0, 0), (1, LANES - 1 - named.shape[1])))[None],
    )
    suffix_span, group_span = suffix_cache.shape[1], group_cache.shape[1]
    suffix_usable = (
        tensor_index * suffix_span + jnp.arange(suffix_span)[None, :] < suffix_length[:, None]
    )
    suffix_holder = jnp.where(suffix_usable, jnp.arange(requests)[:, None], -1).reshape(1, -1)
    group_usable = (
        tensor_index * group_span + jnp.arange(group_span)[None, :] < group_length[:, None]
    )
    group_holder = (
        jnp.where(group_usable, jnp.arange(1, GROUP_OWN + 1)[:, None], -1)
        .reshape(1, -1)
        .astype(jnp.float32)
    )
    experts = jnp.arange(owners * EXP_OWN)
    hits = routes[:, :, None] == experts[None, None, :]
    share = jnp.sum(jnp.where(hits, route_weight[:, :, None], 0.0), axis=1)
    hit = jnp.any(hits, axis=1)
    taken = hit[:, :, None] & (ranks(hit)[:, :, None] == jnp.arange(expert_slots))
    back_weight = jnp.where(taken, share[:, :, None], 0.0)
    back_weight = jnp.repeat(back_weight, split, axis=1)
    token_share = requests // owners
    shared_token = owner_range[:, None] * token_share + jnp.arange(token_share)
    shared_weight = shared_token.reshape(-1)[None, :] == jnp.arange(requests)[:, None]
    shared_weight = jnp.broadcast_to(
        shared_weight.reshape(requests, owners, 1, token_share).astype(jnp.float32),
        (requests, owners, tensors, token_share),
    ).reshape(requests, owners * tensors, token_share)
    back_weight = jnp.concatenate([back_weight, shared_weight], axis=2).reshape(requests, -1)

    queries, back_weight, suffix_holder, group_holder = lax.optimization_barrier(
        (exchange(projected, "tensor"), back_weight, suffix_holder, group_holder)
    )
    queries = gather_pieces(queries)
    arrived = exchange(pick_queries(pick, extra, queries, owners, slots), OWNER)
    if group_span % LANES:
        group_columns = group_cache.reshape(-1, KVW).T[None]
    else:
        group_columns = jnp.swapaxes(group_cache, 1, 2)
    first = root_attention(queries, root_cache.T)
    arrived, first = lax.optimization_barrier((arrived, first))
    all_routes = (
        arrived[:, :, H * KVW + 1 : H * KVW + 1 + named.shape[1]]
        .reshape(owners, requests, fanout)
        .astype(jnp.int32)
    )
    mine = owner_index * EXP_OWN + tensor_index // split
    called = jnp.any(all_routes == mine, axis=2)
    call_rank = ranks(called.T).T
    expert_pick = called[:, None, :] & (
        call_rank[:, None, :] == jnp.arange(expert_slots)[None, :, None]
    )
    seen = owner_range.reshape(2, pairs)
    seen = 2 * (seen % pairs) + seen // pairs
    expert_pick = jnp.where(
        (owner_range[:, None] == seen.reshape(-1)[None, :])[:, None, :, None],
        expert_pick[:, :, None, :],
        False,
    )
    shared_pick = (
        owner_range[:, None, None] * requests
        + owner_index * token_share
        + jnp.arange(token_share)[None, :, None]
    ).reshape(-1, 1) == (seen.reshape(-1, 1) * requests + jnp.arange(requests)).reshape(1, -1)
    expert_pick = jnp.concatenate(
        [expert_pick.reshape(owners * expert_slots, owners * requests), shared_pick], axis=0
    ).astype(jnp.bfloat16)
    answered = group_attention(arrived, group_columns, group_holder)
    back = exchange(answered, OWNER)
    first = suffix_attention(queries, suffix_cache.reshape(-1, KVW), suffix_holder, first)
    back, expert_pick, gain = lax.optimization_barrier((back, expert_pick, mixture_gain[None]))
    parts = local_join(unpick, back.reshape(owners * slots, -1), first, tensors)
    attention = exchange(join(exchange(parts, "tensor")), "tensor")
    mid, copies = output_projection(
        attention.reshape(-1, LAT), out_weight, hidden, owners // 2 * tensors
    )

    half = exchange(copies, ("pair", "tensor"))
    both = lax.all_gather(half.reshape((pairs, tensors) + mid.shape), "core")
    everything = gather_pieces(both.reshape((owners, tensors) + mid.shape))
    results = expert(
        expert_pick,
        everything,
        gain,
        expert_slots,
        (shared_gate, shared_up, shared_down),
        (expert_gate, expert_up, expert_down),
    )
    results = scatter_pieces(results, tensors).reshape((owners * tensors, -1, mid.shape[1]))
    returned = exchange(results, ("pair", "core", "tensor"))
    return final_sum(returned.reshape(-1, mid.shape[1]), back_weight, mid)


def solution(mesh):
    owners, tensors = mesh.shape["owner"], mesh.shape["tensor"]
    devices = mesh.devices.reshape(owners // 2, 2, tensors)
    return jax.shard_map(
        local,
        mesh=Mesh(devices, OWNER + ("tensor",)),
        in_specs=(
            P(OWNER, "tensor"),
            P(),
            P("tensor", None),
            P("tensor", None),
            P("tensor", None),
            P(OWNER, "tensor", None),
            P(OWNER),
            P(OWNER, "tensor", None),
            P(OWNER),
            P(OWNER),
            P(),
            P(OWNER, None),
            P(OWNER, None),
            P(OWNER + ("tensor",), None, None),
            P(OWNER + ("tensor",), None, None),
            P(OWNER + ("tensor",), None, None),
            P("tensor", None),
            P("tensor", None),
            P("tensor", None),
        ),
        out_specs=P(OWNER, "tensor"),
        check_vma=False,
    )
```

```python
import functools

import jax
import jax.numpy as jnp
import numpy as np
from jax import lax
from jax.experimental import pallas as pl
from jax.experimental.pallas import tpu as pltpu
from jax.sharding import Mesh
from jax.sharding import PartitionSpec as P

H = 16
LAT = 512
KVW = 576
EXP_OWN = 8
GROUP_OWN = 12
PIECES = 8
PAIR = 2 * KVW
LANES = 128
OWNER = ("pair", "core")
SHARES = 2
HEADS = H // SHARES
MASS_ROWS = 8
MIB = 1 << 20

score_scale = 192.0 ** (-0.5)
log2e = 1.4426950408889634
ln2 = 0.6931471805599453
lowest = -1e30
epsilon = 1e-06

NT = (((1,), (1,)), ((), ()))


def dot_nt(a, b):
    return lax.dot_general(a, b, NT, preferred_element_type=jnp.float32)


def dot_nn(a, b):
    return jnp.dot(a, b, preferred_element_type=jnp.float32)


def call(body, out_shape, vmem_mib, flops, nbytes, **options):
    return pl.pallas_call(
        body,
        out_shape=out_shape,
        compiler_params=pltpu.CompilerParams(vmem_limit_bytes=vmem_mib * MIB),
        cost_estimate=pl.CostEstimate(
            flops=int(flops), bytes_accessed=int(nbytes), transcendentals=0
        ),
        **options,
    )


VMEM = pl.BlockSpec(memory_space=pltpu.VMEM)
HBM = pl.BlockSpec(memory_space=pltpu.HBM)


def in_hbm(x):
    return pltpu.with_memory_space_constraint(x, pltpu.HBM)


def whole(shape):
    return pl.BlockSpec(shape, lambda *_: (0,) * len(shape))


def split_three(column):
    first = column.astype(jnp.bfloat16).astype(jnp.float32)
    second = (column - first).astype(jnp.bfloat16).astype(jnp.float32)
    third = (column - first - second).astype(jnp.bfloat16).astype(jnp.float32)
    return first, second, third


def normalised(read_piece, gain, width):
    rows = jnp.concatenate([read_piece(k) for k in range(PIECES)], axis=-1).astype(jnp.float32)
    square = jnp.sum(rows * rows, axis=-1, keepdims=True) * (1.0 / width)
    return (rows * lax.rsqrt(square + epsilon) * gain.astype(jnp.float32)).astype(jnp.bfloat16)


def project_body(rows_ref, gain_ref, weight_hbm, out_ref, weight_ref, sems):
    steps, each, width = weight_ref.shape
    copies = [
        pltpu.make_async_copy(
            weight_hbm.at[pl.ds(c * each, each)], weight_ref.at[c], sems.at[c]
        )
        for c in range(steps)
    ]
    for copy in copies:
        copy.start()
    normed = normalised(lambda k: rows_ref[k], gain_ref[...], width)
    for step in range(steps):
        copies[step].wait()
        out = dot_nt(normed, weight_ref[step]).astype(jnp.bfloat16)
        for k in range(out_ref.shape[0]):
            out_ref[k, :, step * each : (step + 1) * each] = out


def project(rows, gain, weight, copies):
    pieces, requests, part = rows.shape
    columns, width = weight.shape
    steps = 3 if columns % (3 * LANES) == 0 else 1
    return call(
        project_body,
        jax.ShapeDtypeStruct((copies, requests, columns), jnp.bfloat16),
        16,
        2 * requests * columns * width,
        2 * columns * width,
        in_specs=[VMEM, VMEM, HBM],
        out_specs=VMEM,
        scratch_shapes=[
            pltpu.VMEM((steps, columns // steps, width), jnp.bfloat16),
            pltpu.SemaphoreType.DMA((steps,)),
        ],
    )(rows, gain, in_hbm(weight))


def pick_body(share, pick_ref, extra_ref, rows_ref, *out_refs):
    slots = extra_ref.shape[1]
    each = PIECES // SHARES
    for k in range(each):
        picked = dot_nn(pick_ref[...], rows_ref[share * each + k]).astype(jnp.bfloat16)
        for o, out_ref in enumerate(out_refs):
            out_ref[:, k * PAIR : (k + 1) * PAIR] = picked[o * slots : (o + 1) * slots]
    for o, out_ref in enumerate(out_refs):
        out_ref[:, each * PAIR :] = extra_ref[o]


def pick_queries(share, pick, extra, rows):
    owners, slots, _ = extra.shape
    return call(
        functools.partial(pick_body, share),
        (jax.ShapeDtypeStruct((slots, HEADS * KVW + LANES), jnp.bfloat16),) * owners,
        16,
        2 * owners * slots * rows.shape[1] * HEADS * KVW,
        4 * owners * slots * HEADS * KVW,
    )(pick, extra, rows)


def sums(scores, usable=None):
    if usable is not None:
        scores = [jnp.where(u, x, lowest) for u, x in zip(usable, scores)]
    peak = functools.reduce(
        jnp.maximum, [jnp.max(x, axis=-1, keepdims=True) for x in scores]
    )
    weights = [jnp.exp2(x - peak) for x in scores]
    if usable is not None:
        weights = [jnp.where(u, w, 0.0) for u, w in zip(usable, weights)]
    total = functools.reduce(jnp.add, [jnp.sum(w, axis=-1, keepdims=True) for w in weights])
    return peak, [w.astype(jnp.bfloat16) for w in weights], total


def own_body(share, rows_ref, holder_ref, root_hbm, suffix_hbm, out_hbm, out_ref, q_ref, root_ref, suffix_ref, s_ref, root_sems, suffix_sems, out_sem):
    requests = rows_ref.shape[1]
    blocks, _, block = root_ref.shape
    groups, span, _ = suffix_ref.shape
    each = requests // groups
    root_copies = [
        pltpu.make_async_copy(
            root_hbm.at[:, pl.ds(b * block, block)], root_ref.at[b], root_sems.at[b]
        )
        for b in range(blocks)
    ]
    suffix_copies = [
        pltpu.make_async_copy(
            suffix_hbm.at[pl.ds(g * span, span)], suffix_ref.at[g], suffix_sems.at[g]
        )
        for g in range(groups)
    ]
    for copy in root_copies + suffix_copies:
        copy.start()
    for h in range(HEADS):
        k, j = divmod(share * HEADS + h, 2)
        q_ref[h * requests : (h + 1) * requests, :] = rows_ref[k, :, j * KVW : (j + 1) * KVW]
    scale = score_scale * log2e
    peaks = []
    for b in range(blocks):
        root_copies[b].wait()
        s_ref[b] = dot_nn(q_ref[...], root_ref[b]) * scale
    root_peak, weights, root_total = sums([s_ref[b] for b in range(blocks)])
    root_out = functools.reduce(
        jnp.add, [dot_nt(weights[b], root_ref[b, :LAT, :]) for b in range(blocks)]
    )
    for g in range(groups):
        suffix_copies[g].wait()
        mine = [slice(h * requests + g * each, h * requests + (g + 1) * each) for h in range(HEADS)]
        scores = dot_nt(
            jnp.concatenate([q_ref[at, :] for at in mine], axis=0), suffix_ref[g]
        )
        request = lax.broadcasted_iota(jnp.int32, (HEADS * each, 1), 0) % each + g * each
        usable = holder_ref[:, g * span : (g + 1) * span] == request
        peak, weights, total = sums([scores * scale], [usable])
        out = dot_nn(weights[0], suffix_ref[g, :, :LAT])
        for h, at in enumerate(mine):
            own = slice(h * each, (h + 1) * each)
            top = jnp.maximum(root_peak[at], peak[own])
            root_scale = jnp.exp2(root_peak[at] - top)
            scaled = jnp.exp2(peak[own] - top)
            both = root_total[at] * root_scale + total[own] * scaled
            out_ref[at, :LAT] = (root_out[at] * root_scale + out[own] * scaled) / both
            out_ref[at, LAT:] = jnp.broadcast_to(top * ln2 + jnp.log(both), (each, LANES))
    copy = pltpu.make_async_copy(out_ref, out_hbm, out_sem)
    copy.start()
    copy.wait()


def own_attention(share, rows, holder, root, suffix):
    count = HEADS * rows.shape[1]
    positions = root.shape[1]
    block = min(1024, positions)
    blocks, groups = positions // block, 2
    span = suffix.shape[0] // groups
    return call(
        functools.partial(own_body, share),
        pltpu.HBM((count, LAT + LANES), jnp.float32),
        44,
        2 * count * (positions + span) * (KVW + LAT),
        2 * KVW * (positions + suffix.shape[0]),
        in_specs=[VMEM, VMEM, HBM, HBM],
        out_specs=HBM,
        scratch_shapes=[
            pltpu.VMEM((count, LAT + LANES), jnp.float32),
            pltpu.VMEM((count, KVW), jnp.bfloat16),
            pltpu.VMEM((blocks, KVW, block), jnp.bfloat16),
            pltpu.VMEM((groups, span, KVW), jnp.bfloat16),
            pltpu.VMEM((blocks, count, block), jnp.float32),
            pltpu.SemaphoreType.DMA((blocks,)),
            pltpu.SemaphoreType.DMA((groups,)),
            pltpu.SemaphoreType.DMA,
        ],
    )(rows, holder, in_hbm(root), in_hbm(suffix))


def group_body(owners, cache_hbm, holder_ref, *refs):
    rows_refs, out_refs = refs[:owners], refs[owners : 2 * owners]
    q_ref, keys_ref, sems = refs[2 * owners :]
    slots = rows_refs[0].shape[0]
    groups, _, span = cache_hbm.shape
    copies = [
        pltpu.make_async_copy(
            cache_hbm.at[g], keys_ref.at[:, pl.ds(g * span, span)], sems.at[g]
        )
        for g in range(groups)
    ]
    for copy in copies:
        copy.start()
    each = HEADS * slots
    for o in range(owners):
        for h in range(HEADS):
            at = o * each + h * slots
            q_ref[at : at + slots, :] = rows_refs[o][:, h * KVW : (h + 1) * KVW]
    lane = lax.broadcasted_iota(jnp.int32, (slots, LANES), 1)
    both = 2 * each
    blocks = 3 if groups % 3 == 0 else 1
    scores = [[] for _ in range(owners // 2)]
    for b in range(blocks):
        for copy in copies[b * groups // blocks : (b + 1) * groups // blocks]:
            copy.wait()
        at = slice(b * groups * span // blocks, (b + 1) * groups * span // blocks)
        for pair in range(owners // 2):
            scores[pair].append(
                dot_nn(q_ref[pair * both : (pair + 1) * both, :], keys_ref[:, at])
            )
    for pair in range(owners // 2):
        asked = [
            rows_refs[o][:, HEADS * KVW :][:, :1].astype(jnp.float32)
            for o in (2 * pair, 2 * pair + 1)
        ]
        asked = jnp.concatenate([asked[0]] * HEADS + [asked[1]] * HEADS, axis=0)
        usable = holder_ref[...] == asked
        block = jnp.concatenate(scores[pair], axis=1) * (score_scale * log2e)
        block = jnp.where(usable, block, lowest)
        peak = jnp.max(block, axis=-1, keepdims=True)
        weights = jnp.where(usable, jnp.exp2(block - peak), 0.0)
        total = jnp.sum(weights, axis=-1, keepdims=True)
        present = total > 0.0
        safe = jnp.where(present, total, 1.0)
        block_out = dot_nt(weights.astype(jnp.bfloat16), keys_ref[:LAT, :]) / safe
        mass = jnp.where(present, peak * ln2 + jnp.log(safe), lowest)
        for o in (2 * pair, 2 * pair + 1):
            out_ref = out_refs[o]
            extra = jnp.zeros((slots, LANES), jnp.float32)
            for h in range(HEADS):
                at = (o - 2 * pair) * each + h * slots
                at = slice(at, at + slots)
                out_ref[:, h * LAT : (h + 1) * LAT] = block_out[at].astype(jnp.bfloat16)
                for k, part in enumerate(split_three(mass[at])):
                    extra = jnp.where(lane == k * HEADS + h, part, extra)
            out_ref[:, HEADS * LAT :] = extra.astype(jnp.bfloat16)


def group_attention(rows, cache, holder):
    owners, slots = len(rows), rows[0].shape[0]
    groups, _, span = cache.shape
    out = jax.ShapeDtypeStruct((slots, HEADS * LAT + LANES), jnp.bfloat16)
    return call(
        functools.partial(group_body, owners),
        (out,) * owners,
        40,
        2 * owners * slots * HEADS * groups * span * (KVW + LAT),
        2 * KVW * groups * span,
        in_specs=[HBM, VMEM] + [VMEM] * owners,
        out_specs=(VMEM,) * owners,
        scratch_shapes=[
            pltpu.VMEM((owners * HEADS * slots, KVW), jnp.bfloat16),
            pltpu.VMEM((KVW, groups * span), jnp.bfloat16),
            pltpu.SemaphoreType.DMA((groups,)),
        ],
    )(in_hbm(cache), holder, *rows)


def local_body(unpick_ref, *refs):
    first_hbm, back_refs = refs[:SHARES], refs[SHARES:-4]
    out_ref, first_ref, out_mass_ref, sems = refs[-4:]
    copies = [
        pltpu.make_async_copy(first_hbm[k], first_ref.at[k], sems.at[k]) for k in range(SHARES)
    ]
    for copy in copies:
        copy.start()
    owners = len(back_refs) // SHARES
    requests = unpick_ref.shape[0]
    unpick = unpick_ref[...]

    def returned(share, at):
        rows = [ref[:, at] for ref in back_refs[share * owners : (share + 1) * owners]]
        return dot_nn(unpick, jnp.concatenate(rows, axis=0))

    extras = [returned(share, slice(HEADS * LAT, None)) for share in range(SHARES)]
    shares, length = out_ref.shape[0], out_ref.shape[1] - MASS_ROWS
    for h in range(H):
        share, head = divmod(h, HEADS)
        if head == 0:
            copies[share].wait()
        at = slice(head * requests, (head + 1) * requests)
        group_out = returned(share, slice(head * LAT, (head + 1) * LAT))
        group_mass = functools.reduce(
            jnp.add,
            [extras[share][:, k * HEADS + head : k * HEADS + head + 1] for k in range(3)],
        )
        first_mass = first_ref[share, at, LAT : LAT + 1]
        peak = jnp.maximum(first_mass, group_mass)
        first_weight = jnp.exp(first_mass - peak)
        group_weight = jnp.exp(group_mass - peak)
        total = first_weight + group_weight
        out = (first_weight * first_ref[share, at, :LAT] + group_weight * group_out) / total
        out = out.astype(jnp.bfloat16)
        each = min(length, requests)
        for k in range(requests // each):
            target, row = divmod(h * requests + k * each, length)
            out_ref[target, row : row + each, :] = out[k * each : (k + 1) * each]
        out_mass_ref[h * requests : (h + 1) * requests, :] = peak + jnp.log(total)
    diagonal = lax.broadcasted_iota(jnp.int32, (length, LAT), 0) == lax.broadcasted_iota(
        jnp.int32, (length, LAT), 1
    )
    row = lax.broadcasted_iota(jnp.int32, (MASS_ROWS, LAT), 0)
    for share in range(shares):
        masses = jnp.where(diagonal, out_mass_ref[share * length : (share + 1) * length, :], 0.0)
        masses = jnp.sum(masses, axis=0, keepdims=True)
        tail = jnp.zeros((MASS_ROWS, LAT), jnp.float32)
        for k, part in enumerate(split_three(masses)):
            tail = jnp.where(row == k, part, tail)
        out_ref[share, length:, :] = tail.astype(jnp.bfloat16)


def local_join(unpick, first, back, shares):
    count = SHARES * first[0].shape[0]
    return call(
        local_body,
        jax.ShapeDtypeStruct((shares, count // shares + MASS_ROWS, LAT), jnp.bfloat16),
        10,
        2 * unpick.shape[0] * unpick.shape[1] * H * LAT,
        4 * count * LAT,
        in_specs=[VMEM] + [HBM] * SHARES + [VMEM] * len(back),
        out_specs=VMEM,
        scratch_shapes=[
            pltpu.VMEM((SHARES,) + first[0].shape, jnp.float32),
            pltpu.VMEM((count, 1), jnp.float32),
            pltpu.SemaphoreType.DMA((SHARES,)),
        ],
    )(unpick, *[in_hbm(x) for x in first], *back)


def join_body(parts_ref, out_ref):
    sources, copies, length = parts_ref.shape[0], out_ref.shape[0], out_ref.shape[1]
    diagonal = lax.broadcasted_iota(jnp.int32, (length, LAT), 0) == lax.broadcasted_iota(
        jnp.int32, (length, LAT), 1
    )
    masses = []
    for s in range(sources):
        tail = parts_ref[s, length:, :].astype(jnp.float32)
        mass = tail[0:1] + tail[1:2] + tail[2:3]
        masses.append(jnp.sum(jnp.where(diagonal, mass, 0.0), axis=1, keepdims=True))
    peak = functools.reduce(jnp.maximum, masses)
    scales = [jnp.exp(mass - peak) for mass in masses]
    total = functools.reduce(jnp.add, scales)
    out = functools.reduce(
        jnp.add,
        [scales[s] * parts_ref[s, :length, :].astype(jnp.float32) for s in range(sources)],
    )
    out = (out / total).astype(jnp.bfloat16)
    for c in range(copies):
        out_ref[c] = out


def join(parts):
    sources, rows, _ = parts.shape
    rows -= MASS_ROWS
    return call(
        join_body,
        jax.ShapeDtypeStruct((sources, rows, LAT), jnp.bfloat16),
        6,
        3e10,
        4 * sources * rows * LAT,
    )(parts)


def output_body(rows_ref, weight_ref, hidden_ref, out_ref, copies_ref):
    requests = hidden_ref.shape[0]
    total = hidden_ref[...].astype(jnp.float32)
    for h in range(H):
        total = total + dot_nt(
            rows_ref[h * requests : (h + 1) * requests, :],
            weight_ref[:, h * LAT : (h + 1) * LAT],
        )
    out = total.astype(jnp.bfloat16)
    out_ref[...] = out
    for c in range(copies_ref.shape[0]):
        copies_ref[c] = out


def output_projection(rows, weight, hidden, copies):
    features, width = weight.shape
    requests = hidden.shape[0]
    return call(
        output_body,
        (
            jax.ShapeDtypeStruct(hidden.shape, jnp.bfloat16),
            jax.ShapeDtypeStruct((copies,) + hidden.shape, jnp.bfloat16),
        ),
        8,
        2 * requests * features * width,
        2 * features * width,
        in_specs=[VMEM] * 3,
        out_specs=(VMEM, VMEM),
    )(rows, weight, hidden)


def gated(rows, gate, up):
    gate_part = dot_nt(rows, gate)
    up_part = dot_nt(rows, up)
    return (gate_part / (1.0 + jnp.exp(-gate_part)) * up_part).astype(jnp.bfloat16)


def expert_body(pick_ref, rows_ref, gain_ref, shared_gate_ref, shared_up_ref, shared_down_ref, gate_ref, up_ref, down_ref, out_ref):
    owners, _, requests, part = rows_ref.shape
    width = gain_ref.shape[1]
    share = requests // owners
    slots = out_ref.shape[2] - share
    rows = jnp.concatenate(
        [
            normalised(lambda k, o=o: rows_ref[o, k], gain_ref[...], width)
            for o in range(owners)
        ],
        axis=0,
    )
    rows = dot_nn(pick_ref[...], rows).astype(jnp.bfloat16)
    named, rest = rows[: owners * slots], rows[owners * slots :]
    shared = dot_nn(gated(rest, shared_gate_ref[...], shared_up_ref[...]), shared_down_ref[...])
    units = gate_ref.shape[1]
    steps = 4 if units % 64 == 0 and units > 704 else 1
    each = units // steps
    total = jnp.zeros((owners * slots, width), jnp.float32)
    for c in range(steps):
        at = slice(c * each, (c + 1) * each)
        total = total + dot_nn(
            gated(named, gate_ref[0, at, :], up_ref[0, at, :]), down_ref[0, at, :]
        )
    for o in range(owners):
        both = jnp.concatenate(
            [total[o * slots : (o + 1) * slots], shared[o * share : (o + 1) * share]], axis=0
        ).astype(jnp.bfloat16)
        for k in range(PIECES):
            out_ref[o, k] = both[:, k * part : (k + 1) * part]


def expert(pick, rows, gain, slots, shared, weights):
    owners, _, requests, part = rows.shape
    _, units, width = weights[0].shape
    return call(
        expert_body,
        jax.ShapeDtypeStruct(
            (owners, PIECES, slots + requests // owners, part), jnp.bfloat16
        ),
        12,
        6 * pick.shape[0] * units * width,
        6 * units * width,
        in_specs=[VMEM] * 9,
        out_specs=VMEM,
    )(pick, rows, gain, *shared, *weights)


def final_body(parts_ref, weight_ref, mid_ref, out_ref):
    weight = weight_ref[...]
    high = weight.astype(jnp.bfloat16)
    rest = weight - high.astype(jnp.float32)
    low = rest.astype(jnp.bfloat16)
    lower = (rest - low.astype(jnp.float32)).astype(jnp.bfloat16)
    parts = parts_ref[...]
    total = dot_nn(high, parts) + (dot_nn(low, parts) + dot_nn(lower, parts))
    out_ref[...] = (mid_ref[...].astype(jnp.float32) + total).astype(jnp.bfloat16)


def final_sum(parts, weight, mid):
    return call(
        final_body,
        jax.ShapeDtypeStruct(mid.shape, jnp.bfloat16),
        16,
        2 * weight.shape[0] * parts.shape[0] * parts.shape[1],
        2 * parts.shape[0] * parts.shape[1],
    )(parts, weight, mid)


def exchange(x, axis):
    return lax.all_to_all(x, axis, 0, 0, tiled=True)


def swap_owners(arrays):
    count = len(arrays)
    out = {0: arrays[0]}
    for k in reversed(range(1, count)):
        out[k] = lax.ppermute(arrays[k], OWNER, [(i, i ^ k) for i in range(count)])
    return [out[k] for k in range(count)]


def gather_pieces(x):
    devices = x.shape[-3]
    each = devices // PIECES
    if each == 1:
        return x
    lead, (rows, columns) = x.shape[:-3], x.shape[-2:]
    x = x.reshape(lead + (PIECES, each, rows, columns))
    return jnp.swapaxes(x, -3, -2).reshape(lead + (PIECES, rows, each * columns))


def scatter_pieces(x, devices):
    each = devices // PIECES
    if each == 1:
        return x
    lead, (rows, columns) = x.shape[:-3], x.shape[-2:]
    x = x.reshape(lead + (PIECES, rows, each, columns // each))
    return jnp.swapaxes(x, -3, -2).reshape(lead + (devices, rows, columns // each))


def ranks(hits):
    count = hits.shape[0]
    ahead = jnp.arange(count)[:, None] > jnp.arange(count)[None, :]
    return jnp.sum(jnp.where(ahead[:, :, None], hits.astype(jnp.int32)[None], 0), axis=1)


def local(
    hidden,
    attention_gain,
    query_weight,
    out_weight,
    root_cache,
    group_cache,
    group_length,
    suffix_cache,
    suffix_length,
    group_of,
    mixture_gain,
    routes,
    route_weight,
    expert_gate,
    expert_up,
    expert_down,
    shared_gate,
    shared_up,
    shared_down,
):
    owners, tensors = lax.axis_size(OWNER), lax.axis_size("tensor")
    owner_index, tensor_index = lax.axis_index(OWNER), lax.axis_index("tensor")
    requests = hidden.shape[0]
    fanout = routes.shape[1]
    token_share = requests // owners
    pairs = owners // 2
    split = tensors // EXP_OWN
    slots = -(-2 * requests // (owners * 16)) * 16
    expert_slots = -(-2 * requests * fanout // (EXP_OWN * owners * 16)) * 16

    if group_cache.shape[1] % LANES:
        group_columns = group_cache.reshape(-1, KVW).T[None]
    else:
        group_columns = jnp.swapaxes(group_cache, 1, 2)
    rows = exchange(jnp.broadcast_to(hidden[None], (tensors,) + hidden.shape), "tensor")

    projected = project(
        gather_pieces(rows), attention_gain[None], query_weight, tensors
    )
    projected, group_of, group_length, suffix_length, routes, route_weight = (
        lax.optimization_barrier(
            (projected, group_of, group_length, suffix_length, routes, route_weight)
        )
    )
    destination = group_of // GROUP_OWN
    owner_range = jnp.arange(owners)
    to_owner = (destination ^ owner_index)[:, None] == owner_range[None, :]
    slot_rank = ranks(to_owner)
    placed = to_owner[:, :, None] & (slot_rank[:, :, None] == jnp.arange(slots))
    unpick = placed.reshape(requests, owners * slots).astype(jnp.bfloat16)
    pick = unpick.T
    asked = jnp.sum(
        jnp.where(placed, (group_of % GROUP_OWN + 1)[:, None, None], 0), axis=0
    ).astype(jnp.bfloat16)
    named = routes.astype(jnp.bfloat16).reshape(slots, requests * fanout // slots)
    extra = jnp.where(
        jnp.arange(LANES) == 0,
        asked[:, :, None],
        jnp.pad(named, ((0, 0), (1, LANES - 1 - named.shape[1])))[None],
    )
    suffix_span, group_span = suffix_cache.shape[1], group_cache.shape[1]
    suffix_usable = (
        tensor_index * suffix_span + jnp.arange(suffix_span)[None, :] < suffix_length[:, None]
    )
    suffix_holder = jnp.where(suffix_usable, jnp.arange(requests)[:, None], -1).reshape(1, -1)
    group_usable = (
        tensor_index * group_span + jnp.arange(group_span)[None, :] < group_length[:, None]
    )
    group_holder = (
        jnp.where(group_usable, jnp.arange(1, GROUP_OWN + 1)[:, None], -1)
        .reshape(1, -1)
        .astype(jnp.float32)
    )
    queries = gather_pieces(exchange(projected, "tensor"))
    arrived, asking = [], queries
    for share in range(SHARES):
        sent = pick_queries(share, pick, extra, asking)
        asking, sent = lax.optimization_barrier((queries, sent))
        arrived.append(swap_owners(sent))
    all_routes = jnp.stack(
        [x[:, HEADS * KVW + 1 : HEADS * KVW + 1 + named.shape[1]] for x in arrived[0]]
    ).reshape(1, owners, requests, fanout)
    turned = owner_range[:, None] ^ owner_index == owner_range[None, :]
    all_routes = jnp.sum(
        jnp.where(turned[:, :, None, None], all_routes.astype(jnp.int32), 0), axis=1
    )
    mine = owner_index * EXP_OWN + tensor_index // split
    called = jnp.any(all_routes == mine, axis=2)
    call_rank = ranks(called.T).T
    expert_pick = called[:, None, :] & (
        call_rank[:, None, :] == jnp.arange(expert_slots)[None, :, None]
    )
    seen = owner_range.reshape(2, pairs)
    seen = 2 * (seen % pairs) + seen // pairs
    expert_pick = jnp.where(
        (owner_range[:, None] == seen.reshape(-1)[None, :])[:, None, :, None],
        expert_pick[:, :, None, :],
        False,
    )
    shared_pick = (
        owner_range[:, None, None] * requests
        + owner_index * token_share
        + jnp.arange(token_share)[None, :, None]
    ).reshape(-1, 1) == (seen.reshape(-1, 1) * requests + jnp.arange(requests)).reshape(1, -1)
    expert_pick = jnp.concatenate(
        [expert_pick.reshape(owners * expert_slots, owners * requests), shared_pick], axis=0
    ).astype(jnp.bfloat16)
    root_columns, suffix_rows = root_cache.T, suffix_cache.reshape(-1, KVW)
    first, back, own = [], [], queries
    for share in range(SHARES):
        first.append(own_attention(share, own, suffix_holder, root_columns, suffix_rows))
        if share == 0:
            before = first[0]
            for k in range(SHARES):
                waited, before = lax.optimization_barrier((arrived[k], before))
                answered = group_attention(waited, group_columns, group_holder)
                before = answered[0]
                back.append(swap_owners(answered))
            own, before, expert_pick = lax.optimization_barrier((own, before, expert_pick))
    back, gain = lax.optimization_barrier((back, mixture_gain[None]))
    parts = local_join(unpick, first, sum(back, []), tensors)
    attention = exchange(join(exchange(parts, "tensor")), "tensor")
    mid, copies = output_projection(
        attention.reshape(-1, LAT), out_weight, hidden, owners // 2 * tensors
    )

    half = exchange(copies, ("pair", "tensor"))
    both = lax.all_gather(half.reshape((pairs, tensors) + mid.shape), "core")
    everything = gather_pieces(both.reshape((owners, tensors) + mid.shape))
    results = expert(
        expert_pick,
        everything,
        gain,
        expert_slots,
        (shared_gate, shared_up, shared_down),
        (expert_gate, expert_up, expert_down),
    )
    results, routes, route_weight = lax.optimization_barrier((results, routes, route_weight))
    results = scatter_pieces(results, tensors).reshape((owners * tensors, -1, mid.shape[1]))
    returned = exchange(results, ("pair", "core", "tensor"))
    experts = jnp.arange(owners * EXP_OWN)
    hits = routes[:, :, None] == experts[None, None, :]
    share = jnp.sum(jnp.where(hits, route_weight[:, :, None], 0.0), axis=1)
    hit = jnp.any(hits, axis=1)
    taken = hit[:, :, None] & (ranks(hit)[:, :, None] == jnp.arange(expert_slots))
    back_weight = jnp.where(taken, share[:, :, None], 0.0)
    back_weight = jnp.repeat(back_weight, split, axis=1)
    shared_weight = np.eye(requests, dtype=np.float32).reshape(requests, owners, 1, token_share)
    shared_weight = np.repeat(shared_weight, tensors, axis=2).reshape(
        requests, owners * tensors, token_share
    )
    back_weight = jnp.concatenate([back_weight, shared_weight], axis=2).reshape(requests, -1)
    return final_sum(returned.reshape(-1, mid.shape[1]), back_weight, mid)


def solution(mesh):
    owners, tensors = mesh.shape["owner"], mesh.shape["tensor"]
    devices = mesh.devices.reshape(owners // 2, 2, tensors)
    return jax.shard_map(
        local,
        mesh=Mesh(devices, OWNER + ("tensor",)),
        in_specs=(
            P(OWNER, "tensor"),
            P(),
            P("tensor", None),
            P("tensor", None),
            P("tensor", None),
            P(OWNER, "tensor", None),
            P(OWNER),
            P(OWNER, "tensor", None),
            P(OWNER),
            P(OWNER),
            P(),
            P(OWNER, None),
            P(OWNER, None),
            P(OWNER + ("tensor",), None, None),
            P(OWNER + ("tensor",), None, None),
            P(OWNER + ("tensor",), None, None),
            P("tensor", None),
            P("tensor", None),
            P("tensor", None),
        ),
        out_specs=P(OWNER, "tensor"),
        check_vma=False,
    )
```

```python
import functools

import jax
import jax.numpy as jnp
import numpy as np
from jax import lax
from jax.experimental import pallas as pl
from jax.experimental.pallas import tpu as pltpu
from jax.sharding import Mesh
from jax.sharding import PartitionSpec as P

H = 16
LAT = 512
KVW = 576
EXP_OWN = 8
GROUP_OWN = 12
PIECES = 8
PAIR = 2 * KVW
LANES = 128
OWNER = ("pair", "core")
SHARES = 2
HEADS = H // SHARES
MASS_ROWS = 8
MIB = 1 << 20

score_scale = 192.0 ** (-0.5)
log2e = 1.4426950408889634
ln2 = 0.6931471805599453
lowest = -1e30
epsilon = 1e-06

NT = (((1,), (1,)), ((), ()))


def dot_nt(a, b):
    return lax.dot_general(a, b, NT, preferred_element_type=jnp.float32)


def dot_nn(a, b):
    return jnp.dot(a, b, preferred_element_type=jnp.float32)


def call(body, out_shape, vmem_mib, flops, nbytes, **options):
    return pl.pallas_call(
        body,
        out_shape=out_shape,
        compiler_params=pltpu.CompilerParams(vmem_limit_bytes=vmem_mib * MIB),
        cost_estimate=pl.CostEstimate(
            flops=int(flops), bytes_accessed=int(nbytes), transcendentals=0
        ),
        **options,
    )


VMEM = pl.BlockSpec(memory_space=pltpu.VMEM)
HBM = pl.BlockSpec(memory_space=pltpu.HBM)


def in_hbm(x):
    return pltpu.with_memory_space_constraint(x, pltpu.HBM)


def whole(shape):
    return pl.BlockSpec(shape, lambda *_: (0,) * len(shape))


def split_three(column):
    first = column.astype(jnp.bfloat16).astype(jnp.float32)
    second = (column - first).astype(jnp.bfloat16).astype(jnp.float32)
    third = (column - first - second).astype(jnp.bfloat16).astype(jnp.float32)
    return first, second, third


def normalised(read_piece, gain, width):
    rows = jnp.concatenate([read_piece(k) for k in range(PIECES)], axis=-1).astype(jnp.float32)
    square = jnp.sum(rows * rows, axis=-1, keepdims=True) * (1.0 / width)
    return (rows * lax.rsqrt(square + epsilon) * gain.astype(jnp.float32)).astype(jnp.bfloat16)


def project_body(rows_ref, gain_ref, weight_hbm, out_ref, weight_ref, sems):
    steps, each, width = weight_ref.shape
    copies = [
        pltpu.make_async_copy(
            weight_hbm.at[pl.ds(c * each, each)], weight_ref.at[c], sems.at[c]
        )
        for c in range(steps)
    ]
    for copy in copies:
        copy.start()
    normed = normalised(lambda k: rows_ref[k], gain_ref[...], width)
    for step in range(steps):
        copies[step].wait()
        out = dot_nt(normed, weight_ref[step]).astype(jnp.bfloat16)
        out_ref[:, step * each : (step + 1) * each] = out


def project(rows, gain, weight):
    pieces, requests, part = rows.shape
    columns, width = weight.shape
    steps = 3 if columns % (3 * LANES) == 0 else 1
    return call(
        project_body,
        jax.ShapeDtypeStruct((requests, columns), jnp.bfloat16),
        16,
        2 * requests * columns * width,
        2 * columns * width,
        in_specs=[VMEM, VMEM, HBM],
        out_specs=VMEM,
        scratch_shapes=[
            pltpu.VMEM((steps, columns // steps, width), jnp.bfloat16),
            pltpu.SemaphoreType.DMA((steps,)),
        ],
    )(rows, gain, in_hbm(weight))


def pick_body(pick_ref, extra_ref, *refs):
    slots = extra_ref.shape[1]
    each = PIECES // SHARES
    rows_refs, out_refs = refs[:each], refs[each:]
    for k in range(each):
        picked = dot_nn(pick_ref[...], rows_refs[k][...]).astype(jnp.bfloat16)
        for o, out_ref in enumerate(out_refs):
            out_ref[:, k * PAIR : (k + 1) * PAIR] = picked[o * slots : (o + 1) * slots]
    for o, out_ref in enumerate(out_refs):
        out_ref[:, each * PAIR :] = extra_ref[o]


def pick_queries(pick, extra, rows):
    owners, slots, _ = extra.shape
    return call(
        pick_body,
        (jax.ShapeDtypeStruct((slots, HEADS * KVW + LANES), jnp.bfloat16),) * owners,
        16,
        2 * owners * slots * pick.shape[1] * HEADS * KVW,
        4 * owners * slots * HEADS * KVW,
    )(pick, extra, *rows)


def sums(scores, usable=None):
    if usable is not None:
        scores = [jnp.where(u, x, lowest) for u, x in zip(usable, scores)]
    peak = functools.reduce(
        jnp.maximum, [jnp.max(x, axis=-1, keepdims=True) for x in scores]
    )
    weights = [jnp.exp2(x - peak) for x in scores]
    if usable is not None:
        weights = [jnp.where(u, w, 0.0) for u, w in zip(usable, weights)]
    total = functools.reduce(jnp.add, [jnp.sum(w, axis=-1, keepdims=True) for w in weights])
    return peak, [w.astype(jnp.bfloat16) for w in weights], total


def own_body(holder_ref, root_hbm, suffix_hbm, *refs):
    rows_refs, out_hbm = refs[: HEADS // 2], refs[HEADS // 2]
    out_ref, q_ref, root_ref, suffix_ref, s_ref, root_sems, suffix_sems, out_sem = refs[
        HEADS // 2 + 1 :
    ]
    requests = rows_refs[0].shape[0]
    blocks, _, block = root_ref.shape
    groups, span, _ = suffix_ref.shape
    each = requests // groups
    root_copies = [
        pltpu.make_async_copy(
            root_hbm.at[:, pl.ds(b * block, block)], root_ref.at[b], root_sems.at[b]
        )
        for b in range(blocks)
    ]
    suffix_copies = [
        pltpu.make_async_copy(
            suffix_hbm.at[pl.ds(g * span, span)], suffix_ref.at[g], suffix_sems.at[g]
        )
        for g in range(groups)
    ]
    for copy in root_copies + suffix_copies:
        copy.start()
    for h in range(HEADS):
        k, j = divmod(h, 2)
        q_ref[h * requests : (h + 1) * requests, :] = rows_refs[k][:, j * KVW : (j + 1) * KVW]
    scale = score_scale * log2e
    for b in range(blocks):
        root_copies[b].wait()
        s_ref[b] = dot_nn(q_ref[...], root_ref[b]) * scale
    root_peak, weights, root_total = sums([s_ref[b] for b in range(blocks)])
    root_out = functools.reduce(
        jnp.add, [dot_nt(weights[b], root_ref[b, :LAT, :]) for b in range(blocks)]
    )
    for g in range(groups):
        suffix_copies[g].wait()
        mine = [slice(h * requests + g * each, h * requests + (g + 1) * each) for h in range(HEADS)]
        scores = dot_nt(
            jnp.concatenate([q_ref[at, :] for at in mine], axis=0), suffix_ref[g]
        )
        request = lax.broadcasted_iota(jnp.int32, (HEADS * each, 1), 0) % each + g * each
        usable = holder_ref[:, g * span : (g + 1) * span] == request
        peak, weights, total = sums([scores * scale], [usable])
        out = dot_nn(weights[0], suffix_ref[g, :, :LAT])
        for h, at in enumerate(mine):
            own = slice(h * each, (h + 1) * each)
            top = jnp.maximum(root_peak[at], peak[own])
            root_scale = jnp.exp2(root_peak[at] - top)
            scaled = jnp.exp2(peak[own] - top)
            both = root_total[at] * root_scale + total[own] * scaled
            out_ref[at, :LAT] = (root_out[at] * root_scale + out[own] * scaled) / both
            out_ref[at, LAT:] = jnp.broadcast_to(top * ln2 + jnp.log(both), (each, LANES))
    copy = pltpu.make_async_copy(out_ref, out_hbm, out_sem)
    copy.start()
    copy.wait()


def own_attention(rows, holder, root, suffix):
    count = HEADS * rows[0].shape[0]
    positions = root.shape[1]
    block = min(1024, positions)
    blocks, groups = positions // block, 2
    span = suffix.shape[0] // groups
    return call(
        own_body,
        pltpu.HBM((count, LAT + LANES), jnp.float32),
        44,
        2 * count * (positions + span) * (KVW + LAT),
        2 * KVW * (positions + suffix.shape[0]),
        in_specs=[VMEM, HBM, HBM] + [VMEM] * len(rows),
        out_specs=HBM,
        scratch_shapes=[
            pltpu.VMEM((count, LAT + LANES), jnp.float32),
            pltpu.VMEM((count, KVW), jnp.bfloat16),
            pltpu.VMEM((blocks, KVW, block), jnp.bfloat16),
            pltpu.VMEM((groups, span, KVW), jnp.bfloat16),
            pltpu.VMEM((blocks, count, block), jnp.float32),
            pltpu.SemaphoreType.DMA((blocks,)),
            pltpu.SemaphoreType.DMA((groups,)),
            pltpu.SemaphoreType.DMA,
        ],
    )(holder, in_hbm(root), in_hbm(suffix), *rows)


def group_body(owners, cache_hbm, holder_ref, *refs):
    rows_refs, out_refs = refs[:owners], refs[owners : 2 * owners]
    q_ref, keys_ref, sems = refs[2 * owners :]
    slots = rows_refs[0].shape[0]
    groups, _, span = cache_hbm.shape
    copies = [
        pltpu.make_async_copy(
            cache_hbm.at[g], keys_ref.at[:, pl.ds(g * span, span)], sems.at[g]
        )
        for g in range(groups)
    ]
    for copy in copies:
        copy.start()
    each = HEADS * slots
    for o in range(owners):
        for h in range(HEADS):
            at = o * each + h * slots
            q_ref[at : at + slots, :] = rows_refs[o][:, h * KVW : (h + 1) * KVW]
    lane = lax.broadcasted_iota(jnp.int32, (slots, LANES), 1)
    both = 2 * each
    blocks = 3 if groups % 3 == 0 else 1
    scores = [[] for _ in range(owners // 2)]
    for b in range(blocks):
        for copy in copies[b * groups // blocks : (b + 1) * groups // blocks]:
            copy.wait()
        at = slice(b * groups * span // blocks, (b + 1) * groups * span // blocks)
        for pair in range(owners // 2):
            scores[pair].append(
                dot_nn(q_ref[pair * both : (pair + 1) * both, :], keys_ref[:, at])
            )
    for pair in range(owners // 2):
        asked = [
            rows_refs[o][:, HEADS * KVW :][:, :1].astype(jnp.float32)
            for o in (2 * pair, 2 * pair + 1)
        ]
        asked = jnp.concatenate([asked[0]] * HEADS + [asked[1]] * HEADS, axis=0)
        usable = holder_ref[...] == asked
        block = jnp.concatenate(scores[pair], axis=1) * (score_scale * log2e)
        block = jnp.where(usable, block, lowest)
        peak = jnp.max(block, axis=-1, keepdims=True)
        weights = jnp.where(usable, jnp.exp2(block - peak), 0.0)
        total = jnp.sum(weights, axis=-1, keepdims=True)
        present = total > 0.0
        safe = jnp.where(present, total, 1.0)
        block_out = dot_nt(weights.astype(jnp.bfloat16), keys_ref[:LAT, :]) / safe
        mass = jnp.where(present, peak * ln2 + jnp.log(safe), lowest)
        for o in (2 * pair, 2 * pair + 1):
            out_ref = out_refs[o]
            extra = jnp.zeros((slots, LANES), jnp.float32)
            for h in range(HEADS):
                at = (o - 2 * pair) * each + h * slots
                at = slice(at, at + slots)
                out_ref[:, h * LAT : (h + 1) * LAT] = block_out[at].astype(jnp.bfloat16)
                for k, part in enumerate(split_three(mass[at])):
                    extra = jnp.where(lane == k * HEADS + h, part, extra)
            out_ref[:, HEADS * LAT :] = extra.astype(jnp.bfloat16)


def group_attention(rows, cache, holder):
    owners, slots = len(rows), rows[0].shape[0]
    groups, _, span = cache.shape
    out = jax.ShapeDtypeStruct((slots, HEADS * LAT + LANES), jnp.bfloat16)
    return call(
        functools.partial(group_body, owners),
        (out,) * owners,
        40,
        2 * owners * slots * HEADS * groups * span * (KVW + LAT),
        2 * KVW * groups * span,
        in_specs=[HBM, VMEM] + [VMEM] * owners,
        out_specs=(VMEM,) * owners,
        scratch_shapes=[
            pltpu.VMEM((owners * HEADS * slots, KVW), jnp.bfloat16),
            pltpu.VMEM((KVW, groups * span), jnp.bfloat16),
            pltpu.SemaphoreType.DMA((groups,)),
        ],
    )(in_hbm(cache), holder, *rows)


def local_body(base_ref, unpick_ref, *refs):
    first_hbm, back_refs = refs[:SHARES], refs[SHARES:-4]
    out_ref, first_ref, out_mass_ref, sems = refs[-4:]
    copies = [
        pltpu.make_async_copy(first_hbm[k], first_ref.at[k], sems.at[k]) for k in range(SHARES)
    ]
    for copy in copies:
        copy.start()
    owners = len(back_refs) // SHARES
    requests = unpick_ref.shape[0]
    unpick = unpick_ref[...]

    def returned(share, at):
        rows = [ref[:, at] for ref in back_refs[share * owners : (share + 1) * owners]]
        return dot_nn(unpick, jnp.concatenate(rows, axis=0))

    extras = [returned(share, slice(HEADS * LAT, None)) for share in range(SHARES)]
    shares, length = out_ref.shape[0], out_ref.shape[1] - MASS_ROWS
    per_piece = shares // PIECES
    for h in range(H):
        share, head = divmod(h, HEADS)
        if head == 0:
            copies[share].wait()
        at = slice(head * requests, (head + 1) * requests)
        group_out = returned(share, slice(head * LAT, (head + 1) * LAT))
        group_mass = functools.reduce(
            jnp.add,
            [extras[share][:, k * HEADS + head : k * HEADS + head + 1] for k in range(3)],
        )
        first_mass = first_ref[share, at, LAT : LAT + 1]
        peak = jnp.maximum(first_mass, group_mass)
        first_weight = jnp.exp(first_mass - peak)
        group_weight = jnp.exp(group_mass - peak)
        total = first_weight + group_weight
        out = (first_weight * first_ref[share, at, :LAT] + group_weight * group_out) / total
        out = out.astype(jnp.bfloat16)
        each = min(length, requests)
        for k in range(requests // each):
            sub, row = divmod(h % 2 * requests + k * each, length)
            target = (h // 2 ^ base_ref[0]) * per_piece + sub
            out_ref[target, row : row + each, :] = out[k * each : (k + 1) * each]
        out_mass_ref[h * requests : (h + 1) * requests, :] = peak + jnp.log(total)
    diagonal = lax.broadcasted_iota(jnp.int32, (length, LAT), 0) == lax.broadcasted_iota(
        jnp.int32, (length, LAT), 1
    )
    row = lax.broadcasted_iota(jnp.int32, (MASS_ROWS, LAT), 0)
    for share in range(shares):
        masses = jnp.where(diagonal, out_mass_ref[share * length : (share + 1) * length, :], 0.0)
        masses = jnp.sum(masses, axis=0, keepdims=True)
        tail = jnp.zeros((MASS_ROWS, LAT), jnp.float32)
        for k, part in enumerate(split_three(masses)):
            tail = jnp.where(row == k, part, tail)
        piece, sub = divmod(share, per_piece)
        target = (piece ^ base_ref[0]) * per_piece + sub
        out_ref[target, length:, :] = tail.astype(jnp.bfloat16)


def local_join(base, unpick, first, back, shares):
    count = SHARES * first[0].shape[0]
    return call(
        local_body,
        jax.ShapeDtypeStruct((shares, count // shares + MASS_ROWS, LAT), jnp.bfloat16),
        10,
        2 * unpick.shape[0] * unpick.shape[1] * H * LAT,
        4 * count * LAT,
        in_specs=[pl.BlockSpec(memory_space=pltpu.SMEM), VMEM]
        + [HBM] * SHARES
        + [VMEM] * len(back),
        out_specs=VMEM,
        scratch_shapes=[
            pltpu.VMEM((SHARES,) + first[0].shape, jnp.float32),
            pltpu.VMEM((count, 1), jnp.float32),
            pltpu.SemaphoreType.DMA((SHARES,)),
        ],
    )(base, unpick, *[in_hbm(x) for x in first], *back)


def join_body(parts_ref, out_ref):
    sources, copies, length = parts_ref.shape[0], out_ref.shape[0], out_ref.shape[1]
    diagonal = lax.broadcasted_iota(jnp.int32, (length, LAT), 0) == lax.broadcasted_iota(
        jnp.int32, (length, LAT), 1
    )
    masses = []
    for s in range(sources):
        tail = parts_ref[s, length:, :].astype(jnp.float32)
        mass = tail[0:1] + tail[1:2] + tail[2:3]
        masses.append(jnp.sum(jnp.where(diagonal, mass, 0.0), axis=1, keepdims=True))
    peak = functools.reduce(jnp.maximum, masses)
    scales = [jnp.exp(mass - peak) for mass in masses]
    total = functools.reduce(jnp.add, scales)
    out = functools.reduce(
        jnp.add,
        [scales[s] * parts_ref[s, :length, :].astype(jnp.float32) for s in range(sources)],
    )
    out = (out / total).astype(jnp.bfloat16)
    for c in range(copies):
        out_ref[c] = out


def join(parts):
    sources, rows, _ = parts.shape
    rows -= MASS_ROWS
    return call(
        join_body,
        jax.ShapeDtypeStruct((sources, rows, LAT), jnp.bfloat16),
        6,
        3e10,
        4 * sources * rows * LAT,
    )(parts)


def output_body(rows_ref, weight_ref, hidden_ref, out_ref, copies_ref):
    requests = hidden_ref.shape[0]
    total = hidden_ref[...].astype(jnp.float32)
    for h in range(H):
        total = total + dot_nt(
            rows_ref[h * requests : (h + 1) * requests, :],
            weight_ref[:, h * LAT : (h + 1) * LAT],
        )
    out = total.astype(jnp.bfloat16)
    out_ref[...] = out
    for c in range(copies_ref.shape[0]):
        copies_ref[c] = out


def output_projection(rows, weight, hidden, copies):
    features, width = weight.shape
    requests = hidden.shape[0]
    return call(
        output_body,
        (
            jax.ShapeDtypeStruct(hidden.shape, jnp.bfloat16),
            jax.ShapeDtypeStruct((copies,) + hidden.shape, jnp.bfloat16),
        ),
        8,
        2 * requests * features * width,
        2 * features * width,
        in_specs=[VMEM] * 3,
        out_specs=(VMEM, VMEM),
    )(rows, weight, hidden)


def gated(rows, gate, up):
    gate_part = dot_nt(rows, gate)
    up_part = dot_nt(rows, up)
    return (gate_part / (1.0 + jnp.exp(-gate_part)) * up_part).astype(jnp.bfloat16)


def expert_body(pick_ref, rows_ref, gain_ref, shared_gate_ref, shared_up_ref, shared_down_ref, gate_ref, up_ref, down_ref, out_ref):
    owners, _, requests, part = rows_ref.shape
    width = gain_ref.shape[1]
    share = requests // owners
    slots = out_ref.shape[2] - share
    rows = jnp.concatenate(
        [
            normalised(lambda k, o=o: rows_ref[o, k], gain_ref[...], width)
            for o in range(owners)
        ],
        axis=0,
    )
    rows = dot_nn(pick_ref[...], rows).astype(jnp.bfloat16)
    named, rest = rows[: owners * slots], rows[owners * slots :]
    shared = dot_nn(gated(rest, shared_gate_ref[...], shared_up_ref[...]), shared_down_ref[...])
    units = gate_ref.shape[1]
    steps = 4 if units % 64 == 0 and units > 704 else 1
    each = units // steps
    total = jnp.zeros((owners * slots, width), jnp.float32)
    for c in range(steps):
        at = slice(c * each, (c + 1) * each)
        total = total + dot_nn(
            gated(named, gate_ref[0, at, :], up_ref[0, at, :]), down_ref[0, at, :]
        )
    for o in range(owners):
        both = jnp.concatenate(
            [total[o * slots : (o + 1) * slots], shared[o * share : (o + 1) * share]], axis=0
        ).astype(jnp.bfloat16)
        for k in range(PIECES):
            out_ref[o, k] = both[:, k * part : (k + 1) * part]


def expert(pick, rows, gain, slots, shared, weights):
    owners, _, requests, part = rows.shape
    _, units, width = weights[0].shape
    return call(
        expert_body,
        jax.ShapeDtypeStruct(
            (owners, PIECES, slots + requests // owners, part), jnp.bfloat16
        ),
        12,
        6 * pick.shape[0] * units * width,
        6 * units * width,
        in_specs=[VMEM] * 9,
        out_specs=VMEM,
    )(pick, rows, gain, *shared, *weights)


def final_body(parts_ref, weight_ref, mid_ref, out_ref):
    weight = weight_ref[...]
    high = weight.astype(jnp.bfloat16)
    rest = weight - high.astype(jnp.float32)
    low = rest.astype(jnp.bfloat16)
    lower = (rest - low.astype(jnp.float32)).astype(jnp.bfloat16)
    parts = parts_ref[...]
    total = dot_nn(high, parts) + (dot_nn(low, parts) + dot_nn(lower, parts))
    out_ref[...] = (mid_ref[...].astype(jnp.float32) + total).astype(jnp.bfloat16)


def final_sum(parts, weight, mid):
    return call(
        final_body,
        jax.ShapeDtypeStruct(mid.shape, jnp.bfloat16),
        16,
        2 * weight.shape[0] * parts.shape[0] * parts.shape[1],
        2 * parts.shape[0] * parts.shape[1],
    )(parts, weight, mid)


def exchange(x, axis):
    return lax.all_to_all(x, axis, 0, 0, tiled=True)


def turn(x, k):
    count = lax.axis_size("tensor")
    return lax.ppermute(x, "tensor", [(i, i ^ k) for i in range(count)])


def swap_owners(arrays):
    count = len(arrays)
    out = {0: arrays[0]}
    for k in reversed(range(1, count)):
        out[k] = lax.ppermute(arrays[k], OWNER, [(i, i ^ k) for i in range(count)])
    return [out[k] for k in range(count)]


def gather_pieces(x):
    devices = x.shape[-3]
    each = devices // PIECES
    if each == 1:
        return x
    lead, (rows, columns) = x.shape[:-3], x.shape[-2:]
    x = x.reshape(lead + (PIECES, each, rows, columns))
    return jnp.swapaxes(x, -3, -2).reshape(lead + (PIECES, rows, each * columns))


def scatter_pieces(x, devices):
    each = devices // PIECES
    if each == 1:
        return x
    lead, (rows, columns) = x.shape[:-3], x.shape[-2:]
    x = x.reshape(lead + (PIECES, rows, each, columns // each))
    return jnp.swapaxes(x, -3, -2).reshape(lead + (devices, rows, columns // each))


def ranks(hits):
    count = hits.shape[0]
    ahead = jnp.arange(count)[:, None] > jnp.arange(count)[None, :]
    return jnp.sum(jnp.where(ahead[:, :, None], hits.astype(jnp.int32)[None], 0), axis=1)


def local(
    hidden,
    attention_gain,
    query_weight,
    out_weight,
    root_cache,
    group_cache,
    group_length,
    suffix_cache,
    suffix_length,
    group_of,
    mixture_gain,
    routes,
    route_weight,
    expert_gate,
    expert_up,
    expert_down,
    shared_gate,
    shared_up,
    shared_down,
):
    owners, tensors = lax.axis_size(OWNER), lax.axis_size("tensor")
    owner_index, tensor_index = lax.axis_index(OWNER), lax.axis_index("tensor")
    requests = hidden.shape[0]
    fanout = routes.shape[1]
    token_share = requests // owners
    pairs = owners // 2
    split = tensors // EXP_OWN
    slots = -(-2 * requests // (owners * 16)) * 16
    expert_slots = -(-2 * requests * fanout // (EXP_OWN * owners * 16)) * 16

    if group_cache.shape[1] % LANES:
        group_columns = group_cache.reshape(-1, KVW).T[None]
    else:
        group_columns = jnp.swapaxes(group_cache, 1, 2)
    rows = exchange(jnp.broadcast_to(hidden[None], (tensors,) + hidden.shape), "tensor")

    projected = project(gather_pieces(rows), attention_gain[None], query_weight)
    projected, group_of, group_length, suffix_length, routes, route_weight = (
        lax.optimization_barrier(
            (projected, group_of, group_length, suffix_length, routes, route_weight)
        )
    )
    destination = group_of // GROUP_OWN
    owner_range = jnp.arange(owners)
    to_owner = (destination ^ owner_index)[:, None] == owner_range[None, :]
    slot_rank = ranks(to_owner)
    placed = to_owner[:, :, None] & (slot_rank[:, :, None] == jnp.arange(slots))
    unpick = placed.reshape(requests, owners * slots).astype(jnp.bfloat16)
    pick = unpick.T
    asked = jnp.sum(
        jnp.where(placed, (group_of % GROUP_OWN + 1)[:, None, None], 0), axis=0
    ).astype(jnp.bfloat16)
    named = routes.astype(jnp.bfloat16).reshape(slots, requests * fanout // slots)
    extra = jnp.where(
        jnp.arange(LANES) == 0,
        asked[:, :, None],
        jnp.pad(named, ((0, 0), (1, LANES - 1 - named.shape[1])))[None],
    )
    suffix_span, group_span = suffix_cache.shape[1], group_cache.shape[1]
    suffix_usable = (
        tensor_index * suffix_span + jnp.arange(suffix_span)[None, :] < suffix_length[:, None]
    )
    suffix_holder = jnp.where(suffix_usable, jnp.arange(requests)[:, None], -1).reshape(1, -1)
    group_usable = (
        tensor_index * group_span + jnp.arange(group_span)[None, :] < group_length[:, None]
    )
    group_holder = (
        jnp.where(group_usable, jnp.arange(1, GROUP_OWN + 1)[:, None], -1)
        .reshape(1, -1)
        .astype(jnp.float32)
    )
    if tensors == PIECES:
        base = tensor_index
        pieces = [projected] + [turn(projected, k) for k in (1, 2, 3)]
        pieces.append(turn(projected, 4))
        pieces += [turn(pieces[4], k) for k in (1, 2, 3)]
    else:
        base = jnp.zeros((), jnp.int32)
        copies = jnp.broadcast_to(projected[None], (tensors,) + projected.shape)
        queries = gather_pieces(exchange(copies, "tensor"))
        pieces = [queries[k] for k in range(PIECES)]
    near, far = pieces[: PIECES // 2], pieces[PIECES // 2 :]
    arrived = [swap_owners(pick_queries(pick, extra, near))]
    all_routes = jnp.stack(
        [x[:, HEADS * KVW + 1 : HEADS * KVW + 1 + named.shape[1]] for x in arrived[0]]
    ).reshape(1, owners, requests, fanout)
    turned = owner_range[:, None] ^ owner_index == owner_range[None, :]
    all_routes = jnp.sum(
        jnp.where(turned[:, :, None, None], all_routes.astype(jnp.int32), 0), axis=1
    )
    mine = owner_index * EXP_OWN + tensor_index // split
    called = jnp.any(all_routes == mine, axis=2)
    call_rank = ranks(called.T).T
    expert_pick = called[:, None, :] & (
        call_rank[:, None, :] == jnp.arange(expert_slots)[None, :, None]
    )
    seen = owner_range.reshape(2, pairs)
    seen = 2 * (seen % pairs) + seen // pairs
    expert_pick = jnp.where(
        (owner_range[:, None] == seen.reshape(-1)[None, :])[:, None, :, None],
        expert_pick[:, :, None, :],
        False,
    )
    shared_pick = (
        owner_range[:, None, None] * requests
        + owner_index * token_share
        + jnp.arange(token_share)[None, :, None]
    ).reshape(-1, 1) == (seen.reshape(-1, 1) * requests + jnp.arange(requests)).reshape(1, -1)
    expert_pick = jnp.concatenate(
        [expert_pick.reshape(owners * expert_slots, owners * requests), shared_pick], axis=0
    ).astype(jnp.bfloat16)
    root_columns, suffix_rows = root_cache.T, suffix_cache.reshape(-1, KVW)
    near, far[0] = lax.optimization_barrier((near, far[0]))
    first = [own_attention(near, suffix_holder, root_columns, suffix_rows)]
    far, first = lax.optimization_barrier((far, first))
    sent = pick_queries(pick, extra, far)
    arrived[0], sent = lax.optimization_barrier((arrived[0], sent))
    arrived.append(swap_owners(sent))
    back = []
    for share in arrived:
        if back:
            share, answered = lax.optimization_barrier((share, answered))
            back[0] = swap_owners(answered)
        answered = group_attention(share, group_columns, group_holder)
        back.append(swap_owners(answered))
    far, answered, expert_pick = lax.optimization_barrier((far, answered, expert_pick))
    back[1] = swap_owners(answered)
    first.append(own_attention(far, suffix_holder, root_columns, suffix_rows))
    back, gain = lax.optimization_barrier((back, mixture_gain[None]))
    parts = local_join(base[None], unpick, first, sum(back, []), tensors)
    attention = exchange(join(exchange(parts, "tensor")), "tensor")
    mid, copies = output_projection(
        attention.reshape(-1, LAT), out_weight, hidden, owners // 2 * tensors
    )

    half = exchange(copies, ("pair", "tensor"))
    both = lax.all_gather(half.reshape((pairs, tensors) + mid.shape), "core")
    everything = gather_pieces(both.reshape((owners, tensors) + mid.shape))
    results = expert(
        expert_pick,
        everything,
        gain,
        expert_slots,
        (shared_gate, shared_up, shared_down),
        (expert_gate, expert_up, expert_down),
    )
    results, routes, route_weight = lax.optimization_barrier((results, routes, route_weight))
    results = scatter_pieces(results, tensors).reshape((owners * tensors, -1, mid.shape[1]))
    returned = exchange(results, ("pair", "core", "tensor"))
    experts = jnp.arange(owners * EXP_OWN)
    hits = routes[:, :, None] == experts[None, None, :]
    share = jnp.sum(jnp.where(hits, route_weight[:, :, None], 0.0), axis=1)
    hit = jnp.any(hits, axis=1)
    taken = hit[:, :, None] & (ranks(hit)[:, :, None] == jnp.arange(expert_slots))
    back_weight = jnp.where(taken, share[:, :, None], 0.0)
    back_weight = jnp.repeat(back_weight, split, axis=1)
    shared_weight = np.eye(requests, dtype=np.float32).reshape(requests, owners, 1, token_share)
    shared_weight = np.repeat(shared_weight, tensors, axis=2).reshape(
        requests, owners * tensors, token_share
    )
    back_weight = jnp.concatenate([back_weight, shared_weight], axis=2).reshape(requests, -1)
    return final_sum(returned.reshape(-1, mid.shape[1]), back_weight, mid)


def solution(mesh):
    owners, tensors = mesh.shape["owner"], mesh.shape["tensor"]
    devices = mesh.devices.reshape(owners // 2, 2, tensors)
    return jax.shard_map(
        local,
        mesh=Mesh(devices, OWNER + ("tensor",)),
        in_specs=(
            P(OWNER, "tensor"),
            P(),
            P("tensor", None),
            P("tensor", None),
            P("tensor", None),
            P(OWNER, "tensor", None),
            P(OWNER),
            P(OWNER, "tensor", None),
            P(OWNER),
            P(OWNER),
            P(),
            P(OWNER, None),
            P(OWNER, None),
            P(OWNER + ("tensor",), None, None),
            P(OWNER + ("tensor",), None, None),
            P(OWNER + ("tensor",), None, None),
            P("tensor", None),
            P("tensor", None),
            P("tensor", None),
        ),
        out_specs=P(OWNER, "tensor"),
        check_vma=False,
    )
```

```python
import functools

import jax
import jax.numpy as jnp
import numpy as np
from jax import lax
from jax.experimental import pallas as pl
from jax.experimental.pallas import tpu as pltpu
from jax.sharding import Mesh
from jax.sharding import PartitionSpec as P

H = 16
LAT = 512
KVW = 576
EXP_OWN = 8
GROUP_OWN = 12
PIECES = 8
PAIR = 2 * KVW
LANES = 128
OWNER = ("pair", "core")
SHARES = 2
HEADS = H // SHARES
MASS_ROWS = 8
MIB = 1 << 20

score_scale = 192.0 ** (-0.5)
log2e = 1.4426950408889634
ln2 = 0.6931471805599453
lowest = -1e30
epsilon = 1e-06

NT = (((1,), (1,)), ((), ()))


def dot_nt(a, b):
    return lax.dot_general(a, b, NT, preferred_element_type=jnp.float32)


def dot_nn(a, b):
    return jnp.dot(a, b, preferred_element_type=jnp.float32)


def call(body, out_shape, vmem_mib, flops, nbytes, **options):
    return pl.pallas_call(
        body,
        out_shape=out_shape,
        compiler_params=pltpu.CompilerParams(vmem_limit_bytes=vmem_mib * MIB),
        cost_estimate=pl.CostEstimate(
            flops=int(flops), bytes_accessed=int(nbytes), transcendentals=0
        ),
        **options,
    )


VMEM = pl.BlockSpec(memory_space=pltpu.VMEM)
HBM = pl.BlockSpec(memory_space=pltpu.HBM)


def in_hbm(x):
    return pltpu.with_memory_space_constraint(x, pltpu.HBM)


def whole(shape):
    return pl.BlockSpec(shape, lambda *_: (0,) * len(shape))


def split_three(column):
    first = column.astype(jnp.bfloat16).astype(jnp.float32)
    second = (column - first).astype(jnp.bfloat16).astype(jnp.float32)
    third = (column - first - second).astype(jnp.bfloat16).astype(jnp.float32)
    return first, second, third


def normalised(read_piece, gain, width):
    rows = jnp.concatenate([read_piece(k) for k in range(PIECES)], axis=-1).astype(jnp.float32)
    square = jnp.sum(rows * rows, axis=-1, keepdims=True) * (1.0 / width)
    return (rows * lax.rsqrt(square + epsilon) * gain.astype(jnp.float32)).astype(jnp.bfloat16)


def project_body(rows_ref, gain_ref, weight_hbm, out_ref, weight_ref, sems):
    steps, each, width = weight_ref.shape
    copies = [
        pltpu.make_async_copy(
            weight_hbm.at[pl.ds(c * each, each)], weight_ref.at[c], sems.at[c]
        )
        for c in range(steps)
    ]
    for copy in copies:
        copy.start()
    normed = normalised(lambda k: rows_ref[k], gain_ref[...], width)
    for step in range(steps):
        copies[step].wait()
        out = dot_nt(normed, weight_ref[step]).astype(jnp.bfloat16)
        out_ref[:, step * each : (step + 1) * each] = out


def project(rows, gain, weight):
    pieces, requests, part = rows.shape
    columns, width = weight.shape
    steps = 3 if columns % (3 * LANES) == 0 else 1
    return call(
        project_body,
        jax.ShapeDtypeStruct((requests, columns), jnp.bfloat16),
        16,
        2 * requests * columns * width,
        2 * columns * width,
        in_specs=[VMEM, VMEM, HBM],
        out_specs=VMEM,
        scratch_shapes=[
            pltpu.VMEM((steps, columns // steps, width), jnp.bfloat16),
            pltpu.SemaphoreType.DMA((steps,)),
        ],
    )(rows, gain, in_hbm(weight))


def pick_body(pick_ref, extra_ref, *refs):
    slots = extra_ref.shape[1]
    each = PIECES // SHARES
    rows_refs, out_refs = refs[:each], refs[each:]
    for k in range(each):
        picked = dot_nn(pick_ref[...], rows_refs[k][...]).astype(jnp.bfloat16)
        for o, out_ref in enumerate(out_refs):
            out_ref[:, k * PAIR : (k + 1) * PAIR] = picked[o * slots : (o + 1) * slots]
    for o, out_ref in enumerate(out_refs):
        out_ref[:, each * PAIR :] = extra_ref[o]


def pick_queries(pick, extra, rows):
    owners, slots, _ = extra.shape
    return call(
        pick_body,
        (jax.ShapeDtypeStruct((slots, HEADS * KVW + LANES), jnp.bfloat16),) * owners,
        16,
        2 * owners * slots * pick.shape[1] * HEADS * KVW,
        4 * owners * slots * HEADS * KVW,
    )(pick, extra, *rows)


def sums(scores, usable=None):
    if usable is not None:
        scores = [jnp.where(u, x, lowest) for u, x in zip(usable, scores)]
    peak = functools.reduce(
        jnp.maximum, [jnp.max(x, axis=-1, keepdims=True) for x in scores]
    )
    weights = [jnp.exp2(x - peak) for x in scores]
    if usable is not None:
        weights = [jnp.where(u, w, 0.0) for u, w in zip(usable, weights)]
    total = functools.reduce(jnp.add, [jnp.sum(w, axis=-1, keepdims=True) for w in weights])
    return peak, [w.astype(jnp.bfloat16) for w in weights], total


def own_body(holder_ref, root_hbm, suffix_hbm, *refs):
    rows_refs, out_hbm = refs[: HEADS // 2], refs[HEADS // 2]
    out_ref, q_ref, root_ref, suffix_ref, s_ref, root_sems, suffix_sems, out_sem = refs[
        HEADS // 2 + 1 :
    ]
    requests = rows_refs[0].shape[0]
    blocks, _, block = root_ref.shape
    groups, span, _ = suffix_ref.shape
    each = requests // groups
    root_copies = [
        pltpu.make_async_copy(
            root_hbm.at[:, pl.ds(b * block, block)], root_ref.at[b], root_sems.at[b]
        )
        for b in range(blocks)
    ]
    suffix_copies = [
        pltpu.make_async_copy(
            suffix_hbm.at[pl.ds(g * span, span)], suffix_ref.at[g], suffix_sems.at[g]
        )
        for g in range(groups)
    ]
    for copy in root_copies + suffix_copies:
        copy.start()
    for h in range(HEADS):
        k, j = divmod(h, 2)
        q_ref[h * requests : (h + 1) * requests, :] = rows_refs[k][:, j * KVW : (j + 1) * KVW]
    scale = score_scale * log2e
    for b in range(blocks):
        root_copies[b].wait()
        s_ref[b] = dot_nn(q_ref[...], root_ref[b]) * scale
    root_peak, weights, root_total = sums([s_ref[b] for b in range(blocks)])
    root_out = functools.reduce(
        jnp.add, [dot_nt(weights[b], root_ref[b, :LAT, :]) for b in range(blocks)]
    )
    for g in range(groups):
        suffix_copies[g].wait()
        mine = [slice(h * requests + g * each, h * requests + (g + 1) * each) for h in range(HEADS)]
        scores = dot_nt(
            jnp.concatenate([q_ref[at, :] for at in mine], axis=0), suffix_ref[g]
        )
        request = lax.broadcasted_iota(jnp.int32, (HEADS * each, 1), 0) % each + g * each
        usable = holder_ref[:, g * span : (g + 1) * span] == request
        peak, weights, total = sums([scores * scale], [usable])
        out = dot_nn(weights[0], suffix_ref[g, :, :LAT])
        for h, at in enumerate(mine):
            own = slice(h * each, (h + 1) * each)
            top = jnp.maximum(root_peak[at], peak[own])
            root_scale = jnp.exp2(root_peak[at] - top)
            scaled = jnp.exp2(peak[own] - top)
            both = root_total[at] * root_scale + total[own] * scaled
            out_ref[at, :LAT] = (root_out[at] * root_scale + out[own] * scaled) / both
            out_ref[at, LAT:] = jnp.broadcast_to(top * ln2 + jnp.log(both), (each, LANES))
    copy = pltpu.make_async_copy(out_ref, out_hbm, out_sem)
    copy.start()
    copy.wait()


def own_attention(rows, holder, root, suffix):
    count = HEADS * rows[0].shape[0]
    positions = root.shape[1]
    block = min(1024, positions)
    blocks, groups = positions // block, 2
    span = suffix.shape[0] // groups
    return call(
        own_body,
        pltpu.HBM((count, LAT + LANES), jnp.float32),
        44,
        2 * count * (positions + span) * (KVW + LAT),
        2 * KVW * (positions + suffix.shape[0]),
        in_specs=[VMEM, HBM, HBM] + [VMEM] * len(rows),
        out_specs=HBM,
        scratch_shapes=[
            pltpu.VMEM((count, LAT + LANES), jnp.float32),
            pltpu.VMEM((count, KVW), jnp.bfloat16),
            pltpu.VMEM((blocks, KVW, block), jnp.bfloat16),
            pltpu.VMEM((groups, span, KVW), jnp.bfloat16),
            pltpu.VMEM((blocks, count, block), jnp.float32),
            pltpu.SemaphoreType.DMA((blocks,)),
            pltpu.SemaphoreType.DMA((groups,)),
            pltpu.SemaphoreType.DMA,
        ],
    )(holder, in_hbm(root), in_hbm(suffix), *rows)


def group_body(owners, cache_hbm, holder_ref, *refs):
    rows_refs, out_refs = refs[:owners], refs[owners : 2 * owners]
    q_ref, keys_ref, sems = refs[2 * owners :]
    slots = rows_refs[0].shape[0]
    groups, _, span = cache_hbm.shape
    copies = [
        pltpu.make_async_copy(
            cache_hbm.at[g], keys_ref.at[:, pl.ds(g * span, span)], sems.at[g]
        )
        for g in range(groups)
    ]
    for copy in copies:
        copy.start()
    each = HEADS * slots
    for o in range(owners):
        for h in range(HEADS):
            at = o * each + h * slots
            q_ref[at : at + slots, :] = rows_refs[o][:, h * KVW : (h + 1) * KVW]
    lane = lax.broadcasted_iota(jnp.int32, (slots, LANES), 1)
    both = 2 * each
    blocks = 3 if groups % 3 == 0 else 1
    scores = [[] for _ in range(owners // 2)]
    for b in range(blocks):
        for copy in copies[b * groups // blocks : (b + 1) * groups // blocks]:
            copy.wait()
        at = slice(b * groups * span // blocks, (b + 1) * groups * span // blocks)
        for pair in range(owners // 2):
            scores[pair].append(
                dot_nn(q_ref[pair * both : (pair + 1) * both, :], keys_ref[:, at])
            )
    for pair in range(owners // 2):
        asked = [
            rows_refs[o][:, HEADS * KVW :][:, :1].astype(jnp.float32)
            for o in (2 * pair, 2 * pair + 1)
        ]
        asked = jnp.concatenate([asked[0]] * HEADS + [asked[1]] * HEADS, axis=0)
        usable = holder_ref[...] == asked
        block = jnp.concatenate(scores[pair], axis=1) * (score_scale * log2e)
        block = jnp.where(usable, block, lowest)
        peak = jnp.max(block, axis=-1, keepdims=True)
        weights = jnp.where(usable, jnp.exp2(block - peak), 0.0)
        total = jnp.sum(weights, axis=-1, keepdims=True)
        present = total > 0.0
        safe = jnp.where(present, total, 1.0)
        block_out = dot_nt(weights.astype(jnp.bfloat16), keys_ref[:LAT, :]) / safe
        mass = jnp.where(present, peak * ln2 + jnp.log(safe), lowest)
        for o in (2 * pair, 2 * pair + 1):
            out_ref = out_refs[o]
            extra = jnp.zeros((slots, LANES), jnp.float32)
            for h in range(HEADS):
                at = (o - 2 * pair) * each + h * slots
                at = slice(at, at + slots)
                out_ref[:, h * LAT : (h + 1) * LAT] = block_out[at].astype(jnp.bfloat16)
                for k, part in enumerate(split_three(mass[at])):
                    extra = jnp.where(lane == k * HEADS + h, part, extra)
            out_ref[:, HEADS * LAT :] = extra.astype(jnp.bfloat16)


def group_attention(rows, cache, holder):
    owners, slots = len(rows), rows[0].shape[0]
    groups, _, span = cache.shape
    out = jax.ShapeDtypeStruct((slots, HEADS * LAT + LANES), jnp.bfloat16)
    return call(
        functools.partial(group_body, owners),
        (out,) * owners,
        40,
        2 * owners * slots * HEADS * groups * span * (KVW + LAT),
        2 * KVW * groups * span,
        in_specs=[HBM, VMEM] + [VMEM] * owners,
        out_specs=(VMEM,) * owners,
        scratch_shapes=[
            pltpu.VMEM((owners * HEADS * slots, KVW), jnp.bfloat16),
            pltpu.VMEM((KVW, groups * span), jnp.bfloat16),
            pltpu.SemaphoreType.DMA((groups,)),
        ],
    )(in_hbm(cache), holder, *rows)


def mass_rows(mass):
    length = mass.shape[0]
    diagonal = lax.broadcasted_iota(jnp.int32, (length, LAT), 0) == lax.broadcasted_iota(
        jnp.int32, (length, LAT), 1
    )
    line = jnp.sum(jnp.where(diagonal, mass, 0.0), axis=0, keepdims=True)
    row = lax.broadcasted_iota(jnp.int32, (MASS_ROWS, LAT), 0)
    tail = jnp.zeros((MASS_ROWS, LAT), jnp.float32)
    for k, part in enumerate(split_three(line)):
        tail = jnp.where(row == k, part, tail)
    return tail.astype(jnp.bfloat16)


def mass_column(tail, length):
    diagonal = lax.broadcasted_iota(jnp.int32, (length, LAT), 0) == lax.broadcasted_iota(
        jnp.int32, (length, LAT), 1
    )
    tail = tail.astype(jnp.float32)
    line = tail[0:1] + tail[1:2] + tail[2:3]
    return jnp.sum(jnp.where(diagonal, line, 0.0), axis=1, keepdims=True)


def local_body(unpick_ref, *refs):
    first_hbm, refs = refs[:SHARES], refs[SHARES:]
    back_refs, refs = refs[: -PIECES - 3], refs[-PIECES - 3 :]
    out_refs, (first_ref, out_mass_ref, sems) = refs[:PIECES], refs[PIECES:]
    copies = [
        pltpu.make_async_copy(first_hbm[k], first_ref.at[k], sems.at[k]) for k in range(SHARES)
    ]
    for copy in copies:
        copy.start()
    owners = len(back_refs) // SHARES
    requests = unpick_ref.shape[0]
    unpick = unpick_ref[...]

    def returned(share, at):
        rows = [ref[:, at] for ref in back_refs[share * owners : (share + 1) * owners]]
        return dot_nn(unpick, jnp.concatenate(rows, axis=0))

    extras = [returned(share, slice(HEADS * LAT, None)) for share in range(SHARES)]
    cuts, length = out_refs[0].shape[0], out_refs[0].shape[1] - MASS_ROWS
    each = min(length, requests)
    for h in range(H):
        share, head = divmod(h, HEADS)
        if head == 0:
            copies[share].wait()
        at = slice(head * requests, (head + 1) * requests)
        group_out = returned(share, slice(head * LAT, (head + 1) * LAT))
        group_mass = functools.reduce(
            jnp.add,
            [extras[share][:, k * HEADS + head : k * HEADS + head + 1] for k in range(3)],
        )
        first_mass = first_ref[share, at, LAT : LAT + 1]
        peak = jnp.maximum(first_mass, group_mass)
        first_weight = jnp.exp(first_mass - peak)
        group_weight = jnp.exp(group_mass - peak)
        total = first_weight + group_weight
        out = (first_weight * first_ref[share, at, :LAT] + group_weight * group_out) / total
        out = out.astype(jnp.bfloat16)
        for k in range(requests // each):
            cut, row = divmod(h % 2 * requests + k * each, length)
            out_refs[h // 2][cut, row : row + each, :] = out[k * each : (k + 1) * each]
        out_mass_ref[h * requests : (h + 1) * requests, :] = peak + jnp.log(total)
    for piece in range(PIECES):
        for cut in range(cuts):
            at = piece * 2 * requests + cut * length
            out_refs[piece][cut, length:, :] = mass_rows(out_mass_ref[at : at + length, :])


def local_join(unpick, first, back, cuts):
    count = SHARES * first[0].shape[0]
    out = jax.ShapeDtypeStruct((cuts, count // PIECES // cuts + MASS_ROWS, LAT), jnp.bfloat16)
    return call(
        local_body,
        (out,) * PIECES,
        10,
        2 * unpick.shape[0] * unpick.shape[1] * H * LAT,
        4 * count * LAT,
        in_specs=[VMEM] + [HBM] * SHARES + [VMEM] * len(back),
        out_specs=(VMEM,) * PIECES,
        scratch_shapes=[
            pltpu.VMEM((SHARES,) + first[0].shape, jnp.float32),
            pltpu.VMEM((count, 1), jnp.float32),
            pltpu.SemaphoreType.DMA((SHARES,)),
        ],
    )(unpick, *[in_hbm(x) for x in first], *back)


def join_body(further, *refs):
    parts_refs, out_ref = refs[:-1], refs[-1]
    length = parts_refs[0].shape[0] - MASS_ROWS
    masses = [mass_column(ref[length:, :], length) for ref in parts_refs]
    peak = functools.reduce(jnp.maximum, masses)
    scales = [jnp.exp(mass - peak) for mass in masses]
    total = functools.reduce(jnp.add, scales)
    out = functools.reduce(
        jnp.add,
        [scale * ref[:length, :].astype(jnp.float32) for scale, ref in zip(scales, parts_refs)],
    )
    out = (out / total).astype(jnp.bfloat16)
    if further:
        out_ref[:length, :] = out
        out_ref[length:, :] = mass_rows(peak + jnp.log(total))
    else:
        for c in range(out_ref.shape[0]):
            out_ref[c] = out


def join(parts, copies=0):
    rows = parts[0].shape[0]
    shape = (copies, rows - MASS_ROWS, LAT) if copies else (rows, LAT)
    return call(
        functools.partial(join_body, not copies),
        jax.ShapeDtypeStruct(shape, jnp.bfloat16),
        6,
        3e10 if copies else 2 * len(parts) * rows * LAT,
        4 * len(parts) * rows * LAT,
        in_specs=[VMEM] * len(parts),
        out_specs=VMEM,
    )(*parts)


def output_body(rows_ref, weight_ref, hidden_ref, out_ref, copies_ref):
    requests = hidden_ref.shape[0]
    total = hidden_ref[...].astype(jnp.float32)
    for h in range(H):
        total = total + dot_nt(
            rows_ref[h * requests : (h + 1) * requests, :],
            weight_ref[:, h * LAT : (h + 1) * LAT],
        )
    out = total.astype(jnp.bfloat16)
    out_ref[...] = out
    for c in range(copies_ref.shape[0]):
        copies_ref[c] = out


def output_projection(rows, weight, hidden, copies):
    features, width = weight.shape
    requests = hidden.shape[0]
    return call(
        output_body,
        (
            jax.ShapeDtypeStruct(hidden.shape, jnp.bfloat16),
            jax.ShapeDtypeStruct((copies,) + hidden.shape, jnp.bfloat16),
        ),
        8,
        2 * requests * features * width,
        2 * features * width,
        in_specs=[VMEM] * 3,
        out_specs=(VMEM, VMEM),
    )(rows, weight, hidden)


def gated(rows, gate, up):
    gate_part = dot_nt(rows, gate)
    up_part = dot_nt(rows, up)
    return (gate_part / (1.0 + jnp.exp(-gate_part)) * up_part).astype(jnp.bfloat16)


def expert_body(pick_ref, rows_ref, gain_ref, shared_gate_ref, shared_up_ref, shared_down_ref, gate_ref, up_ref, down_ref, out_ref):
    owners, _, requests, part = rows_ref.shape
    width = gain_ref.shape[1]
    share = requests // owners
    slots = out_ref.shape[2] - share
    rows = jnp.concatenate(
        [
            normalised(lambda k, o=o: rows_ref[o, k], gain_ref[...], width)
            for o in range(owners)
        ],
        axis=0,
    )
    rows = dot_nn(pick_ref[...], rows).astype(jnp.bfloat16)
    named, rest = rows[: owners * slots], rows[owners * slots :]
    shared = dot_nn(gated(rest, shared_gate_ref[...], shared_up_ref[...]), shared_down_ref[...])
    units = gate_ref.shape[1]
    steps = 4 if units % 64 == 0 and units > 704 else 1
    each = units // steps
    total = jnp.zeros((owners * slots, width), jnp.float32)
    for c in range(steps):
        at = slice(c * each, (c + 1) * each)
        total = total + dot_nn(
            gated(named, gate_ref[0, at, :], up_ref[0, at, :]), down_ref[0, at, :]
        )
    for o in range(owners):
        both = jnp.concatenate(
            [total[o * slots : (o + 1) * slots], shared[o * share : (o + 1) * share]], axis=0
        ).astype(jnp.bfloat16)
        for k in range(PIECES):
            out_ref[o, k] = both[:, k * part : (k + 1) * part]


def expert(pick, rows, gain, slots, shared, weights):
    owners, _, requests, part = rows.shape
    _, units, width = weights[0].shape
    return call(
        expert_body,
        jax.ShapeDtypeStruct(
            (owners, PIECES, slots + requests // owners, part), jnp.bfloat16
        ),
        12,
        6 * pick.shape[0] * units * width,
        6 * units * width,
        in_specs=[VMEM] * 9,
        out_specs=VMEM,
    )(pick, rows, gain, *shared, *weights)


def final_body(parts_ref, weight_ref, mid_ref, out_ref):
    weight = weight_ref[...]
    high = weight.astype(jnp.bfloat16)
    rest = weight - high.astype(jnp.float32)
    low = rest.astype(jnp.bfloat16)
    lower = (rest - low.astype(jnp.float32)).astype(jnp.bfloat16)
    parts = parts_ref[...]
    total = dot_nn(high, parts) + (dot_nn(low, parts) + dot_nn(lower, parts))
    out_ref[...] = (mid_ref[...].astype(jnp.float32) + total).astype(jnp.bfloat16)


def final_sum(parts, weight, mid):
    return call(
        final_body,
        jax.ShapeDtypeStruct(mid.shape, jnp.bfloat16),
        16,
        2 * weight.shape[0] * parts.shape[0] * parts.shape[1],
        2 * parts.shape[0] * parts.shape[1],
    )(parts, weight, mid)


def exchange(x, axis):
    return lax.all_to_all(x, axis, 0, 0, tiled=True)


def turn(x, k):
    count = lax.axis_size("tensor")
    return lax.ppermute(x, "tensor", [(i, i ^ k) for i in range(count)])


def swap_owners(arrays):
    count = len(arrays)
    out = {0: arrays[0]}
    for k in reversed(range(1, count)):
        out[k] = lax.ppermute(arrays[k], OWNER, [(i, i ^ k) for i in range(count)])
    return [out[k] for k in range(count)]


def gather_pieces(x):
    devices = x.shape[-3]
    each = devices // PIECES
    if each == 1:
        return x
    lead, (rows, columns) = x.shape[:-3], x.shape[-2:]
    x = x.reshape(lead + (PIECES, each, rows, columns))
    return jnp.swapaxes(x, -3, -2).reshape(lead + (PIECES, rows, each * columns))


def scatter_pieces(x, devices):
    each = devices // PIECES
    if each == 1:
        return x
    lead, (rows, columns) = x.shape[:-3], x.shape[-2:]
    x = x.reshape(lead + (PIECES, rows, each, columns // each))
    return jnp.swapaxes(x, -3, -2).reshape(lead + (devices, rows, columns // each))


def ranks(hits):
    count = hits.shape[0]
    ahead = jnp.arange(count)[:, None] > jnp.arange(count)[None, :]
    return jnp.sum(jnp.where(ahead[:, :, None], hits.astype(jnp.int32)[None], 0), axis=1)


def local(
    hidden,
    attention_gain,
    query_weight,
    out_weight,
    root_cache,
    group_cache,
    group_length,
    suffix_cache,
    suffix_length,
    group_of,
    mixture_gain,
    routes,
    route_weight,
    expert_gate,
    expert_up,
    expert_down,
    shared_gate,
    shared_up,
    shared_down,
):
    owners, tensors = lax.axis_size(OWNER), lax.axis_size("tensor")
    owner_index, tensor_index = lax.axis_index(OWNER), lax.axis_index("tensor")
    requests = hidden.shape[0]
    fanout = routes.shape[1]
    token_share = requests // owners
    pairs = owners // 2
    split = tensors // EXP_OWN
    slots = -(-2 * requests // (owners * 16)) * 16
    expert_slots = -(-2 * requests * fanout // (EXP_OWN * owners * 16)) * 16

    if group_cache.shape[1] % LANES:
        group_columns = group_cache.reshape(-1, KVW).T[None]
    else:
        group_columns = jnp.swapaxes(group_cache, 1, 2)
    rows = exchange(jnp.broadcast_to(hidden[None], (tensors,) + hidden.shape), "tensor")

    projected = project(gather_pieces(rows), attention_gain[None], query_weight)
    projected, group_of, group_length, suffix_length, routes, route_weight = (
        lax.optimization_barrier(
            (projected, group_of, group_length, suffix_length, routes, route_weight)
        )
    )
    destination = group_of // GROUP_OWN
    owner_range = jnp.arange(owners)
    to_owner = (destination ^ owner_index)[:, None] == owner_range[None, :]
    slot_rank = ranks(to_owner)
    placed = to_owner[:, :, None] & (slot_rank[:, :, None] == jnp.arange(slots))
    unpick = placed.reshape(requests, owners * slots).astype(jnp.bfloat16)
    pick = unpick.T
    asked = jnp.sum(
        jnp.where(placed, (group_of % GROUP_OWN + 1)[:, None, None], 0), axis=0
    ).astype(jnp.bfloat16)
    named = routes.astype(jnp.bfloat16).reshape(slots, requests * fanout // slots)
    extra = jnp.where(
        jnp.arange(LANES) == 0,
        asked[:, :, None],
        jnp.pad(named, ((0, 0), (1, LANES - 1 - named.shape[1])))[None],
    )
    suffix_span, group_span = suffix_cache.shape[1], group_cache.shape[1]
    suffix_usable = (
        tensor_index * suffix_span + jnp.arange(suffix_span)[None, :] < suffix_length[:, None]
    )
    suffix_holder = jnp.where(suffix_usable, jnp.arange(requests)[:, None], -1).reshape(1, -1)
    group_usable = (
        tensor_index * group_span + jnp.arange(group_span)[None, :] < group_length[:, None]
    )
    group_holder = (
        jnp.where(group_usable, jnp.arange(1, GROUP_OWN + 1)[:, None], -1)
        .reshape(1, -1)
        .astype(jnp.float32)
    )
    if tensors == PIECES:
        pieces = [projected] + [turn(projected, k) for k in (1, 2, 3)]
        pieces.append(turn(projected, 4))
        pieces += [turn(pieces[4], k) for k in (1, 2, 3)]
    else:
        copies = jnp.broadcast_to(projected[None], (tensors,) + projected.shape)
        queries = gather_pieces(exchange(copies, "tensor"))
        pieces = [queries[k] for k in range(PIECES)]
    near, far = pieces[: PIECES // 2], pieces[PIECES // 2 :]
    arrived = [swap_owners(pick_queries(pick, extra, near))]
    all_routes = jnp.stack(
        [x[:, HEADS * KVW + 1 : HEADS * KVW + 1 + named.shape[1]] for x in arrived[0]]
    ).reshape(1, owners, requests, fanout)
    turned = owner_range[:, None] ^ owner_index == owner_range[None, :]
    all_routes = jnp.sum(
        jnp.where(turned[:, :, None, None], all_routes.astype(jnp.int32), 0), axis=1
    )
    mine = owner_index * EXP_OWN + tensor_index // split
    called = jnp.any(all_routes == mine, axis=2)
    call_rank = ranks(called.T).T
    expert_pick = called[:, None, :] & (
        call_rank[:, None, :] == jnp.arange(expert_slots)[None, :, None]
    )
    seen = owner_range.reshape(2, pairs)
    seen = 2 * (seen % pairs) + seen // pairs
    expert_pick = jnp.where(
        (owner_range[:, None] == seen.reshape(-1)[None, :])[:, None, :, None],
        expert_pick[:, :, None, :],
        False,
    )
    shared_pick = (
        owner_range[:, None, None] * requests
        + owner_index * token_share
        + jnp.arange(token_share)[None, :, None]
    ).reshape(-1, 1) == (seen.reshape(-1, 1) * requests + jnp.arange(requests)).reshape(1, -1)
    expert_pick = jnp.concatenate(
        [expert_pick.reshape(owners * expert_slots, owners * requests), shared_pick], axis=0
    ).astype(jnp.bfloat16)
    root_columns, suffix_rows = root_cache.T, suffix_cache.reshape(-1, KVW)
    near, far[0] = lax.optimization_barrier((near, far[0]))
    first = [own_attention(near, suffix_holder, root_columns, suffix_rows)]
    far, first = lax.optimization_barrier((far, first))
    sent = pick_queries(pick, extra, far)
    arrived[0], sent = lax.optimization_barrier((arrived[0], sent))
    arrived.append(swap_owners(sent))
    back = []
    for share in arrived:
        if back:
            share, answered = lax.optimization_barrier((share, answered))
            back[0] = swap_owners(answered)
        answered = group_attention(share, group_columns, group_holder)
        back.append(swap_owners(answered))
    far, answered, expert_pick = lax.optimization_barrier((far, answered, expert_pick))
    back[1] = swap_owners(answered)
    first.append(own_attention(far, suffix_holder, root_columns, suffix_rows))
    back, gain = lax.optimization_barrier((back, mixture_gain[None]))
    parts = local_join(unpick, first, sum(back, []), tensors // PIECES)
    if tensors == PIECES:
        parts = [part[0] for part in parts]
        crossing = join([parts[4]] + [turn(parts[4 + k], k) for k in (1, 2, 3)])
        parts = [parts[0]] + [turn(parts[k], k) for k in (1, 2, 3)] + [turn(crossing, 4)]
    else:
        parts = exchange(jnp.concatenate(parts, axis=0), "tensor")
        parts = [parts[k] for k in range(tensors)]
    attention = exchange(join(parts, tensors), "tensor")
    mid, copies = output_projection(
        attention.reshape(-1, LAT), out_weight, hidden, owners // 2 * tensors
    )

    half = exchange(copies, ("pair", "tensor"))
    both = lax.all_gather(half.reshape((pairs, tensors) + mid.shape), "core")
    everything = gather_pieces(both.reshape((owners, tensors) + mid.shape))
    results = expert(
        expert_pick,
        everything,
        gain,
        expert_slots,
        (shared_gate, shared_up, shared_down),
        (expert_gate, expert_up, expert_down),
    )
    results, routes, route_weight = lax.optimization_barrier((results, routes, route_weight))
    results = scatter_pieces(results, tensors).reshape((owners * tensors, -1, mid.shape[1]))
    returned = exchange(results, ("pair", "core", "tensor"))
    experts = jnp.arange(owners * EXP_OWN)
    hits = routes[:, :, None] == experts[None, None, :]
    share = jnp.sum(jnp.where(hits, route_weight[:, :, None], 0.0), axis=1)
    hit = jnp.any(hits, axis=1)
    taken = hit[:, :, None] & (ranks(hit)[:, :, None] == jnp.arange(expert_slots))
    back_weight = jnp.where(taken, share[:, :, None], 0.0)
    back_weight = jnp.repeat(back_weight, split, axis=1)
    shared_weight = np.eye(requests, dtype=np.float32).reshape(requests, owners, 1, token_share)
    shared_weight = np.repeat(shared_weight, tensors, axis=2).reshape(
        requests, owners * tensors, token_share
    )
    back_weight = jnp.concatenate([back_weight, shared_weight], axis=2).reshape(requests, -1)
    return final_sum(returned.reshape(-1, mid.shape[1]), back_weight, mid)


def solution(mesh):
    owners, tensors = mesh.shape["owner"], mesh.shape["tensor"]
    devices = mesh.devices.reshape(owners // 2, 2, tensors)
    return jax.shard_map(
        local,
        mesh=Mesh(devices, OWNER + ("tensor",)),
        in_specs=(
            P(OWNER, "tensor"),
            P(),
            P("tensor", None),
            P("tensor", None),
            P("tensor", None),
            P(OWNER, "tensor", None),
            P(OWNER),
            P(OWNER, "tensor", None),
            P(OWNER),
            P(OWNER),
            P(),
            P(OWNER, None),
            P(OWNER, None),
            P(OWNER + ("tensor",), None, None),
            P(OWNER + ("tensor",), None, None),
            P(OWNER + ("tensor",), None, None),
            P("tensor", None),
            P("tensor", None),
            P("tensor", None),
        ),
        out_specs=P(OWNER, "tensor"),
        check_vma=False,
    )
```

```python
import functools

import jax
import jax.numpy as jnp
import numpy as np
from jax import lax
from jax.experimental import pallas as pl
from jax.experimental.pallas import tpu as pltpu
from jax.sharding import Mesh
from jax.sharding import PartitionSpec as P

H = 16
LAT = 512
KVW = 576
EXP_OWN = 8
GROUP_OWN = 12
PIECES = 8
PAIR = 2 * KVW
LANES = 128
OWNER = ("pair", "core")
SHARES = 2
HEADS = H // SHARES
MASS_ROWS = 8
MIB = 1 << 20

score_scale = 192.0 ** (-0.5)
log2e = 1.4426950408889634
ln2 = 0.6931471805599453
lowest = -1e30
epsilon = 1e-06

NT = (((1,), (1,)), ((), ()))


def dot_nt(a, b):
    return lax.dot_general(a, b, NT, preferred_element_type=jnp.float32)


def dot_nn(a, b):
    return jnp.dot(a, b, preferred_element_type=jnp.float32)


def call(body, out_shape, vmem_mib, flops, nbytes, **options):
    return pl.pallas_call(
        body,
        out_shape=out_shape,
        compiler_params=pltpu.CompilerParams(vmem_limit_bytes=vmem_mib * MIB),
        cost_estimate=pl.CostEstimate(
            flops=int(flops), bytes_accessed=int(nbytes), transcendentals=0
        ),
        **options,
    )


VMEM = pl.BlockSpec(memory_space=pltpu.VMEM)
HBM = pl.BlockSpec(memory_space=pltpu.HBM)


def in_hbm(x):
    return pltpu.with_memory_space_constraint(x, pltpu.HBM)


def whole(shape):
    return pl.BlockSpec(shape, lambda *_: (0,) * len(shape))


def split_three(column):
    first = column.astype(jnp.bfloat16).astype(jnp.float32)
    second = (column - first).astype(jnp.bfloat16).astype(jnp.float32)
    third = (column - first - second).astype(jnp.bfloat16).astype(jnp.float32)
    return first, second, third


def normalised(read_piece, gain, width):
    rows = jnp.concatenate([read_piece(k) for k in range(PIECES)], axis=-1).astype(jnp.float32)
    square = jnp.sum(rows * rows, axis=-1, keepdims=True) * (1.0 / width)
    return (rows * lax.rsqrt(square + epsilon) * gain.astype(jnp.float32)).astype(jnp.bfloat16)


def project_body(base_ref, gain_ref, weight_hbm, *refs):
    rows_refs, (out_ref, rows_ref, weight_ref, sems) = refs[:PIECES], refs[PIECES:]
    steps, each, width = weight_ref.shape
    copies = [
        pltpu.make_async_copy(
            weight_hbm.at[pl.ds(c * each, each)], weight_ref.at[c], sems.at[c]
        )
        for c in range(steps)
    ]
    for copy in copies:
        copy.start()
    part = width // PIECES
    for k in range(PIECES):
        at = pl.multiple_of((k ^ base_ref[0]) * part, part)
        rows_ref[:, pl.ds(at, part)] = rows_refs[k][...]
    normed = normalised(
        lambda k: rows_ref[:, k * part : (k + 1) * part], gain_ref[...], width
    )
    for step in range(steps):
        copies[step].wait()
        out = dot_nt(normed, weight_ref[step]).astype(jnp.bfloat16)
        out_ref[:, step * each : (step + 1) * each] = out


def project(base, rows, gain, weight):
    requests, _ = rows[0].shape
    columns, width = weight.shape
    steps = 3 if columns % (3 * LANES) == 0 else 1
    return call(
        project_body,
        jax.ShapeDtypeStruct((requests, columns), jnp.bfloat16),
        16,
        2 * requests * columns * width,
        2 * columns * width,
        in_specs=[pl.BlockSpec(memory_space=pltpu.SMEM), VMEM, HBM] + [VMEM] * PIECES,
        out_specs=VMEM,
        scratch_shapes=[
            pltpu.VMEM((requests, width), jnp.bfloat16),
            pltpu.VMEM((steps, columns // steps, width), jnp.bfloat16),
            pltpu.SemaphoreType.DMA((steps,)),
        ],
    )(base[None], gain, in_hbm(weight), *rows)


def pick_body(pick_ref, extra_ref, *refs):
    slots = extra_ref.shape[1]
    each = PIECES // SHARES
    rows_refs, out_refs = refs[:each], refs[each:]
    for k in range(each):
        picked = dot_nn(pick_ref[...], rows_refs[k][...]).astype(jnp.bfloat16)
        for o, out_ref in enumerate(out_refs):
            out_ref[:, k * PAIR : (k + 1) * PAIR] = picked[o * slots : (o + 1) * slots]
    for o, out_ref in enumerate(out_refs):
        out_ref[:, each * PAIR :] = extra_ref[o]


def pick_queries(pick, extra, rows):
    owners, slots, _ = extra.shape
    return call(
        pick_body,
        (jax.ShapeDtypeStruct((slots, HEADS * KVW + LANES), jnp.bfloat16),) * owners,
        16,
        2 * owners * slots * pick.shape[1] * HEADS * KVW,
        4 * owners * slots * HEADS * KVW,
    )(pick, extra, *rows)


def sums(scores, usable=None):
    if usable is not None:
        scores = [jnp.where(u, x, lowest) for u, x in zip(usable, scores)]
    peak = functools.reduce(
        jnp.maximum, [jnp.max(x, axis=-1, keepdims=True) for x in scores]
    )
    weights = [jnp.exp2(x - peak) for x in scores]
    if usable is not None:
        weights = [jnp.where(u, w, 0.0) for u, w in zip(usable, weights)]
    total = functools.reduce(jnp.add, [jnp.sum(w, axis=-1, keepdims=True) for w in weights])
    return peak, [w.astype(jnp.bfloat16) for w in weights], total


def own_body(holder_ref, root_hbm, suffix_hbm, *refs):
    rows_refs, out_hbm = refs[: HEADS // 2], refs[HEADS // 2]
    out_ref, q_ref, root_ref, suffix_ref, s_ref, root_sems, suffix_sems, out_sem = refs[
        HEADS // 2 + 1 :
    ]
    requests = rows_refs[0].shape[0]
    blocks, _, block = root_ref.shape
    groups, span, _ = suffix_ref.shape
    each = requests // groups
    root_copies = [
        pltpu.make_async_copy(
            root_hbm.at[:, pl.ds(b * block, block)], root_ref.at[b], root_sems.at[b]
        )
        for b in range(blocks)
    ]
    suffix_copies = [
        pltpu.make_async_copy(
            suffix_hbm.at[pl.ds(g * span, span)], suffix_ref.at[g], suffix_sems.at[g]
        )
        for g in range(groups)
    ]
    for copy in root_copies + suffix_copies:
        copy.start()
    for h in range(HEADS):
        k, j = divmod(h, 2)
        q_ref[h * requests : (h + 1) * requests, :] = rows_refs[k][:, j * KVW : (j + 1) * KVW]
    scale = score_scale * log2e
    for b in range(blocks):
        root_copies[b].wait()
        s_ref[b] = dot_nn(q_ref[...], root_ref[b]) * scale
    root_peak, weights, root_total = sums([s_ref[b] for b in range(blocks)])
    root_out = functools.reduce(
        jnp.add, [dot_nt(weights[b], root_ref[b, :LAT, :]) for b in range(blocks)]
    )
    for g in range(groups):
        suffix_copies[g].wait()
        mine = [slice(h * requests + g * each, h * requests + (g + 1) * each) for h in range(HEADS)]
        scores = dot_nt(
            jnp.concatenate([q_ref[at, :] for at in mine], axis=0), suffix_ref[g]
        )
        request = lax.broadcasted_iota(jnp.int32, (HEADS * each, 1), 0) % each + g * each
        usable = holder_ref[:, g * span : (g + 1) * span] == request
        peak, weights, total = sums([scores * scale], [usable])
        out = dot_nn(weights[0], suffix_ref[g, :, :LAT])
        for h, at in enumerate(mine):
            own = slice(h * each, (h + 1) * each)
            top = jnp.maximum(root_peak[at], peak[own])
            root_scale = jnp.exp2(root_peak[at] - top)
            scaled = jnp.exp2(peak[own] - top)
            both = root_total[at] * root_scale + total[own] * scaled
            out_ref[at, :LAT] = (root_out[at] * root_scale + out[own] * scaled) / both
            out_ref[at, LAT:] = jnp.broadcast_to(top * ln2 + jnp.log(both), (each, LANES))
    copy = pltpu.make_async_copy(out_ref, out_hbm, out_sem)
    copy.start()
    copy.wait()


def own_attention(rows, holder, root, suffix):
    count = HEADS * rows[0].shape[0]
    positions = root.shape[1]
    block = min(1024, positions)
    blocks, groups = positions // block, 2
    span = suffix.shape[0] // groups
    return call(
        own_body,
        pltpu.HBM((count, LAT + LANES), jnp.float32),
        44,
        2 * count * (positions + span) * (KVW + LAT),
        2 * KVW * (positions + suffix.shape[0]),
        in_specs=[VMEM, HBM, HBM] + [VMEM] * len(rows),
        out_specs=HBM,
        scratch_shapes=[
            pltpu.VMEM((count, LAT + LANES), jnp.float32),
            pltpu.VMEM((count, KVW), jnp.bfloat16),
            pltpu.VMEM((blocks, KVW, block), jnp.bfloat16),
            pltpu.VMEM((groups, span, KVW), jnp.bfloat16),
            pltpu.VMEM((blocks, count, block), jnp.float32),
            pltpu.SemaphoreType.DMA((blocks,)),
            pltpu.SemaphoreType.DMA((groups,)),
            pltpu.SemaphoreType.DMA,
        ],
    )(holder, in_hbm(root), in_hbm(suffix), *rows)


def group_body(owners, cache_hbm, holder_ref, *refs):
    rows_refs, out_refs = refs[:owners], refs[owners : 2 * owners]
    q_ref, keys_ref, sems = refs[2 * owners :]
    slots = rows_refs[0].shape[0]
    groups, _, span = cache_hbm.shape
    copies = [
        pltpu.make_async_copy(
            cache_hbm.at[g], keys_ref.at[:, pl.ds(g * span, span)], sems.at[g]
        )
        for g in range(groups)
    ]
    for copy in copies:
        copy.start()
    each = HEADS * slots
    for o in range(owners):
        for h in range(HEADS):
            at = o * each + h * slots
            q_ref[at : at + slots, :] = rows_refs[o][:, h * KVW : (h + 1) * KVW]
    lane = lax.broadcasted_iota(jnp.int32, (slots, LANES), 1)
    both = 2 * each
    blocks = 3 if groups % 3 == 0 else 1
    scores = [[] for _ in range(owners // 2)]
    for b in range(blocks):
        for copy in copies[b * groups // blocks : (b + 1) * groups // blocks]:
            copy.wait()
        at = slice(b * groups * span // blocks, (b + 1) * groups * span // blocks)
        for pair in range(owners // 2):
            scores[pair].append(
                dot_nn(q_ref[pair * both : (pair + 1) * both, :], keys_ref[:, at])
            )
    for pair in range(owners // 2):
        asked = [
            rows_refs[o][:, HEADS * KVW :][:, :1].astype(jnp.float32)
            for o in (2 * pair, 2 * pair + 1)
        ]
        asked = jnp.concatenate([asked[0]] * HEADS + [asked[1]] * HEADS, axis=0)
        usable = holder_ref[...] == asked
        block = jnp.concatenate(scores[pair], axis=1) * (score_scale * log2e)
        block = jnp.where(usable, block, lowest)
        peak = jnp.max(block, axis=-1, keepdims=True)
        weights = jnp.where(usable, jnp.exp2(block - peak), 0.0)
        total = jnp.sum(weights, axis=-1, keepdims=True)
        present = total > 0.0
        safe = jnp.where(present, total, 1.0)
        block_out = dot_nt(weights.astype(jnp.bfloat16), keys_ref[:LAT, :]) / safe
        mass = jnp.where(present, peak * ln2 + jnp.log(safe), lowest)
        for o in (2 * pair, 2 * pair + 1):
            out_ref = out_refs[o]
            extra = jnp.zeros((slots, LANES), jnp.float32)
            for h in range(HEADS):
                at = (o - 2 * pair) * each + h * slots
                at = slice(at, at + slots)
                out_ref[:, h * LAT : (h + 1) * LAT] = block_out[at].astype(jnp.bfloat16)
                for k, part in enumerate(split_three(mass[at])):
                    extra = jnp.where(lane == k * HEADS + h, part, extra)
            out_ref[:, HEADS * LAT :] = extra.astype(jnp.bfloat16)


def group_attention(rows, cache, holder):
    owners, slots = len(rows), rows[0].shape[0]
    groups, _, span = cache.shape
    out = jax.ShapeDtypeStruct((slots, HEADS * LAT + LANES), jnp.bfloat16)
    return call(
        functools.partial(group_body, owners),
        (out,) * owners,
        40,
        2 * owners * slots * HEADS * groups * span * (KVW + LAT),
        2 * KVW * groups * span,
        in_specs=[HBM, VMEM] + [VMEM] * owners,
        out_specs=(VMEM,) * owners,
        scratch_shapes=[
            pltpu.VMEM((owners * HEADS * slots, KVW), jnp.bfloat16),
            pltpu.VMEM((KVW, groups * span), jnp.bfloat16),
            pltpu.SemaphoreType.DMA((groups,)),
        ],
    )(in_hbm(cache), holder, *rows)


def mass_rows(mass):
    length = mass.shape[0]
    diagonal = lax.broadcasted_iota(jnp.int32, (length, LAT), 0) == lax.broadcasted_iota(
        jnp.int32, (length, LAT), 1
    )
    line = jnp.sum(jnp.where(diagonal, mass, 0.0), axis=0, keepdims=True)
    row = lax.broadcasted_iota(jnp.int32, (MASS_ROWS, LAT), 0)
    tail = jnp.zeros((MASS_ROWS, LAT), jnp.float32)
    for k, part in enumerate(split_three(line)):
        tail = jnp.where(row == k, part, tail)
    return tail.astype(jnp.bfloat16)


def mass_column(tail, length):
    diagonal = lax.broadcasted_iota(jnp.int32, (length, LAT), 0) == lax.broadcasted_iota(
        jnp.int32, (length, LAT), 1
    )
    tail = tail.astype(jnp.float32)
    line = tail[0:1] + tail[1:2] + tail[2:3]
    return jnp.sum(jnp.where(diagonal, line, 0.0), axis=1, keepdims=True)


def local_body(unpick_ref, *refs):
    first_hbm, refs = refs[:SHARES], refs[SHARES:]
    back_refs, refs = refs[: -PIECES - 3], refs[-PIECES - 3 :]
    out_refs, (first_ref, out_mass_ref, sems) = refs[:PIECES], refs[PIECES:]
    copies = [
        pltpu.make_async_copy(first_hbm[k], first_ref.at[k], sems.at[k]) for k in range(SHARES)
    ]
    for copy in copies:
        copy.start()
    owners = len(back_refs) // SHARES
    requests = unpick_ref.shape[0]
    unpick = unpick_ref[...]

    def returned(share, at):
        rows = [ref[:, at] for ref in back_refs[share * owners : (share + 1) * owners]]
        return dot_nn(unpick, jnp.concatenate(rows, axis=0))

    extras = [returned(share, slice(HEADS * LAT, None)) for share in range(SHARES)]
    cuts, length = out_refs[0].shape[0], out_refs[0].shape[1] - MASS_ROWS
    each = min(length, requests)
    for h in range(H):
        share, head = divmod(h, HEADS)
        if head == 0:
            copies[share].wait()
        at = slice(head * requests, (head + 1) * requests)
        group_out = returned(share, slice(head * LAT, (head + 1) * LAT))
        group_mass = functools.reduce(
            jnp.add,
            [extras[share][:, k * HEADS + head : k * HEADS + head + 1] for k in range(3)],
        )
        first_mass = first_ref[share, at, LAT : LAT + 1]
        peak = jnp.maximum(first_mass, group_mass)
        first_weight = jnp.exp(first_mass - peak)
        group_weight = jnp.exp(group_mass - peak)
        total = first_weight + group_weight
        out = (first_weight * first_ref[share, at, :LAT] + group_weight * group_out) / total
        out = out.astype(jnp.bfloat16)
        for k in range(requests // each):
            cut, row = divmod(h % 2 * requests + k * each, length)
            out_refs[h // 2][cut, row : row + each, :] = out[k * each : (k + 1) * each]
        out_mass_ref[h * requests : (h + 1) * requests, :] = peak + jnp.log(total)
    for piece in range(PIECES):
        for cut in range(cuts):
            at = piece * 2 * requests + cut * length
            out_refs[piece][cut, length:, :] = mass_rows(out_mass_ref[at : at + length, :])


def local_join(unpick, first, back, cuts):
    count = SHARES * first[0].shape[0]
    out = jax.ShapeDtypeStruct((cuts, count // PIECES // cuts + MASS_ROWS, LAT), jnp.bfloat16)
    return call(
        local_body,
        (out,) * PIECES,
        10,
        2 * unpick.shape[0] * unpick.shape[1] * H * LAT,
        4 * count * LAT,
        in_specs=[VMEM] + [HBM] * SHARES + [VMEM] * len(back),
        out_specs=(VMEM,) * PIECES,
        scratch_shapes=[
            pltpu.VMEM((SHARES,) + first[0].shape, jnp.float32),
            pltpu.VMEM((count, 1), jnp.float32),
            pltpu.SemaphoreType.DMA((SHARES,)),
        ],
    )(unpick, *[in_hbm(x) for x in first], *back)


def join_body(further, *refs):
    parts_refs, out_ref = refs[:-1], refs[-1]
    length = parts_refs[0].shape[0] - MASS_ROWS
    masses = [mass_column(ref[length:, :], length) for ref in parts_refs]
    peak = functools.reduce(jnp.maximum, masses)
    scales = [jnp.exp(mass - peak) for mass in masses]
    total = functools.reduce(jnp.add, scales)
    out = functools.reduce(
        jnp.add,
        [scale * ref[:length, :].astype(jnp.float32) for scale, ref in zip(scales, parts_refs)],
    )
    out = (out / total).astype(jnp.bfloat16)
    if further:
        out_ref[:length, :] = out
        out_ref[length:, :] = mass_rows(peak + jnp.log(total))
    else:
        for c in range(out_ref.shape[0]):
            out_ref[c] = out


def join(parts, copies=0):
    rows = parts[0].shape[0]
    shape = (copies, rows - MASS_ROWS, LAT) if copies else (rows, LAT)
    return call(
        functools.partial(join_body, not copies),
        jax.ShapeDtypeStruct(shape, jnp.bfloat16),
        6,
        2 * len(parts) * rows * LAT,
        4 * len(parts) * rows * LAT,
        in_specs=[VMEM] * len(parts),
        out_specs=VMEM,
    )(*parts)


def output_body(share, base_ref, weight_hbm, start_ref, *refs):
    count = PIECES // SHARES
    rows_refs, out_refs = refs[:count], refs[count:-2]
    weight_ref, sems = refs[-2:]
    requests, _ = start_ref.shape
    width = weight_ref.shape[2]
    copies = []
    for k in range(count):
        piece = share * count + k ^ base_ref[0]
        copy = pltpu.make_async_copy(
            weight_hbm.at[:, pl.ds(pl.multiple_of(piece * width, width), width)],
            weight_ref.at[k],
            sems.at[k],
        )
        copy.start()
        copies.append(copy)
    total = start_ref[...].astype(jnp.float32)
    for k in range(count):
        copies[k].wait()
        for j in range(2):
            total = total + dot_nt(
                rows_refs[k][j * requests : (j + 1) * requests, :],
                weight_ref[k, :, j * LAT : (j + 1) * LAT],
            )
    if share < SHARES - 1:
        out_refs[0][...] = total
    else:
        out = total.astype(jnp.bfloat16)
        out_refs[0][...] = out
        for c in range(out_refs[1].shape[0]):
            out_refs[1][c] = out


def output_projection(share, base, rows, weight, start, copies):
    features, width = weight.shape
    last = share == SHARES - 1
    if last:
        out = (
            jax.ShapeDtypeStruct(start.shape, jnp.bfloat16),
            jax.ShapeDtypeStruct((copies,) + start.shape, jnp.bfloat16),
        )
    else:
        out = jax.ShapeDtypeStruct(start.shape, jnp.float32)
    return call(
        functools.partial(output_body, share),
        out,
        8,
        3e10 if last else 2 * start.shape[0] * features * width // SHARES,
        2 * features * width // SHARES,
        in_specs=[pl.BlockSpec(memory_space=pltpu.SMEM), HBM, VMEM] + [VMEM] * len(rows),
        out_specs=(VMEM, VMEM) if last else VMEM,
        scratch_shapes=[
            pltpu.VMEM((len(rows), features, width // PIECES), jnp.bfloat16),
            pltpu.SemaphoreType.DMA((len(rows),)),
        ],
    )(base[None], in_hbm(weight), start, *rows)


def gated(rows, gate, up):
    gate_part = dot_nt(rows, gate)
    up_part = dot_nt(rows, up)
    return (gate_part / (1.0 + jnp.exp(-gate_part)) * up_part).astype(jnp.bfloat16)


def expert_body(pick_ref, rows_ref, gain_ref, shared_gate_ref, shared_up_ref, shared_down_ref, gate_ref, up_ref, down_ref, out_ref):
    owners, _, requests, part = rows_ref.shape
    width = gain_ref.shape[1]
    share = requests // owners
    slots = out_ref.shape[2] - share
    rows = jnp.concatenate(
        [
            normalised(lambda k, o=o: rows_ref[o, k], gain_ref[...], width)
            for o in range(owners)
        ],
        axis=0,
    )
    rows = dot_nn(pick_ref[...], rows).astype(jnp.bfloat16)
    named, rest = rows[: owners * slots], rows[owners * slots :]
    shared = dot_nn(gated(rest, shared_gate_ref[...], shared_up_ref[...]), shared_down_ref[...])
    units = gate_ref.shape[1]
    steps = 4 if units % 64 == 0 and units > 704 else 1
    each = units // steps
    total = jnp.zeros((owners * slots, width), jnp.float32)
    for c in range(steps):
        at = slice(c * each, (c + 1) * each)
        total = total + dot_nn(
            gated(named, gate_ref[0, at, :], up_ref[0, at, :]), down_ref[0, at, :]
        )
    for o in range(owners):
        both = jnp.concatenate(
            [total[o * slots : (o + 1) * slots], shared[o * share : (o + 1) * share]], axis=0
        ).astype(jnp.bfloat16)
        for k in range(PIECES):
            out_ref[o, k] = both[:, k * part : (k + 1) * part]


def expert(pick, rows, gain, slots, shared, weights):
    owners, _, requests, part = rows.shape
    _, units, width = weights[0].shape
    return call(
        expert_body,
        jax.ShapeDtypeStruct(
            (owners, PIECES, slots + requests // owners, part), jnp.bfloat16
        ),
        12,
        6 * pick.shape[0] * units * width,
        6 * units * width,
        in_specs=[VMEM] * 9,
        out_specs=VMEM,
    )(pick, rows, gain, *shared, *weights)


def final_body(parts_ref, weight_ref, mid_ref, out_ref):
    weight = weight_ref[...]
    high = weight.astype(jnp.bfloat16)
    rest = weight - high.astype(jnp.float32)
    low = rest.astype(jnp.bfloat16)
    lower = (rest - low.astype(jnp.float32)).astype(jnp.bfloat16)
    parts = parts_ref[...]
    total = dot_nn(high, parts) + (dot_nn(low, parts) + dot_nn(lower, parts))
    out_ref[...] = (mid_ref[...].astype(jnp.float32) + total).astype(jnp.bfloat16)


def final_sum(parts, weight, mid):
    return call(
        final_body,
        jax.ShapeDtypeStruct(mid.shape, jnp.bfloat16),
        16,
        2 * weight.shape[0] * parts.shape[0] * parts.shape[1],
        2 * parts.shape[0] * parts.shape[1],
    )(parts, weight, mid)


def exchange(x, axis):
    return lax.all_to_all(x, axis, 0, 0, tiled=True)


def turn(x, k):
    count = lax.axis_size("tensor")
    return lax.ppermute(x, "tensor", [(i, i ^ k) for i in range(count)])


def gather_by_turns(x):
    near = [x] + [turn(x, k) for k in (1, 2, 3)]
    crossed = turn(x, 4)
    return near + [crossed] + [turn(crossed, k) for k in (1, 2, 3)]


def swap_owners(arrays):
    count = len(arrays)
    out = {0: arrays[0]}
    for k in reversed(range(1, count)):
        out[k] = lax.ppermute(arrays[k], OWNER, [(i, i ^ k) for i in range(count)])
    return [out[k] for k in range(count)]


def gather_pieces(x):
    devices = x.shape[-3]
    each = devices // PIECES
    if each == 1:
        return x
    lead, (rows, columns) = x.shape[:-3], x.shape[-2:]
    x = x.reshape(lead + (PIECES, each, rows, columns))
    return jnp.swapaxes(x, -3, -2).reshape(lead + (PIECES, rows, each * columns))


def scatter_pieces(x, devices):
    each = devices // PIECES
    if each == 1:
        return x
    lead, (rows, columns) = x.shape[:-3], x.shape[-2:]
    x = x.reshape(lead + (PIECES, rows, each, columns // each))
    return jnp.swapaxes(x, -3, -2).reshape(lead + (devices, rows, columns // each))


def ranks(hits):
    count = hits.shape[0]
    ahead = jnp.arange(count)[:, None] > jnp.arange(count)[None, :]
    return jnp.sum(jnp.where(ahead[:, :, None], hits.astype(jnp.int32)[None], 0), axis=1)


def local(
    hidden,
    attention_gain,
    query_weight,
    out_weight,
    root_cache,
    group_cache,
    group_length,
    suffix_cache,
    suffix_length,
    group_of,
    mixture_gain,
    routes,
    route_weight,
    expert_gate,
    expert_up,
    expert_down,
    shared_gate,
    shared_up,
    shared_down,
):
    owners, tensors = lax.axis_size(OWNER), lax.axis_size("tensor")
    owner_index, tensor_index = lax.axis_index(OWNER), lax.axis_index("tensor")
    requests = hidden.shape[0]
    fanout = routes.shape[1]
    token_share = requests // owners
    pairs = owners // 2
    split = tensors // EXP_OWN
    slots = -(-2 * requests // (owners * 16)) * 16
    expert_slots = -(-2 * requests * fanout // (EXP_OWN * owners * 16)) * 16

    if group_cache.shape[1] % LANES:
        group_columns = group_cache.reshape(-1, KVW).T[None]
    else:
        group_columns = jnp.swapaxes(group_cache, 1, 2)
    by_turns = tensors == PIECES
    base = tensor_index if by_turns else jnp.zeros((), jnp.int32)
    if by_turns:
        rows = gather_by_turns(hidden)
    else:
        copies = jnp.broadcast_to(hidden[None], (tensors,) + hidden.shape)
        rows = gather_pieces(exchange(copies, "tensor"))
        rows = [rows[k] for k in range(PIECES)]

    projected = project(base, rows, attention_gain[None], query_weight)
    projected, group_of, group_length, suffix_length, routes, route_weight = (
        lax.optimization_barrier(
            (projected, group_of, group_length, suffix_length, routes, route_weight)
        )
    )
    destination = group_of // GROUP_OWN
    owner_range = jnp.arange(owners)
    to_owner = (destination ^ owner_index)[:, None] == owner_range[None, :]
    slot_rank = ranks(to_owner)
    placed = to_owner[:, :, None] & (slot_rank[:, :, None] == jnp.arange(slots))
    unpick = placed.reshape(requests, owners * slots).astype(jnp.bfloat16)
    pick = unpick.T
    asked = jnp.sum(
        jnp.where(placed, (group_of % GROUP_OWN + 1)[:, None, None], 0), axis=0
    ).astype(jnp.bfloat16)
    named = routes.astype(jnp.bfloat16).reshape(slots, requests * fanout // slots)
    extra = jnp.where(
        jnp.arange(LANES) == 0,
        asked[:, :, None],
        jnp.pad(named, ((0, 0), (1, LANES - 1 - named.shape[1])))[None],
    )
    suffix_span, group_span = suffix_cache.shape[1], group_cache.shape[1]
    suffix_usable = (
        tensor_index * suffix_span + jnp.arange(suffix_span)[None, :] < suffix_length[:, None]
    )
    suffix_holder = jnp.where(suffix_usable, jnp.arange(requests)[:, None], -1).reshape(1, -1)
    group_usable = (
        tensor_index * group_span + jnp.arange(group_span)[None, :] < group_length[:, None]
    )
    group_holder = (
        jnp.where(group_usable, jnp.arange(1, GROUP_OWN + 1)[:, None], -1)
        .reshape(1, -1)
        .astype(jnp.float32)
    )
    if by_turns:
        pieces = gather_by_turns(projected)
    else:
        copies = jnp.broadcast_to(projected[None], (tensors,) + projected.shape)
        queries = gather_pieces(exchange(copies, "tensor"))
        pieces = [queries[k] for k in range(PIECES)]
    near, far = pieces[: PIECES // 2], pieces[PIECES // 2 :]
    arrived = [swap_owners(pick_queries(pick, extra, near))]
    all_routes = jnp.stack(
        [x[:, HEADS * KVW + 1 : HEADS * KVW + 1 + named.shape[1]] for x in arrived[0]]
    ).reshape(1, owners, requests, fanout)
    turned = owner_range[:, None] ^ owner_index == owner_range[None, :]
    all_routes = jnp.sum(
        jnp.where(turned[:, :, None, None], all_routes.astype(jnp.int32), 0), axis=1
    )
    mine = owner_index * EXP_OWN + tensor_index // split
    called = jnp.any(all_routes == mine, axis=2)
    call_rank = ranks(called.T).T
    expert_pick = called[:, None, :] & (
        call_rank[:, None, :] == jnp.arange(expert_slots)[None, :, None]
    )
    seen = owner_range.reshape(2, pairs)
    seen = 2 * (seen % pairs) + seen // pairs
    expert_pick = jnp.where(
        (owner_range[:, None] == seen.reshape(-1)[None, :])[:, None, :, None],
        expert_pick[:, :, None, :],
        False,
    )
    shared_pick = (
        owner_range[:, None, None] * requests
        + owner_index * token_share
        + jnp.arange(token_share)[None, :, None]
    ).reshape(-1, 1) == (seen.reshape(-1, 1) * requests + jnp.arange(requests)).reshape(1, -1)
    expert_pick = jnp.concatenate(
        [expert_pick.reshape(owners * expert_slots, owners * requests), shared_pick], axis=0
    ).astype(jnp.bfloat16)
    root_columns, suffix_rows = root_cache.T, suffix_cache.reshape(-1, KVW)
    near, far[0] = lax.optimization_barrier((near, far[0]))
    first = [own_attention(near, suffix_holder, root_columns, suffix_rows)]
    far, first = lax.optimization_barrier((far, first))
    sent = pick_queries(pick, extra, far)
    arrived[0], sent = lax.optimization_barrier((arrived[0], sent))
    arrived.append(swap_owners(sent))
    back = []
    for share in arrived:
        if back:
            share, answered = lax.optimization_barrier((share, answered))
            back[0] = swap_owners(answered)
        answered = group_attention(share, group_columns, group_holder)
        back.append(swap_owners(answered))
    far, answered, expert_pick = lax.optimization_barrier((far, answered, expert_pick))
    back[1] = swap_owners(answered)
    first.append(own_attention(far, suffix_holder, root_columns, suffix_rows))
    back, gain = lax.optimization_barrier((back, mixture_gain[None]))
    parts = local_join(unpick, first, sum(back, []), tensors // PIECES)
    if by_turns:
        parts = [part[0] for part in parts]
        crossing = join([parts[4]] + [turn(parts[4 + k], k) for k in (1, 2, 3)])
        parts = [parts[0]] + [turn(parts[k], k) for k in (1, 2, 3)] + [turn(crossing, 4)]
    else:
        parts = exchange(jnp.concatenate(parts, axis=0), "tensor")
        parts = [parts[k] for k in range(tensors)]
    if by_turns:
        attention = gather_by_turns(join(parts, 1)[0])
    else:
        attention = exchange(join(parts, tensors), "tensor").reshape(PIECES, -1, LAT)
        attention = [attention[k] for k in range(PIECES)]
    half = PIECES // SHARES
    total = output_projection(0, base, attention[:half], out_weight, hidden, 0)
    rest, total = lax.optimization_barrier((attention[half:], total))
    mid, copies = output_projection(1, base, rest, out_weight, total, pairs * tensors)

    half = exchange(copies, ("pair", "tensor"))
    both = lax.all_gather(half.reshape((pairs, tensors) + mid.shape), "core")
    everything = gather_pieces(both.reshape((owners, tensors) + mid.shape))
    results = expert(
        expert_pick,
        everything,
        gain,
        expert_slots,
        (shared_gate, shared_up, shared_down),
        (expert_gate, expert_up, expert_down),
    )
    results, routes, route_weight = lax.optimization_barrier((results, routes, route_weight))
    results = scatter_pieces(results, tensors).reshape((owners * tensors, -1, mid.shape[1]))
    returned = exchange(results, ("pair", "core", "tensor"))
    experts = jnp.arange(owners * EXP_OWN)
    hits = routes[:, :, None] == experts[None, None, :]
    share = jnp.sum(jnp.where(hits, route_weight[:, :, None], 0.0), axis=1)
    hit = jnp.any(hits, axis=1)
    taken = hit[:, :, None] & (ranks(hit)[:, :, None] == jnp.arange(expert_slots))
    back_weight = jnp.where(taken, share[:, :, None], 0.0)
    back_weight = jnp.repeat(back_weight, split, axis=1)
    shared_weight = np.eye(requests, dtype=np.float32).reshape(requests, owners, 1, token_share)
    shared_weight = np.repeat(shared_weight, tensors, axis=2).reshape(
        requests, owners * tensors, token_share
    )
    back_weight = jnp.concatenate([back_weight, shared_weight], axis=2).reshape(requests, -1)
    return final_sum(returned.reshape(-1, mid.shape[1]), back_weight, mid)


def solution(mesh):
    owners, tensors = mesh.shape["owner"], mesh.shape["tensor"]
    devices = mesh.devices.reshape(owners // 2, 2, tensors)
    return jax.shard_map(
        local,
        mesh=Mesh(devices, OWNER + ("tensor",)),
        in_specs=(
            P(OWNER, "tensor"),
            P(),
            P("tensor", None),
            P("tensor", None),
            P("tensor", None),
            P(OWNER, "tensor", None),
            P(OWNER),
            P(OWNER, "tensor", None),
            P(OWNER),
            P(OWNER),
            P(),
            P(OWNER, None),
            P(OWNER, None),
            P(OWNER + ("tensor",), None, None),
            P(OWNER + ("tensor",), None, None),
            P(OWNER + ("tensor",), None, None),
            P("tensor", None),
            P("tensor", None),
            P("tensor", None),
        ),
        out_specs=P(OWNER, "tensor"),
        check_vma=False,
    )
```

```python
import functools

import jax
import jax.numpy as jnp
import numpy as np
from jax import lax
from jax.experimental import pallas as pl
from jax.experimental.pallas import tpu as pltpu
from jax.sharding import Mesh
from jax.sharding import PartitionSpec as P

H = 16
LAT = 512
KVW = 576
EXP_OWN = 8
GROUP_OWN = 12
PIECES = 8
PAIR = 2 * KVW
LANES = 128
OWNER = ("pair", "core")
SHARES = 2
HEADS = H // SHARES
MASS_ROWS = 8
MIB = 1 << 20

score_scale = 192.0 ** (-0.5)
log2e = 1.4426950408889634
ln2 = 0.6931471805599453
lowest = -1e30
epsilon = 1e-06

NT = (((1,), (1,)), ((), ()))


def dot_nt(a, b):
    return lax.dot_general(a, b, NT, preferred_element_type=jnp.float32)


def dot_nn(a, b):
    return jnp.dot(a, b, preferred_element_type=jnp.float32)


def call(body, out_shape, vmem_mib, flops, nbytes, **options):
    return pl.pallas_call(
        body,
        out_shape=out_shape,
        compiler_params=pltpu.CompilerParams(vmem_limit_bytes=vmem_mib * MIB),
        cost_estimate=pl.CostEstimate(
            flops=int(flops), bytes_accessed=int(nbytes), transcendentals=0
        ),
        **options,
    )


VMEM = pl.BlockSpec(memory_space=pltpu.VMEM)
HBM = pl.BlockSpec(memory_space=pltpu.HBM)


def in_hbm(x):
    return pltpu.with_memory_space_constraint(x, pltpu.HBM)


def whole(shape):
    return pl.BlockSpec(shape, lambda *_: (0,) * len(shape))


def split_three(column):
    first = column.astype(jnp.bfloat16).astype(jnp.float32)
    second = (column - first).astype(jnp.bfloat16).astype(jnp.float32)
    third = (column - first - second).astype(jnp.bfloat16).astype(jnp.float32)
    return first, second, third


def normalised(read_piece, gain, width):
    rows = jnp.concatenate([read_piece(k) for k in range(PIECES)], axis=-1).astype(jnp.float32)
    square = jnp.sum(rows * rows, axis=-1, keepdims=True) * (1.0 / width)
    return (rows * lax.rsqrt(square + epsilon) * gain.astype(jnp.float32)).astype(jnp.bfloat16)


def project_body(base_ref, gain_ref, weight_hbm, *refs):
    rows_refs, (out_ref, rows_ref, weight_ref, sems) = refs[:PIECES], refs[PIECES:]
    steps, each, width = weight_ref.shape
    copies = [
        pltpu.make_async_copy(
            weight_hbm.at[pl.ds(c * each, each)], weight_ref.at[c], sems.at[c]
        )
        for c in range(steps)
    ]
    for copy in copies:
        copy.start()
    part = width // PIECES
    for k in range(PIECES):
        at = pl.multiple_of((k ^ base_ref[0]) * part, part)
        rows_ref[:, pl.ds(at, part)] = rows_refs[k][...]
    normed = normalised(
        lambda k: rows_ref[:, k * part : (k + 1) * part], gain_ref[...], width
    )
    for step in range(steps):
        copies[step].wait()
        out = dot_nt(normed, weight_ref[step]).astype(jnp.bfloat16)
        out_ref[:, step * each : (step + 1) * each] = out


def project(base, rows, gain, weight):
    requests, _ = rows[0].shape
    columns, width = weight.shape
    steps = 3 if columns % (3 * LANES) == 0 else 1
    return call(
        project_body,
        jax.ShapeDtypeStruct((requests, columns), jnp.bfloat16),
        16,
        2 * requests * columns * width,
        2 * columns * width,
        in_specs=[pl.BlockSpec(memory_space=pltpu.SMEM), VMEM, HBM] + [VMEM] * PIECES,
        out_specs=VMEM,
        scratch_shapes=[
            pltpu.VMEM((requests, width), jnp.bfloat16),
            pltpu.VMEM((steps, columns // steps, width), jnp.bfloat16),
            pltpu.SemaphoreType.DMA((steps,)),
        ],
    )(base[None], gain, in_hbm(weight), *rows)


def pick_body(pick_ref, extra_ref, *refs):
    slots = extra_ref.shape[1]
    each = PIECES // SHARES
    rows_refs, out_refs = refs[:each], refs[each:]
    for k in range(each):
        picked = dot_nn(pick_ref[...], rows_refs[k][...]).astype(jnp.bfloat16)
        for o, out_ref in enumerate(out_refs):
            out_ref[:, k * PAIR : (k + 1) * PAIR] = picked[o * slots : (o + 1) * slots]
    for o, out_ref in enumerate(out_refs):
        out_ref[:, each * PAIR :] = extra_ref[o]


def pick_queries(pick, extra, rows):
    owners, slots, _ = extra.shape
    return call(
        pick_body,
        (jax.ShapeDtypeStruct((slots, HEADS * KVW + LANES), jnp.bfloat16),) * owners,
        16,
        2 * owners * slots * pick.shape[1] * HEADS * KVW,
        4 * owners * slots * HEADS * KVW,
    )(pick, extra, *rows)


def sums(scores, usable=None):
    if usable is not None:
        scores = [jnp.where(u, x, lowest) for u, x in zip(usable, scores)]
    peak = functools.reduce(
        jnp.maximum, [jnp.max(x, axis=-1, keepdims=True) for x in scores]
    )
    weights = [jnp.exp2(x - peak) for x in scores]
    if usable is not None:
        weights = [jnp.where(u, w, 0.0) for u, w in zip(usable, weights)]
    total = functools.reduce(jnp.add, [jnp.sum(w, axis=-1, keepdims=True) for w in weights])
    return peak, [w.astype(jnp.bfloat16) for w in weights], total


def own_body(holder_ref, root_hbm, suffix_hbm, *refs):
    rows_refs, out_hbm = refs[: HEADS // 2], refs[HEADS // 2]
    out_ref, q_ref, root_ref, suffix_ref, s_ref, root_sems, suffix_sems, out_sem = refs[
        HEADS // 2 + 1 :
    ]
    requests = rows_refs[0].shape[0]
    blocks, _, block = root_ref.shape
    groups, span, _ = suffix_ref.shape
    each = requests // groups
    root_copies = [
        pltpu.make_async_copy(
            root_hbm.at[:, pl.ds(b * block, block)], root_ref.at[b], root_sems.at[b]
        )
        for b in range(blocks)
    ]
    suffix_copies = [
        pltpu.make_async_copy(
            suffix_hbm.at[pl.ds(g * span, span)], suffix_ref.at[g], suffix_sems.at[g]
        )
        for g in range(groups)
    ]
    for copy in root_copies + suffix_copies:
        copy.start()
    for h in range(HEADS):
        k, j = divmod(h, 2)
        q_ref[h * requests : (h + 1) * requests, :] = rows_refs[k][:, j * KVW : (j + 1) * KVW]
    scale = score_scale * log2e
    for b in range(blocks):
        root_copies[b].wait()
        s_ref[b] = dot_nn(q_ref[...], root_ref[b]) * scale
    root_peak, weights, root_total = sums([s_ref[b] for b in range(blocks)])
    root_out = functools.reduce(
        jnp.add, [dot_nt(weights[b], root_ref[b, :LAT, :]) for b in range(blocks)]
    )
    for g in range(groups):
        suffix_copies[g].wait()
        mine = [slice(h * requests + g * each, h * requests + (g + 1) * each) for h in range(HEADS)]
        scores = dot_nt(
            jnp.concatenate([q_ref[at, :] for at in mine], axis=0), suffix_ref[g]
        )
        request = lax.broadcasted_iota(jnp.int32, (HEADS * each, 1), 0) % each + g * each
        usable = holder_ref[:, g * span : (g + 1) * span] == request
        peak, weights, total = sums([scores * scale], [usable])
        out = dot_nn(weights[0], suffix_ref[g, :, :LAT])
        for h, at in enumerate(mine):
            own = slice(h * each, (h + 1) * each)
            top = jnp.maximum(root_peak[at], peak[own])
            root_scale = jnp.exp2(root_peak[at] - top)
            scaled = jnp.exp2(peak[own] - top)
            both = root_total[at] * root_scale + total[own] * scaled
            out_ref[at, :LAT] = (root_out[at] * root_scale + out[own] * scaled) / both
            out_ref[at, LAT:] = jnp.broadcast_to(top * ln2 + jnp.log(both), (each, LANES))
    copy = pltpu.make_async_copy(out_ref, out_hbm, out_sem)
    copy.start()
    copy.wait()


def own_attention(rows, holder, root, suffix):
    count = HEADS * rows[0].shape[0]
    positions = root.shape[1]
    block = min(1024, positions)
    blocks, groups = positions // block, 2
    span = suffix.shape[0] // groups
    return call(
        own_body,
        pltpu.HBM((count, LAT + LANES), jnp.float32),
        44,
        2 * count * (positions + span) * (KVW + LAT),
        2 * KVW * (positions + suffix.shape[0]),
        in_specs=[VMEM, HBM, HBM] + [VMEM] * len(rows),
        out_specs=HBM,
        scratch_shapes=[
            pltpu.VMEM((count, LAT + LANES), jnp.float32),
            pltpu.VMEM((count, KVW), jnp.bfloat16),
            pltpu.VMEM((blocks, KVW, block), jnp.bfloat16),
            pltpu.VMEM((groups, span, KVW), jnp.bfloat16),
            pltpu.VMEM((blocks, count, block), jnp.float32),
            pltpu.SemaphoreType.DMA((blocks,)),
            pltpu.SemaphoreType.DMA((groups,)),
            pltpu.SemaphoreType.DMA,
        ],
    )(holder, in_hbm(root), in_hbm(suffix), *rows)


def group_body(owners, cache_hbm, holder_ref, *refs):
    rows_refs, out_refs = refs[:owners], refs[owners : 2 * owners]
    q_ref, keys_ref, sems = refs[2 * owners :]
    slots = rows_refs[0].shape[0]
    groups, _, span = cache_hbm.shape
    copies = [
        pltpu.make_async_copy(
            cache_hbm.at[g], keys_ref.at[:, pl.ds(g * span, span)], sems.at[g]
        )
        for g in range(groups)
    ]
    for copy in copies:
        copy.start()
    each = HEADS * slots
    for o in range(owners):
        for h in range(HEADS):
            at = o * each + h * slots
            q_ref[at : at + slots, :] = rows_refs[o][:, h * KVW : (h + 1) * KVW]
    lane = lax.broadcasted_iota(jnp.int32, (slots, LANES), 1)
    both = 2 * each
    blocks = 3 if groups % 3 == 0 else 1
    scores = [[] for _ in range(owners // 2)]
    for b in range(blocks):
        for copy in copies[b * groups // blocks : (b + 1) * groups // blocks]:
            copy.wait()
        at = slice(b * groups * span // blocks, (b + 1) * groups * span // blocks)
        for pair in range(owners // 2):
            scores[pair].append(
                dot_nn(q_ref[pair * both : (pair + 1) * both, :], keys_ref[:, at])
            )
    for pair in range(owners // 2):
        asked = [
            rows_refs[o][:, HEADS * KVW :][:, :1].astype(jnp.float32)
            for o in (2 * pair, 2 * pair + 1)
        ]
        asked = jnp.concatenate([asked[0]] * HEADS + [asked[1]] * HEADS, axis=0)
        usable = holder_ref[...] == asked
        block = jnp.concatenate(scores[pair], axis=1) * (score_scale * log2e)
        block = jnp.where(usable, block, lowest)
        peak = jnp.max(block, axis=-1, keepdims=True)
        weights = jnp.where(usable, jnp.exp2(block - peak), 0.0)
        total = jnp.sum(weights, axis=-1, keepdims=True)
        present = total > 0.0
        safe = jnp.where(present, total, 1.0)
        block_out = dot_nt(weights.astype(jnp.bfloat16), keys_ref[:LAT, :]) / safe
        mass = jnp.where(present, peak * ln2 + jnp.log(safe), lowest)
        for o in (2 * pair, 2 * pair + 1):
            out_ref = out_refs[o]
            extra = jnp.zeros((slots, LANES), jnp.float32)
            for h in range(HEADS):
                at = (o - 2 * pair) * each + h * slots
                at = slice(at, at + slots)
                out_ref[:, h * LAT : (h + 1) * LAT] = block_out[at].astype(jnp.bfloat16)
                for k, part in enumerate(split_three(mass[at])):
                    extra = jnp.where(lane == k * HEADS + h, part, extra)
            out_ref[:, HEADS * LAT :] = extra.astype(jnp.bfloat16)


def group_attention(rows, cache, holder):
    owners, slots = len(rows), rows[0].shape[0]
    groups, _, span = cache.shape
    out = jax.ShapeDtypeStruct((slots, HEADS * LAT + LANES), jnp.bfloat16)
    return call(
        functools.partial(group_body, owners),
        (out,) * owners,
        40,
        2 * owners * slots * HEADS * groups * span * (KVW + LAT),
        2 * KVW * groups * span,
        in_specs=[HBM, VMEM] + [VMEM] * owners,
        out_specs=(VMEM,) * owners,
        scratch_shapes=[
            pltpu.VMEM((owners * HEADS * slots, KVW), jnp.bfloat16),
            pltpu.VMEM((KVW, groups * span), jnp.bfloat16),
            pltpu.SemaphoreType.DMA((groups,)),
        ],
    )(in_hbm(cache), holder, *rows)


def mass_rows(mass):
    length = mass.shape[0]
    diagonal = lax.broadcasted_iota(jnp.int32, (length, LAT), 0) == lax.broadcasted_iota(
        jnp.int32, (length, LAT), 1
    )
    line = jnp.sum(jnp.where(diagonal, mass, 0.0), axis=0, keepdims=True)
    row = lax.broadcasted_iota(jnp.int32, (MASS_ROWS, LAT), 0)
    tail = jnp.zeros((MASS_ROWS, LAT), jnp.float32)
    for k, part in enumerate(split_three(line)):
        tail = jnp.where(row == k, part, tail)
    return tail.astype(jnp.bfloat16)


def mass_column(tail, length):
    diagonal = lax.broadcasted_iota(jnp.int32, (length, LAT), 0) == lax.broadcasted_iota(
        jnp.int32, (length, LAT), 1
    )
    tail = tail.astype(jnp.float32)
    line = tail[0:1] + tail[1:2] + tail[2:3]
    return jnp.sum(jnp.where(diagonal, line, 0.0), axis=1, keepdims=True)


def local_body(unpick_ref, *refs):
    first_hbm, refs = refs[:SHARES], refs[SHARES:]
    back_refs, refs = refs[: -PIECES - 3], refs[-PIECES - 3 :]
    out_refs, (first_ref, out_mass_ref, sems) = refs[:PIECES], refs[PIECES:]
    copies = [
        pltpu.make_async_copy(first_hbm[k], first_ref.at[k], sems.at[k]) for k in range(SHARES)
    ]
    for copy in copies:
        copy.start()
    owners = len(back_refs) // SHARES
    requests = unpick_ref.shape[0]
    unpick = unpick_ref[...]

    def returned(share, at):
        rows = [ref[:, at] for ref in back_refs[share * owners : (share + 1) * owners]]
        return dot_nn(unpick, jnp.concatenate(rows, axis=0))

    extras = [returned(share, slice(HEADS * LAT, None)) for share in range(SHARES)]
    cuts, length = out_refs[0].shape[0], out_refs[0].shape[1] - MASS_ROWS
    each = min(length, requests)
    for h in range(H):
        share, head = divmod(h, HEADS)
        if head == 0:
            copies[share].wait()
        at = slice(head * requests, (head + 1) * requests)
        group_out = returned(share, slice(head * LAT, (head + 1) * LAT))
        group_mass = functools.reduce(
            jnp.add,
            [extras[share][:, k * HEADS + head : k * HEADS + head + 1] for k in range(3)],
        )
        first_mass = first_ref[share, at, LAT : LAT + 1]
        peak = jnp.maximum(first_mass, group_mass)
        first_weight = jnp.exp(first_mass - peak)
        group_weight = jnp.exp(group_mass - peak)
        total = first_weight + group_weight
        out = (first_weight * first_ref[share, at, :LAT] + group_weight * group_out) / total
        out = out.astype(jnp.bfloat16)
        for k in range(requests // each):
            cut, row = divmod(h % 2 * requests + k * each, length)
            out_refs[h // 2][cut, row : row + each, :] = out[k * each : (k + 1) * each]
        out_mass_ref[h * requests : (h + 1) * requests, :] = peak + jnp.log(total)
    for piece in range(PIECES):
        for cut in range(cuts):
            at = piece * 2 * requests + cut * length
            out_refs[piece][cut, length:, :] = mass_rows(out_mass_ref[at : at + length, :])


def local_join(unpick, first, back, cuts):
    count = SHARES * first[0].shape[0]
    out = jax.ShapeDtypeStruct((cuts, count // PIECES // cuts + MASS_ROWS, LAT), jnp.bfloat16)
    return call(
        local_body,
        (out,) * PIECES,
        10,
        2 * unpick.shape[0] * unpick.shape[1] * H * LAT,
        4 * count * LAT,
        in_specs=[VMEM] + [HBM] * SHARES + [VMEM] * len(back),
        out_specs=(VMEM,) * PIECES,
        scratch_shapes=[
            pltpu.VMEM((SHARES,) + first[0].shape, jnp.float32),
            pltpu.VMEM((count, 1), jnp.float32),
            pltpu.SemaphoreType.DMA((SHARES,)),
        ],
    )(unpick, *[in_hbm(x) for x in first], *back)


def join_body(further, *refs):
    parts_refs, out_ref = refs[:-1], refs[-1]
    length = parts_refs[0].shape[0] - MASS_ROWS
    masses = [mass_column(ref[length:, :], length) for ref in parts_refs]
    peak = functools.reduce(jnp.maximum, masses)
    scales = [jnp.exp(mass - peak) for mass in masses]
    total = functools.reduce(jnp.add, scales)
    out = functools.reduce(
        jnp.add,
        [scale * ref[:length, :].astype(jnp.float32) for scale, ref in zip(scales, parts_refs)],
    )
    out = (out / total).astype(jnp.bfloat16)
    if further:
        out_ref[:length, :] = out
        out_ref[length:, :] = mass_rows(peak + jnp.log(total))
    else:
        for c in range(out_ref.shape[0]):
            out_ref[c] = out


def join(parts, copies=0):
    rows = parts[0].shape[0]
    shape = (copies, rows - MASS_ROWS, LAT) if copies else (rows, LAT)
    return call(
        functools.partial(join_body, not copies),
        jax.ShapeDtypeStruct(shape, jnp.bfloat16),
        6,
        2 * len(parts) * rows * LAT,
        4 * len(parts) * rows * LAT,
        in_specs=[VMEM] * len(parts),
        out_specs=VMEM,
    )(*parts)


def output_body(first, count, base_ref, weight_hbm, start_ref, *refs):
    rows_refs, out_refs = refs[:count], refs[count:-2]
    weight_ref, sems = refs[-2:]
    requests, _ = start_ref.shape
    width = weight_ref.shape[2]
    copies = []
    for k in range(count):
        piece = (first + k) ^ base_ref[0]
        copy = pltpu.make_async_copy(
            weight_hbm.at[:, pl.ds(pl.multiple_of(piece * width, width), width)],
            weight_ref.at[k],
            sems.at[k],
        )
        copy.start()
        copies.append(copy)
    total = start_ref[...].astype(jnp.float32)
    for k in range(count):
        copies[k].wait()
        for j in range(2):
            total = total + dot_nt(
                rows_refs[k][j * requests : (j + 1) * requests, :],
                weight_ref[k, :, j * LAT : (j + 1) * LAT],
            )
    if first + count < PIECES:
        out_refs[0][...] = total
    else:
        out = total.astype(jnp.bfloat16)
        out_refs[0][...] = out
        for c in range(out_refs[1].shape[0]):
            out_refs[1][c] = out


def output_projection(first, base, rows, weight, start, copies):
    features, width = weight.shape
    last = first + len(rows) == PIECES
    if last:
        out = (
            jax.ShapeDtypeStruct(start.shape, jnp.bfloat16),
            jax.ShapeDtypeStruct((copies,) + start.shape, jnp.bfloat16),
        )
    else:
        out = jax.ShapeDtypeStruct(start.shape, jnp.float32)
    return call(
        functools.partial(output_body, first, len(rows)),
        out,
        8,
        3e10 if last else 2 * start.shape[0] * features * width // 2,
        features * width,
        in_specs=[pl.BlockSpec(memory_space=pltpu.SMEM), HBM, VMEM] + [VMEM] * len(rows),
        out_specs=(VMEM, VMEM) if last else VMEM,
        scratch_shapes=[
            pltpu.VMEM((len(rows), features, width // PIECES), jnp.bfloat16),
            pltpu.SemaphoreType.DMA((len(rows),)),
        ],
    )(base[None], in_hbm(weight), start, *rows)


def gated(rows, gate, up):
    gate_part = dot_nt(rows, gate)
    up_part = dot_nt(rows, up)
    return (gate_part / (1.0 + jnp.exp(-gate_part)) * up_part).astype(jnp.bfloat16)


def expert_body(pick_ref, rows_ref, gain_ref, shared_gate_ref, shared_up_ref, shared_down_ref, gate_ref, up_ref, down_ref, out_ref):
    owners, _, requests, part = rows_ref.shape
    width = gain_ref.shape[1]
    share = requests // owners
    slots = out_ref.shape[2] - share
    rows = jnp.concatenate(
        [
            normalised(lambda k, o=o: rows_ref[o, k], gain_ref[...], width)
            for o in range(owners)
        ],
        axis=0,
    )
    rows = dot_nn(pick_ref[...], rows).astype(jnp.bfloat16)
    named, rest = rows[: owners * slots], rows[owners * slots :]
    shared = dot_nn(gated(rest, shared_gate_ref[...], shared_up_ref[...]), shared_down_ref[...])
    units = gate_ref.shape[1]
    steps = 4 if units % 64 == 0 and units > 704 else 1
    each = units // steps
    total = jnp.zeros((owners * slots, width), jnp.float32)
    for c in range(steps):
        at = slice(c * each, (c + 1) * each)
        total = total + dot_nn(
            gated(named, gate_ref[0, at, :], up_ref[0, at, :]), down_ref[0, at, :]
        )
    for o in range(owners):
        both = jnp.concatenate(
            [total[o * slots : (o + 1) * slots], shared[o * share : (o + 1) * share]], axis=0
        ).astype(jnp.bfloat16)
        for k in range(PIECES):
            out_ref[o, k] = both[:, k * part : (k + 1) * part]


def expert(pick, rows, gain, slots, shared, weights):
    owners, _, requests, part = rows.shape
    _, units, width = weights[0].shape
    return call(
        expert_body,
        jax.ShapeDtypeStruct(
            (owners, PIECES, slots + requests // owners, part), jnp.bfloat16
        ),
        12,
        6 * pick.shape[0] * units * width,
        6 * units * width,
        in_specs=[VMEM] * 9,
        out_specs=VMEM,
    )(pick, rows, gain, *shared, *weights)


def final_body(parts_ref, weight_ref, mid_ref, out_ref):
    weight = weight_ref[...]
    high = weight.astype(jnp.bfloat16)
    rest = weight - high.astype(jnp.float32)
    low = rest.astype(jnp.bfloat16)
    lower = (rest - low.astype(jnp.float32)).astype(jnp.bfloat16)
    parts = parts_ref[...]
    total = dot_nn(high, parts) + (dot_nn(low, parts) + dot_nn(lower, parts))
    out_ref[...] = (mid_ref[...].astype(jnp.float32) + total).astype(jnp.bfloat16)


def final_sum(parts, weight, mid):
    return call(
        final_body,
        jax.ShapeDtypeStruct(mid.shape, jnp.bfloat16),
        16,
        2 * weight.shape[0] * parts.shape[0] * parts.shape[1],
        2 * parts.shape[0] * parts.shape[1],
    )(parts, weight, mid)


def exchange(x, axis):
    return lax.all_to_all(x, axis, 0, 0, tiled=True)


def turn(x, k):
    count = lax.axis_size("tensor")
    return lax.ppermute(x, "tensor", [(i, i ^ k) for i in range(count)])


def gather_by_turns(x):
    near = [x] + [turn(x, k) for k in (1, 2, 3)]
    crossed = turn(x, 4)
    return near + [crossed] + [turn(crossed, k) for k in (1, 2, 3)]


def swap_owners(arrays):
    count = len(arrays)
    out = {0: arrays[0]}
    for k in reversed(range(1, count)):
        out[k] = lax.ppermute(arrays[k], OWNER, [(i, i ^ k) for i in range(count)])
    return [out[k] for k in range(count)]


def gather_pieces(x):
    devices = x.shape[-3]
    each = devices // PIECES
    if each == 1:
        return x
    lead, (rows, columns) = x.shape[:-3], x.shape[-2:]
    x = x.reshape(lead + (PIECES, each, rows, columns))
    return jnp.swapaxes(x, -3, -2).reshape(lead + (PIECES, rows, each * columns))


def scatter_pieces(x, devices):
    each = devices // PIECES
    if each == 1:
        return x
    lead, (rows, columns) = x.shape[:-3], x.shape[-2:]
    x = x.reshape(lead + (PIECES, rows, each, columns // each))
    return jnp.swapaxes(x, -3, -2).reshape(lead + (devices, rows, columns // each))


def ranks(hits):
    count = hits.shape[0]
    ahead = jnp.arange(count)[:, None] > jnp.arange(count)[None, :]
    return jnp.sum(jnp.where(ahead[:, :, None], hits.astype(jnp.int32)[None], 0), axis=1)


def local(
    hidden,
    attention_gain,
    query_weight,
    out_weight,
    root_cache,
    group_cache,
    group_length,
    suffix_cache,
    suffix_length,
    group_of,
    mixture_gain,
    routes,
    route_weight,
    expert_gate,
    expert_up,
    expert_down,
    shared_gate,
    shared_up,
    shared_down,
):
    owners, tensors = lax.axis_size(OWNER), lax.axis_size("tensor")
    owner_index, tensor_index = lax.axis_index(OWNER), lax.axis_index("tensor")
    requests = hidden.shape[0]
    fanout = routes.shape[1]
    token_share = requests // owners
    pairs = owners // 2
    split = tensors // EXP_OWN
    slots = -(-2 * requests // (owners * 16)) * 16
    expert_slots = -(-2 * requests * fanout // (EXP_OWN * owners * 16)) * 16

    if group_cache.shape[1] % LANES:
        group_columns = group_cache.reshape(-1, KVW).T[None]
    else:
        group_columns = jnp.swapaxes(group_cache, 1, 2)
    by_turns = tensors == PIECES
    base = tensor_index if by_turns else jnp.zeros((), jnp.int32)
    if by_turns:
        rows = gather_by_turns(hidden)
    else:
        copies = jnp.broadcast_to(hidden[None], (tensors,) + hidden.shape)
        rows = gather_pieces(exchange(copies, "tensor"))
        rows = [rows[k] for k in range(PIECES)]

    projected = project(base, rows, attention_gain[None], query_weight)
    projected, group_of, group_length, suffix_length, routes, route_weight = (
        lax.optimization_barrier(
            (projected, group_of, group_length, suffix_length, routes, route_weight)
        )
    )
    destination = group_of // GROUP_OWN
    owner_range = jnp.arange(owners)
    to_owner = (destination ^ owner_index)[:, None] == owner_range[None, :]
    slot_rank = ranks(to_owner)
    placed = to_owner[:, :, None] & (slot_rank[:, :, None] == jnp.arange(slots))
    unpick = placed.reshape(requests, owners * slots).astype(jnp.bfloat16)
    pick = unpick.T
    asked = jnp.sum(
        jnp.where(placed, (group_of % GROUP_OWN + 1)[:, None, None], 0), axis=0
    ).astype(jnp.bfloat16)
    named = routes.astype(jnp.bfloat16).reshape(slots, requests * fanout // slots)
    extra = jnp.where(
        jnp.arange(LANES) == 0,
        asked[:, :, None],
        jnp.pad(named, ((0, 0), (1, LANES - 1 - named.shape[1])))[None],
    )
    suffix_span, group_span = suffix_cache.shape[1], group_cache.shape[1]
    suffix_usable = (
        tensor_index * suffix_span + jnp.arange(suffix_span)[None, :] < suffix_length[:, None]
    )
    suffix_holder = jnp.where(suffix_usable, jnp.arange(requests)[:, None], -1).reshape(1, -1)
    group_usable = (
        tensor_index * group_span + jnp.arange(group_span)[None, :] < group_length[:, None]
    )
    group_holder = (
        jnp.where(group_usable, jnp.arange(1, GROUP_OWN + 1)[:, None], -1)
        .reshape(1, -1)
        .astype(jnp.float32)
    )
    if by_turns:
        pieces = gather_by_turns(projected)
    else:
        copies = jnp.broadcast_to(projected[None], (tensors,) + projected.shape)
        queries = gather_pieces(exchange(copies, "tensor"))
        pieces = [queries[k] for k in range(PIECES)]
    near, far = pieces[: PIECES // 2], pieces[PIECES // 2 :]
    arrived = [swap_owners(pick_queries(pick, extra, near))]
    root_columns, suffix_rows = root_cache.T, suffix_cache.reshape(-1, KVW)
    near, far[0] = lax.optimization_barrier((near, far[0]))
    first = [own_attention(near, suffix_holder, root_columns, suffix_rows)]
    far, first = lax.optimization_barrier((far, first))
    sent = pick_queries(pick, extra, far)
    arrived[0], sent = lax.optimization_barrier((arrived[0], sent))
    arrived.append(swap_owners(sent))
    answered = group_attention(arrived[0], group_columns, group_holder)
    asked_rows, answered = lax.optimization_barrier((arrived[0], answered))
    all_routes = jnp.stack(
        [x[:, HEADS * KVW + 1 : HEADS * KVW + 1 + named.shape[1]] for x in asked_rows]
    ).reshape(1, owners, requests, fanout)
    turned = owner_range[:, None] ^ owner_index == owner_range[None, :]
    all_routes = jnp.sum(
        jnp.where(turned[:, :, None, None], all_routes.astype(jnp.int32), 0), axis=1
    )
    mine = owner_index * EXP_OWN + tensor_index // split
    called = jnp.any(all_routes == mine, axis=2)
    call_rank = ranks(called.T).T
    expert_pick = called[:, None, :] & (
        call_rank[:, None, :] == jnp.arange(expert_slots)[None, :, None]
    )
    seen = owner_range.reshape(2, pairs)
    seen = 2 * (seen % pairs) + seen // pairs
    expert_pick = jnp.where(
        (owner_range[:, None] == seen.reshape(-1)[None, :])[:, None, :, None],
        expert_pick[:, :, None, :],
        False,
    )
    shared_pick = (
        owner_range[:, None, None] * requests
        + owner_index * token_share
        + jnp.arange(token_share)[None, :, None]
    ).reshape(-1, 1) == (seen.reshape(-1, 1) * requests + jnp.arange(requests)).reshape(1, -1)
    expert_pick = jnp.concatenate(
        [expert_pick.reshape(owners * expert_slots, owners * requests), shared_pick], axis=0
    ).astype(jnp.bfloat16)
    share, answered, expert_pick = lax.optimization_barrier((arrived[1], answered, expert_pick))
    back = [swap_owners(answered)]
    answered = group_attention(share, group_columns, group_holder)
    far, answered = lax.optimization_barrier((far, answered))
    back.append(swap_owners(answered))
    first.append(own_attention(far, suffix_holder, root_columns, suffix_rows))
    back, gain = lax.optimization_barrier((back, mixture_gain[None]))
    parts = local_join(unpick, first, sum(back, []), tensors // PIECES)
    if by_turns:
        parts = [part[0] for part in parts]
        crossing = join([parts[4]] + [turn(parts[4 + k], k) for k in (1, 2, 3)])
        parts = [parts[0]] + [turn(parts[k], k) for k in (1, 2, 3)] + [turn(crossing, 4)]
    else:
        parts = exchange(jnp.concatenate(parts, axis=0), "tensor")
        parts = [parts[k] for k in range(tensors)]
    if by_turns:
        attention = gather_by_turns(join(parts, 1)[0])
    else:
        attention = exchange(join(parts, tensors), "tensor").reshape(PIECES, -1, LAT)
        attention = [attention[k] for k in range(PIECES)]
    early = PIECES // 2 + 1
    total = output_projection(0, base, attention[:early], out_weight, hidden, 0)
    rest, total = lax.optimization_barrier((attention[early:], total))
    mid, copies = output_projection(early, base, rest, out_weight, total, pairs * tensors)

    half = exchange(copies, ("pair", "tensor"))
    both = lax.all_gather(half.reshape((pairs, tensors) + mid.shape), "core")
    everything = gather_pieces(both.reshape((owners, tensors) + mid.shape))
    results = expert(
        expert_pick,
        everything,
        gain,
        expert_slots,
        (shared_gate, shared_up, shared_down),
        (expert_gate, expert_up, expert_down),
    )
    results, routes, route_weight = lax.optimization_barrier((results, routes, route_weight))
    results = scatter_pieces(results, tensors).reshape((owners * tensors, -1, mid.shape[1]))
    returned = exchange(results, ("pair", "core", "tensor"))
    experts = jnp.arange(owners * EXP_OWN)
    hits = routes[:, :, None] == experts[None, None, :]
    share = jnp.sum(jnp.where(hits, route_weight[:, :, None], 0.0), axis=1)
    hit = jnp.any(hits, axis=1)
    taken = hit[:, :, None] & (ranks(hit)[:, :, None] == jnp.arange(expert_slots))
    back_weight = jnp.where(taken, share[:, :, None], 0.0)
    back_weight = jnp.repeat(back_weight, split, axis=1)
    shared_weight = np.eye(requests, dtype=np.float32).reshape(requests, owners, 1, token_share)
    shared_weight = np.repeat(shared_weight, tensors, axis=2).reshape(
        requests, owners * tensors, token_share
    )
    back_weight = jnp.concatenate([back_weight, shared_weight], axis=2).reshape(requests, -1)
    return final_sum(returned.reshape(-1, mid.shape[1]), back_weight, mid)


def solution(mesh):
    owners, tensors = mesh.shape["owner"], mesh.shape["tensor"]
    devices = mesh.devices.reshape(owners // 2, 2, tensors)
    return jax.shard_map(
        local,
        mesh=Mesh(devices, OWNER + ("tensor",)),
        in_specs=(
            P(OWNER, "tensor"),
            P(),
            P("tensor", None),
            P("tensor", None),
            P("tensor", None),
            P(OWNER, "tensor", None),
            P(OWNER),
            P(OWNER, "tensor", None),
            P(OWNER),
            P(OWNER),
            P(),
            P(OWNER, None),
            P(OWNER, None),
            P(OWNER + ("tensor",), None, None),
            P(OWNER + ("tensor",), None, None),
            P(OWNER + ("tensor",), None, None),
            P("tensor", None),
            P("tensor", None),
            P("tensor", None),
        ),
        out_specs=P(OWNER, "tensor"),
        check_vma=False,
    )
```
